256 devices in a mesh: dp: 64 (over x_lo, z, y), tensor: 4 (over x_hi, core).
Axes of the slice: x: 4 (x_hi: 2, x_lo: 2; x = x_hi * 2 + x_lo), y: 4, z: 8, core: 2. Of those that a mesh axis runs over, the one named last changes fastest.
Arguments:
- queries: bfloat16 [64, 256, 4096], P('dp', None, 'tensor'), may hold values from -8 to 8
- keys: bfloat16 [64, 256, 512], P('dp', None, 'tensor'), may hold values from -8 to 8
- values: bfloat16 [64, 256, 512], P('dp', None, 'tensor'), may hold values from -6 to 6
- attn_out: bfloat16 [64, 256, 4096], P('dp', None, 'tensor'), may hold values from -6 to 6
- layer_in: bfloat16 [64, 256, 2560], P('dp', 'tensor'), may hold values from -16 to 16
- out_grad: bfloat16 [64, 256, 2560], P('dp', 'tensor'), may hold values from -16 to 16
- w_out: bfloat16 [4096, 2560], P('tensor', 'dp'), may hold values from -0.09375 to 0.09375
- w_value: bfloat16 [2560, 512], P('dp', 'tensor'), may hold values from -0.125 to 0.125
Outputs:
- query_grad: bfloat16 [64, 256, 4096], P('dp', None, 'tensor')
- key_grad: bfloat16 [64, 256, 512], P('dp', None, 'tensor')
- value_grad: bfloat16 [64, 256, 512], P('dp', None, 'tensor')
- input_grad: bfloat16 [64, 256, 2560], P('dp', 'tensor')
- out_weight_grad: float32 [4096, 2560], P('tensor', 'dp')
- value_weight_grad: float32 [2560, 512], P('dp', 'tensor')
The draws below stay inside these ranges and needn't reach their ends.
All inputs are finite; a program needn't handle non-finite values.
Results may differ from the reference program's by a relative error of at most 0.015.
Values may be sent and summed in bfloat16 or wider, within the bound.
No kernel may reach another device: no remote copies, remote signals or barrier semaphores. Data moves between devices by JAX's collectives and lax.ppermute only.
A program may use at most 128 MiB of HBM per device.

```python
import jax
import jax.numpy as jnp
from jax import lax

D = 2560
HQ = 32
KV = 4
HEAD = 128
SEQ = 256
SEQS = 64
N_DP = 64


def draw_keys(key, part):
    key = jax.random.fold_in(key, 7)
    drawn = jnp.clip(jax.random.normal(key, (SEQS, SEQ, KV, HEAD), jnp.float32), -8.0, 8.0)
    return drawn.reshape(SEQS, SEQ, KV * HEAD).astype(jnp.bfloat16)


def draw_queries(key, part):
    key = jax.random.fold_in(key, 9)
    drawn = jnp.clip(jax.random.normal(key, (SEQS, SEQ, HQ, HEAD), jnp.float32), -8.0, 8.0)
    return drawn.reshape(SEQS, SEQ, HQ * HEAD).astype(jnp.bfloat16)


def raised(array, rng, source, target, blocks, factor):
    def block_of(axis_at):
        return (jnp.arange(array.shape[axis_at]) // (array.shape[axis_at] // blocks)).reshape((-1,) + (1,) * (array.ndim - 1 - axis_at))

    first = jax.random.permutation(rng, blocks)[block_of(target)]
    second = (block_of(target) + blocks // 2) % blocks
    return jnp.where((block_of(source) == first) | (block_of(source) == second), factor * array, array)


def steps_of(stream_key, dims, pieces, least, largest):
    def one(axis_at, blocks):
        heights = jax.random.uniform(jax.random.fold_in(jax.random.fold_in(stream_key, 6), axis_at), (blocks,), jnp.float32, least / len(pieces), largest / len(pieces))
        return jnp.repeat(jnp.exp(heights), dims[axis_at] // blocks).reshape((-1,) + (1,) * (len(dims) - axis_at - 1))

    loudness = one(*pieces[0])
    for cut in pieces[1:]:
        loudness = loudness * one(*cut)
    return loudness


def gaussian(rng, shape, scale, most, cuts=(), kind=jnp.bfloat16):
    values = scale * jax.random.normal(rng, shape, jnp.float32)
    if cuts:
        values = values * steps_of(rng, shape, cuts, -0.22, 0.18)
    return jnp.clip(values, -most, most).astype(kind)


def noise_with(rng, dims, deviation, most, cuts, heavy, held_as=jnp.bfloat16):
    values = deviation * jax.random.normal(rng, dims, jnp.float32)
    if cuts:
        values = values * steps_of(rng, dims, cuts, -0.22, 0.18)
    return jnp.clip(raised(values, jax.random.fold_in(rng, 3), *heavy), -most, most).astype(held_as)


def setup_inputs(seed: int = 0) -> dict:
    seeds = jax.random.split(jax.random.key(seed), 9)
    return {
        "queries": draw_queries(jax.random.fold_in(seeds[8], 71), 0),
        "keys": draw_keys(jax.random.fold_in(seeds[8], 71), 0),
        "values": gaussian(seeds[2], (SEQS, SEQ, KV * HEAD), 1.0, 6.0, ((0, 64), (2, 4))),
        "attn_out": gaussian(seeds[3], (SEQS, SEQ, HQ * HEAD), 1.0, 6.0, ((0, 64), (2, 4))),
        "layer_in": noise_with(seeds[4], (SEQS, SEQ, D), 1.0, 16.0, ((0, 64), (1, 4)), (0, 2, 64, 4.0)),
        "out_grad": noise_with(seeds[5], (SEQS, SEQ, D), 1.0, 16.0, ((0, 64), (1, 4)), (0, 2, 64, 4.0)),
        "w_out": gaussian(seeds[6], (HQ * HEAD, D), (HQ * HEAD) ** -0.5, 0.09375, ((0, 4), (1, 64))),
        "w_value": gaussian(seeds[7], (D, KV * HEAD), D ** -0.5, 0.125, ((0, 64), (1, 4))),
    }


def reference(queries, keys, values, attn_out, layer_in, out_grad, w_out, w_value):
    score_scale = HEAD ** -0.5
    per_group = HQ // KV
    causal = jnp.arange(SEQ)[:, None] >= jnp.arange(SEQ)[None, :]

    def one_sequence(totals, inputs):
        query_rows, key_rows, value_rows, output_rows, rows_in, grad_rows = inputs
        head_grad = jnp.dot(grad_rows, w_out.T, preferred_element_type=jnp.float32).astype(jnp.bfloat16)
        query_all = query_rows.reshape(SEQ, HQ, HEAD).astype(jnp.float32)
        key_all = jnp.repeat(key_rows.reshape(SEQ, KV, HEAD), per_group, axis=1).astype(jnp.float32)
        value_all = jnp.repeat(value_rows.reshape(SEQ, KV, HEAD), per_group, axis=1).astype(jnp.float32)
        output_all = output_rows.reshape(SEQ, HQ, HEAD).astype(jnp.float32)
        grad_all = head_grad.reshape(SEQ, HQ, HEAD).astype(jnp.float32)
        scores = jnp.einsum("ihd,jhd->hij", query_all, key_all) * score_scale
        scores = jnp.where(causal[None], scores, -jnp.inf)
        row_peak = jnp.max(scores, axis=2, keepdims=True)
        exponent = jnp.exp(scores - row_peak)
        weights = exponent / jnp.sum(exponent, axis=2, keepdims=True)
        weights_low = lax.optimization_barrier(weights.astype(jnp.bfloat16)).astype(jnp.float32)
        weight_grad = jnp.einsum("ihd,jhd->hij", grad_all, value_all)
        row_dot = jnp.sum(grad_all * output_all, axis=2).T[:, :, None]
        score_grad = weights * (weight_grad - row_dot)
        score_grad = lax.optimization_barrier(score_grad.astype(jnp.bfloat16)).astype(jnp.float32)
        query_grad = (jnp.einsum("hij,jhd->ihd", score_grad, key_all) * score_scale).astype(jnp.bfloat16)
        key_grad = jnp.einsum("hij,ihd->jhd", score_grad, query_all) * score_scale
        key_grad = key_grad.reshape(SEQ, KV, per_group, HEAD).sum(axis=2).astype(jnp.bfloat16)
        value_grad = jnp.einsum("hij,ihd->jhd", weights_low, grad_all)
        value_grad = value_grad.reshape(SEQ, KV, per_group, HEAD).sum(axis=2).astype(jnp.bfloat16)
        value_grad = value_grad.reshape(SEQ, KV * HEAD)
        input_grad = jnp.dot(value_grad, w_value.T, preferred_element_type=jnp.float32).astype(jnp.bfloat16)
        out_total = totals[0] + jnp.dot(output_rows.T, grad_rows, preferred_element_type=jnp.float32)
        value_total = totals[1] + jnp.dot(rows_in.T, value_grad, preferred_element_type=jnp.float32)
        outputs = (query_grad.reshape(SEQ, HQ * HEAD), key_grad.reshape(SEQ, KV * HEAD), value_grad, input_grad)
        return (out_total, value_total), outputs

    initial = (jnp.zeros((HQ * HEAD, D), jnp.float32), jnp.zeros((D, KV * HEAD), jnp.float32))
    totals, gradients = lax.scan(one_sequence, initial, (queries, keys, values, attn_out, layer_in, out_grad))
    return gradients[0], gradients[1], gradients[2], gradients[3], totals[0] / N_DP, totals[1] / N_DP
```

```python
import functools

import jax
import jax.numpy as jnp
from jax import lax
from jax.experimental import pallas as pl
from jax.experimental.pallas import tpu as pltpu
from jax.sharding import Mesh
from jax.sharding import PartitionSpec as P

HEAD = 128
SIZES = {"xl": 2, "z": 8, "y": 4, "xh": 2, "c": 2}
DP = ("xl", "z", "y")
TENSOR = ("xh", "c")
F32 = jnp.float32
BF16 = jnp.bfloat16


def shift(array, axis, by):
    count = SIZES[axis]
    return lax.ppermute(array, axis, [(i, (i + by) % count) for i in range(count)])


def put(buffer, block, *where):
    starts = list(where) + [0] * (buffer.ndim - len(where))
    block = block.reshape((1,) * (buffer.ndim - block.ndim) + block.shape)
    return lax.dynamic_update_slice(buffer, block, starts)


def attention_kernel(
    scale, heads, q_ref, k_ref, v_ref, ao_ref, own_ref, recv_ref, dq_ref, dk_ref, dv_ref, dk_sum, dv_sum
):
    step = pl.program_id(0)

    @pl.when(step == 0)
    def _():
        dk_sum[...] = jnp.zeros_like(dk_sum)
        dv_sum[...] = jnp.zeros_like(dv_sum)

    seq = k_ref.shape[0]
    keys = k_ref[...]
    vals = v_ref[...]
    rows = lax.broadcasted_iota(jnp.int32, (seq, seq), 0)
    cols = lax.broadcasted_iota(jnp.int32, (seq, seq), 1)
    causal = rows >= cols
    last = (((1,), (1,)), ((), ()))
    first = (((0,), (0,)), ((), ()))
    dk_here = jnp.zeros((seq, HEAD), F32)
    dv_here = jnp.zeros((seq, HEAD), F32)
    for h in range(heads):
        span = slice(h * HEAD, (h + 1) * HEAD)
        q = q_ref[:, span]
        grad = (own_ref[:, span] + recv_ref[:, span].astype(F32)).astype(BF16)
        scores = lax.dot_general(q, keys, last, preferred_element_type=F32) * scale
        scores = jnp.where(causal, scores, -jnp.inf)
        peak = jnp.max(scores, axis=1, keepdims=True)
        exponent = jnp.exp(scores - peak)
        probs = exponent / jnp.sum(exponent, axis=1, keepdims=True)
        prob_grad = lax.dot_general(grad, vals, last, preferred_element_type=F32)
        row_dot = jnp.sum(grad.astype(F32) * ao_ref[:, span].astype(F32), axis=1, keepdims=True)
        score_grad = (probs * (prob_grad - row_dot)).astype(BF16)
        dq_ref[:, span] = (jnp.dot(score_grad, keys, preferred_element_type=F32) * scale).astype(BF16)
        dk_here += lax.dot_general(score_grad, q, first, preferred_element_type=F32)
        dv_here += lax.dot_general(probs.astype(BF16), grad, first, preferred_element_type=F32)
    dk_sum[...] += dk_here
    dv_sum[...] += dv_here

    @pl.when(step == pl.num_programs(0) - 1)
    def _():
        dk_ref[...] = (dk_sum[...] * scale).astype(BF16)
        dv_ref[...] = dv_sum[...].astype(BF16)


def attention(q, k, v, ao, own, recv):
    seq, width = q.shape
    heads = 2
    block = heads * HEAD
    wide = pl.BlockSpec((seq, block), lambda i: (0, i))
    whole = pl.BlockSpec((seq, HEAD), lambda i: (0, 0))
    count = width // HEAD
    return pl.pallas_call(
        functools.partial(attention_kernel, HEAD**-0.5, heads),
        grid=(width // block,),
        in_specs=[wide, whole, whole, wide, wide, wide],
        out_specs=[wide, whole, whole],
        out_shape=[
            jax.ShapeDtypeStruct((seq, width), BF16),
            jax.ShapeDtypeStruct((seq, HEAD), BF16),
            jax.ShapeDtypeStruct((seq, HEAD), BF16),
        ],
        scratch_shapes=[pltpu.VMEM((seq, HEAD), F32), pltpu.VMEM((seq, HEAD), F32)],
        cost_estimate=pl.CostEstimate(
            flops=10 * count * seq * seq * HEAD, bytes_accessed=6 * seq * width * 2, transcendentals=count * seq * seq
        ),
        compiler_params=pltpu.CompilerParams(vmem_limit_bytes=32 * 1024 * 1024),
    )(q, k, v, ao, own, recv)


def on_device(queries, keys, values, attn_out, layer_in, out_grad, w_out, w_value):
    xl, z, y, xh, c = (lax.axis_index(a) for a in ("xl", "z", "y", "xh", "c"))
    n_xl, n_z, n_y = SIZES["xl"], SIZES["z"], SIZES["y"]
    n_dp = n_xl * n_z * n_y
    q, k, v, ao, li, og = (a[0] for a in (queries, keys, values, attn_out, layer_in, out_grad))
    seq, width = q.shape
    rows, feats = og.shape
    half = feats // n_xl
    cols = feats // n_dp

    mine = lax.dynamic_slice(og, (0, xl * half), (rows, half))
    other = lax.dynamic_slice(og, (0, (1 - xl) * half), (rows, half))
    pair = jnp.stack([mine, shift(other, "xl", 1)])
    grads = jnp.zeros((2, 2, 2, rows, half), BF16)
    pair5 = pair[:, None, None]
    grads = put(grads, pair5, 0, xh, c)
    grads = put(grads, shift(pair5, "xh", 1), 0, 1 - xh, c)
    column = lax.dynamic_slice(grads, (0, 0, c, 0, 0), (2, 2, 1, rows, half))
    grads = put(grads, shift(column, "c", 1), 0, 0, 1 - c)
    grads = grads.reshape(2 * seq, half)

    shard = jnp.concatenate([w_out.T, w_value], axis=1)
    plane = put(jnp.zeros((n_y,) + shard.shape, BF16), shard, y)
    for step in range(1, n_y):
        plane = put(plane, shift(shard, "y", step), (y - step) % n_y)
    weights = put(jnp.zeros((n_z,) + plane.shape, BF16), plane, z)
    ahead = back = plane
    for step in range(1, n_z // 2):
        ahead = shift(ahead, "z", 1)
        back = shift(back, "z", -1)
        weights = put(weights, ahead, (z - step) % n_z)
        weights = put(weights, back, (z + step) % n_z)
    middle = n_y // 2
    far = (z + n_z // 2) % n_z
    weights = put(weights, shift(ahead[:middle], "z", 1), far)
    weights = put(weights, shift(back[middle:], "z", -1), far, middle)
    weights = weights.reshape(half, width + HEAD)

    ao_other = shift(ao, "xl", 1)
    first = (((0,), (0,)), ((), ()))
    out_part = lax.dot_general(grads[:seq], ao, first, preferred_element_type=F32)
    out_part += lax.dot_general(grads[seq:], ao_other, first, preferred_element_type=F32)
    out_sum = lax.psum_scatter(out_part.astype(BF16), "z", scatter_dimension=0, tiled=True)
    out_sum = lax.psum_scatter(out_sum, "y", scatter_dimension=0, tiled=True)
    out_weight_grad = (out_sum.astype(F32) / n_dp).T

    head_part = jnp.dot(grads, weights[:, :width], preferred_element_type=F32)
    head_recv = shift(head_part[seq:].astype(BF16), "xl", 1)
    query_grad, key_grad, value_grad = attention(q, k, v, ao, head_part[:seq], head_recv)

    rows_in = jnp.zeros((2, 2, rows, feats), BF16)
    rows_in = put(rows_in, li, xh, c)
    rows_in = put(rows_in, shift(li, "xh", 1), 1 - xh, c)
    column = lax.dynamic_slice(rows_in, (0, c, 0, 0), (2, 1, rows, feats))
    rows_in = put(rows_in, shift(column, "c", 1), 0, 1 - c)
    rows_in = rows_in.reshape(seq, feats)

    wv_half = weights[:, width:]
    wv = jnp.zeros((n_xl, half, HEAD), BF16)
    wv = put(wv, wv_half, xl)
    wv = put(wv, shift(wv_half, "xl", 1), 1 - xl).reshape(feats, HEAD)

    partial = lax.dot_general(value_grad, wv, (((1,), (1,)), ((), ())), preferred_element_type=F32)
    partial = partial.reshape(2, 2, rows, feats)
    keep = lax.dynamic_slice(partial, (0, c, 0, 0), (2, 1, rows, feats))
    give = lax.dynamic_slice(partial, (0, 1 - c, 0, 0), (2, 1, rows, feats)).astype(BF16)
    keep = keep + shift(give, "c", 1).astype(F32)
    give = lax.dynamic_slice(keep, (1 - xh, 0, 0, 0), (1, 1, rows, feats)).astype(BF16)
    keep = lax.dynamic_slice(keep, (xh, 0, 0, 0), (1, 1, rows, feats))
    input_grad = (keep + shift(give, "xh", 1).astype(F32)).astype(BF16).reshape(rows, feats)

    value_part = lax.dot_general(rows_in, value_grad, first, preferred_element_type=F32).astype(BF16)
    value_parts = lax.all_to_all(value_part.reshape(n_dp, cols, HEAD), DP, 0, 0, tiled=True)
    value_weight_grad = jnp.sum(value_parts.astype(F32), axis=0) / n_dp

    return (
        query_grad[None],
        key_grad[None],
        value_grad[None],
        input_grad[None],
        out_weight_grad,
        value_weight_grad,
    )


def solution(mesh):
    fine = Mesh(mesh.devices.reshape(tuple(SIZES.values())), tuple(SIZES))
    heads = P(DP, None, TENSOR)
    tokens = P(DP, TENSOR, None)
    return jax.shard_map(
        on_device,
        mesh=fine,
        in_specs=(heads, heads, heads, heads, tokens, tokens, P(TENSOR, DP), P(DP, TENSOR)),
        out_specs=(heads, heads, heads, tokens, P(TENSOR, DP), P(DP, TENSOR)),
        check_vma=False,
    )
```

```python
import functools

import jax
import jax.numpy as jnp
from jax import lax
from jax.experimental import pallas as pl
from jax.experimental.pallas import tpu as pltpu
from jax.sharding import Mesh
from jax.sharding import PartitionSpec as P

HEAD = 128
SIZES = {"xl": 2, "z": 8, "y": 4, "xh": 2, "c": 2}
DP = ("xl", "z", "y")
TENSOR = ("xh", "c")
F32 = jnp.float32
BF16 = jnp.bfloat16


def shift(array, axis, by):
    count = SIZES[axis]
    return lax.ppermute(array, axis, [(i, (i + by) % count) for i in range(count)])


LAST = (((1,), (1,)), ((), ()))
FIRST = (((0,), (0,)), ((), ()))


def after(array, *earlier):
    return lax.optimization_barrier((array,) + earlier)[0]


def limits():
    return pltpu.CompilerParams(vmem_limit_bytes=40 * 1024 * 1024)


def whole(shape):
    return pl.BlockSpec(shape, lambda *_: (0,) * len(shape))


def probs_kernel(scale, heads, q_ref, k_ref, probs_ref):
    keys = k_ref[...]
    seq = keys.shape[0]
    rows = lax.broadcasted_iota(jnp.int32, (seq, seq), 0)
    cols = lax.broadcasted_iota(jnp.int32, (seq, seq), 1)
    for h in range(heads):
        q = q_ref[:, h * HEAD : (h + 1) * HEAD]
        scores = lax.dot_general(keys, q, LAST, preferred_element_type=F32) * scale
        scores = jnp.where(cols >= rows, scores, -jnp.inf)
        exponent = jnp.exp(scores - jnp.max(scores, axis=0, keepdims=True))
        probs_ref[h] = (exponent / jnp.sum(exponent, axis=0, keepdims=True)).astype(BF16)


def probabilities(q, k):
    seq, width = q.shape
    heads = 2
    count = width // HEAD
    return pl.pallas_call(
        functools.partial(probs_kernel, HEAD**-0.5, heads),
        grid=(count // heads,),
        in_specs=[pl.BlockSpec((seq, heads * HEAD), lambda i: (0, i)), whole((seq, HEAD))],
        out_specs=pl.BlockSpec((heads, seq, seq), lambda i: (i, 0, 0)),
        out_shape=jax.ShapeDtypeStruct((count, seq, seq), BF16),
        cost_estimate=pl.CostEstimate(
            flops=2 * count * seq * seq * HEAD,
            bytes_accessed=2 * count * seq * (seq + HEAD),
            transcendentals=count * seq * seq,
        ),
        compiler_params=limits(),
    )(q, k)


def out_kernel(n_y, cols, place, near_ref, far_ref, ao_ref, ao_other_ref, grads_ref, part_ref):
    step = pl.program_id(0)
    xl, c = place[0], place[1]
    rows = near_ref.shape[1]
    seq = ao_ref.shape[0]

    @pl.when(step == 0)
    def _():
        for other in range(2):
            for xh in range(2):
                index = (xl + other) % 2 * 2 + xh
                start = other * seq + xh * 2 * rows
                grads_ref[pl.ds(pl.multiple_of(start + c * rows, rows), rows)] = near_ref[index]
                grads_ref[pl.ds(pl.multiple_of(start + (1 - c) * rows, rows), rows)] = far_ref[index]

    chunk = part_ref.shape[1] * n_y * cols
    span = pl.ds(pl.multiple_of(step * chunk, chunk), chunk)
    total = lax.dot_general(grads_ref[:seq, span], ao_ref[...], FIRST, preferred_element_type=F32)
    total += lax.dot_general(grads_ref[seq:, span], ao_other_ref[...], FIRST, preferred_element_type=F32)
    for i in range(part_ref.shape[1]):
        for y in range(n_y):
            start = (i * n_y + y) * cols
            part_ref[y, i] = total[start : start + cols].astype(BF16)


def out_parts(place, near, far, ao, ao_other, n_y, n_z, cols):
    seq, width = ao.shape
    half = near.shape[2]
    steps = 2
    return pl.pallas_call(
        functools.partial(out_kernel, n_y, cols),
        grid_spec=pltpu.PrefetchScalarGridSpec(
            num_scalar_prefetch=1,
            grid=(steps,),
            in_specs=[whole(near.shape), whole(far.shape), whole(ao.shape), whole(ao.shape)],
            out_specs=[
                whole((2 * seq, half)),
                pl.BlockSpec((n_y, n_z // steps, cols, width), lambda i, place: (0, i, 0, 0)),
            ],
        ),
        out_shape=[
            jax.ShapeDtypeStruct((2 * seq, half), BF16),
            jax.ShapeDtypeStruct((n_y, n_z, cols, width), BF16),
        ],
        cost_estimate=pl.CostEstimate(
            flops=4 * seq * half * width, bytes_accessed=8 * seq * half + 2 * half * width, transcendentals=0
        ),
        compiler_params=limits(),
    )(place, near, far, ao, ao_other)


def head_kernel(heads, grads_ref, w_ref, probs_ref, probs_other_ref, own_ref, send_ref, dv_ref, dv_send_ref, sums):
    step = pl.program_id(0)

    @pl.when(step == 0)
    def _():
        sums[...] = jnp.zeros_like(sums)

    seq = own_ref.shape[0]
    both = jnp.dot(grads_ref[...], w_ref[...], preferred_element_type=F32)
    own_ref[...] = both[:seq]
    low = both.astype(BF16)
    send_ref[...] = low[seq:]
    for i, ref in enumerate((probs_ref, probs_other_ref)):
        total = sums[i]
        for h in range(heads):
            piece = low[i * seq : (i + 1) * seq, h * HEAD : (h + 1) * HEAD]
            total += jnp.dot(ref[h], piece, preferred_element_type=F32)
        sums[i] = total

    @pl.when(step == pl.num_programs(0) - 1)
    def _():
        dv_ref[...] = sums[0]
        dv_send_ref[...] = sums[1].astype(BF16)


def head_parts(grads, weights, probs, probs_other, width):
    tokens, half = grads.shape
    seq = tokens // 2
    heads = 2
    block = heads * HEAD
    pairs = pl.BlockSpec((heads, seq, seq), lambda i: (i, 0, 0))
    wide = pl.BlockSpec((seq, block), lambda i: (0, i))
    return pl.pallas_call(
        functools.partial(head_kernel, heads),
        grid=(width // block,),
        in_specs=[whole(grads.shape), pl.BlockSpec((half, block), lambda i: (0, i)), pairs, pairs],
        out_specs=[wide, wide, whole((seq, HEAD)), whole((seq, HEAD))],
        out_shape=[
            jax.ShapeDtypeStruct((seq, width), F32),
            jax.ShapeDtypeStruct((seq, width), BF16),
            jax.ShapeDtypeStruct((seq, HEAD), F32),
            jax.ShapeDtypeStruct((seq, HEAD), BF16),
        ],
        scratch_shapes=[pltpu.VMEM((2, seq, HEAD), F32)],
        cost_estimate=pl.CostEstimate(
            flops=2 * tokens * half * width + 2 * tokens * seq * width,
            bytes_accessed=2 * half * (width + tokens) + 8 * tokens * width,
            transcendentals=0,
        ),
        compiler_params=limits(),
    )(grads, weights, probs, probs_other)


def score_kernel(scale, heads, q_ref, k_ref, v_ref, ao_ref, own_ref, recv_ref, dq_ref, dk_ref, dk_sum):
    step = pl.program_id(0)

    @pl.when(step == 0)
    def _():
        dk_sum[...] = jnp.zeros_like(dk_sum)

    keys = k_ref[...]
    vals = v_ref[...]
    seq = keys.shape[0]
    rows = lax.broadcasted_iota(jnp.int32, (seq, seq), 0)
    cols = lax.broadcasted_iota(jnp.int32, (seq, seq), 1)
    dk_here = jnp.zeros(dk_sum.shape, F32)
    for h in range(heads):
        span = slice(h * HEAD, (h + 1) * HEAD)
        q = q_ref[:, span]
        grad = (own_ref[:, span] + recv_ref[:, span].astype(F32)).astype(BF16)
        scores = lax.dot_general(q, keys, LAST, preferred_element_type=F32) * scale
        scores = jnp.where(rows >= cols, scores, -jnp.inf)
        exponent = jnp.exp(scores - jnp.max(scores, axis=1, keepdims=True))
        probs = exponent / jnp.sum(exponent, axis=1, keepdims=True)
        prob_grad = lax.dot_general(grad, vals, LAST, preferred_element_type=F32)
        row_dot = jnp.sum(grad.astype(F32) * ao_ref[:, span].astype(F32), axis=1, keepdims=True)
        score_grad = (probs * (prob_grad - row_dot)).astype(BF16)
        dq_ref[:, span] = (jnp.dot(score_grad, keys, preferred_element_type=F32) * scale).astype(BF16)
        dk_here += lax.dot_general(score_grad, q, FIRST, preferred_element_type=F32)
    dk_sum[...] += dk_here

    @pl.when(step == pl.num_programs(0) - 1)
    def _():
        dk_ref[...] = (dk_sum[...] * scale).astype(BF16)


def score_gradients(q, k, v, ao, own, recv):
    seq, width = q.shape
    heads = 2
    count = width // HEAD
    wide = pl.BlockSpec((seq, heads * HEAD), lambda i: (0, i))
    narrow = whole((seq, HEAD))
    return pl.pallas_call(
        functools.partial(score_kernel, HEAD**-0.5, heads),
        grid=(count // heads,),
        in_specs=[wide, narrow, narrow, wide, wide, wide],
        out_specs=[wide, narrow],
        out_shape=[jax.ShapeDtypeStruct((seq, width), BF16), jax.ShapeDtypeStruct((seq, HEAD), BF16)],
        scratch_shapes=[pltpu.VMEM((seq, HEAD), F32)],
        cost_estimate=pl.CostEstimate(
            flops=8 * count * seq * seq * HEAD, bytes_accessed=12 * seq * width, transcendentals=count * seq * seq
        ),
        compiler_params=limits(),
    )(q, k, v, ao, own, recv)


def input_kernel(place, dv_ref, near_ref, far_ref, keep_ref, give_ref):
    c = place[1]
    rows = dv_ref.shape[2]
    for xh in range(2):
        keep = dv_ref[xh, c]
        give = dv_ref[xh, 1 - c]
        span = slice(xh * rows, (xh + 1) * rows)
        for i, ref in enumerate((near_ref, far_ref)):
            keep_ref[i, span] = lax.dot_general(keep, ref[...], LAST, preferred_element_type=F32)
            give_ref[i, span] = lax.dot_general(give, ref[...], LAST, preferred_element_type=F32).astype(BF16)


def input_parts(place, dv, near, far):
    _, _, rows, _ = dv.shape
    half = near.shape[0]
    shape = (2, 2 * rows, half)
    return pl.pallas_call(
        input_kernel,
        grid_spec=pltpu.PrefetchScalarGridSpec(
            num_scalar_prefetch=1,
            grid=(1,),
            in_specs=[whole(dv.shape), whole(near.shape), whole(far.shape)],
            out_specs=[whole(shape), whole(shape)],
        ),
        out_shape=[jax.ShapeDtypeStruct(shape, F32), jax.ShapeDtypeStruct(shape, BF16)],
        cost_estimate=pl.CostEstimate(
            flops=16 * rows * half * HEAD, bytes_accessed=4 * half * HEAD + 24 * rows * half, transcendentals=0
        ),
        compiler_params=limits(),
    )(place, dv, near, far)


def on_device(queries, keys, values, attn_out, layer_in, out_grad, w_out, w_value):
    xl, xh, c = (lax.axis_index(a) for a in ("xl", "xh", "c"))
    place = jnp.stack([xl, c]).astype(jnp.int32)
    n_xl, n_z, n_y = SIZES["xl"], SIZES["z"], SIZES["y"]
    n_dp = n_xl * n_z * n_y
    q, k, v, ao, li, og = (a[0] for a in (queries, keys, values, attn_out, layer_in, out_grad))
    seq, width = q.shape
    rows, feats = og.shape
    half = feats // n_xl
    cols = feats // n_dp

    shard = jnp.concatenate([w_out.T, w_value], axis=1)
    plane = lax.all_to_all(jnp.broadcast_to(shard, (n_y,) + shard.shape), "y", 0, 0, tiled=True)
    weights = lax.all_gather(plane.reshape(n_y * cols, width + HEAD), "z", axis=0, tiled=True)

    halves = og.reshape(rows, n_xl, 1, half).transpose(1, 2, 0, 3)
    halves = jnp.broadcast_to(halves, (n_xl, 2, rows, half)).reshape(n_xl * 2, rows, half)
    near = lax.all_to_all(halves, ("xl", "xh"), 0, 0, tiled=True)
    far = shift(near, "c", 1)
    ao_other = shift(ao, "xl", 1)
    q_other = shift(after(q, near, ao_other), "xl", 1)
    k_other = shift(after(k, near, ao_other), "xl", 1)

    grads, part = out_parts(place, near, far, ao, ao_other, n_y, n_z, cols)
    part = lax.all_to_all(part, "y", 0, 0, tiled=True)
    part = jnp.sum(part.astype(F32), axis=0).astype(BF16)
    part = lax.all_to_all(part, "z", 0, 0, tiled=True)
    out_weight_grad = (jnp.sum(part.astype(F32), axis=0) / n_dp).T

    probs = probabilities(after(q, near), k)
    probs_other = probabilities(q_other, k_other)

    own, send, dv_own, dv_send = head_parts(grads, weights, probs, probs_other, width)
    dv_recv = shift(dv_send, "xl", 1)
    value_grad = (dv_own + dv_recv.astype(F32)).astype(BF16)
    wv = weights[:, width:]
    wv_other = shift(wv, "xl", 1)
    recv = shift(after(send, dv_recv), "xl", 1)

    rows_in = lax.all_gather(after(li, weights), ("xh", "c"), axis=0, tiled=True)
    value_part = lax.dot_general(rows_in, value_grad, FIRST, preferred_element_type=F32).astype(BF16)
    value_parts = lax.all_to_all(value_part.reshape(n_dp, cols, HEAD), DP, 0, 0, tiled=True)
    value_weight_grad = jnp.sum(value_parts.astype(F32), axis=0) / n_dp

    keep, give = input_parts(place, value_grad.reshape(2, 2, rows, HEAD), wv, wv_other)
    keep = keep + shift(give, "c", 1).astype(F32)
    give = lax.dynamic_slice(keep, (0, (1 - xh) * rows, 0), (2, rows, half)).astype(BF16)
    keep = lax.dynamic_slice(keep, (0, xh * rows, 0), (2, rows, half))
    keep = (keep + shift(give, "xh", 1).astype(F32)).astype(BF16)
    input_grad = jnp.where(
        xl == 0, jnp.concatenate([keep[0], keep[1]], axis=1), jnp.concatenate([keep[1], keep[0]], axis=1)
    )

    query_grad, key_grad = score_gradients(q, k, v, ao, own, recv)

    return (
        query_grad[None],
        key_grad[None],
        value_grad[None],
        input_grad[None],
        out_weight_grad,
        value_weight_grad,
    )


def solution(mesh):
    fine = Mesh(mesh.devices.reshape(tuple(SIZES.values())), tuple(SIZES))
    heads = P(DP, None, TENSOR)
    tokens = P(DP, TENSOR, None)
    return jax.shard_map(
        on_device,
        mesh=fine,
        in_specs=(heads, heads, heads, heads, tokens, tokens, P(TENSOR, DP), P(DP, TENSOR)),
        out_specs=(heads, heads, heads, tokens, P(TENSOR, DP), P(DP, TENSOR)),
        check_vma=False,
    )
```

```python
import functools

import jax
import jax.numpy as jnp
from jax import lax
from jax.experimental import pallas as pl
from jax.experimental.pallas import tpu as pltpu
from jax.sharding import Mesh
from jax.sharding import PartitionSpec as P

HEAD = 128
SIZES = {"xl": 2, "z": 8, "y": 4, "xh": 2, "c": 2}
DP = ("xl", "z", "y")
TENSOR = ("xh", "c")
F32 = jnp.float32
BF16 = jnp.bfloat16


def shift(array, axis, by):
    count = SIZES[axis]
    return lax.ppermute(array, axis, [(i, (i + by) % count) for i in range(count)])


LAST = (((1,), (1,)), ((), ()))
FIRST = (((0,), (0,)), ((), ()))


def after(array, *earlier):
    return lax.optimization_barrier((array,) + earlier)[0]


LIGHT = pl.CostEstimate(flops=1, bytes_accessed=1, transcendentals=0)


def limits():
    return pltpu.CompilerParams(vmem_limit_bytes=16 * 1024 * 1024)


def whole(shape):
    return pl.BlockSpec(shape, lambda *_: (0,) * len(shape))


def probs_kernel(scale, heads, q_ref, k_ref, probs_ref):
    keys = k_ref[...]
    seq = keys.shape[0]
    rows = lax.broadcasted_iota(jnp.int32, (seq, seq), 0)
    cols = lax.broadcasted_iota(jnp.int32, (seq, seq), 1)
    for h in range(heads):
        q = q_ref[:, h * HEAD : (h + 1) * HEAD]
        scores = lax.dot_general(keys, q, LAST, preferred_element_type=F32) * scale
        scores = jnp.where(cols >= rows, scores, -jnp.inf)
        exponent = jnp.exp(scores - jnp.max(scores, axis=0, keepdims=True))
        probs_ref[h] = (exponent / jnp.sum(exponent, axis=0, keepdims=True)).astype(BF16)


def probabilities(q, k):
    seq, width = q.shape
    heads = 2
    count = width // HEAD
    return pl.pallas_call(
        functools.partial(probs_kernel, HEAD**-0.5, heads),
        grid=(count // heads,),
        in_specs=[pl.BlockSpec((seq, heads * HEAD), lambda i: (0, i)), whole((seq, HEAD))],
        out_specs=pl.BlockSpec((heads, seq, seq), lambda i: (i, 0, 0)),
        out_shape=jax.ShapeDtypeStruct((count, seq, seq), BF16),
        cost_estimate=LIGHT,
        compiler_params=limits(),
    )(q, k)


def plane_kernel(place, *refs):
    n_y = len(refs) - 1
    for k in range(n_y):
        refs[n_y][(place[2] + n_y - k) % n_y] = refs[k][...]


def in_order(place, pieces):
    shape = (len(pieces),) + pieces[0].shape
    return pl.pallas_call(
        plane_kernel,
        grid_spec=pltpu.PrefetchScalarGridSpec(
            num_scalar_prefetch=1,
            grid=(1,),
            in_specs=[whole(piece.shape) for piece in pieces],
            out_specs=whole(shape),
        ),
        out_shape=jax.ShapeDtypeStruct(shape, BF16),
        cost_estimate=LIGHT,
        compiler_params=limits(),
    )(place, *pieces)


def gather_rows(xl, c, near_ref, far_ref, rows_ref):
    rows = near_ref.shape[1]
    for other in range(2):
        for xh in range(2):
            index = (xl + other) % 2 * 2 + xh
            start = (other * 2 + xh) * 2 * rows
            rows_ref[pl.ds(pl.multiple_of(start + c * rows, rows), rows)] = near_ref[index]
            rows_ref[pl.ds(pl.multiple_of(start + (1 - c) * rows, rows), rows)] = far_ref[index]


def out_kernel(cols, place, near_ref, far_ref, ao_ref, ao_other_ref, grads_ref, *rest):
    parts, total = rest[:-1], rest[-1]
    n_y = len(parts)
    step = pl.program_id(0)
    seq = ao_ref.shape[0]

    @pl.when(step == 0)
    def _():
        gather_rows(place[0], place[1], near_ref, far_ref, grads_ref)

    blocks = parts[0].shape[0]
    chunk = blocks * n_y * cols
    span = pl.ds(pl.multiple_of(step * chunk, chunk), chunk)
    total[...] = lax.dot_general(grads_ref[:seq, span], ao_ref[...], FIRST, preferred_element_type=F32)
    total[...] += lax.dot_general(grads_ref[seq:, span], ao_other_ref[...], FIRST, preferred_element_type=F32)
    for k in range(n_y):
        y = (place[2] + k) % n_y
        for i in range(blocks):
            start = pl.multiple_of((i * n_y + y) * cols, 8)
            parts[k][i] = total[pl.ds(start, cols)].astype(BF16)


def out_parts(place, near, far, ao, ao_other, n_y, n_z, cols):
    seq, width = ao.shape
    half = near.shape[2]
    steps = 2
    return pl.pallas_call(
        functools.partial(out_kernel, cols),
        grid_spec=pltpu.PrefetchScalarGridSpec(
            num_scalar_prefetch=1,
            grid=(steps,),
            in_specs=[whole(near.shape), whole(far.shape), whole(ao.shape), whole(ao.shape)],
            out_specs=[whole((2 * seq, half))]
            + [pl.BlockSpec((n_z // steps, cols, width), lambda i, place: (i, 0, 0))] * n_y,
            scratch_shapes=[pltpu.VMEM((half // steps, width), F32)],
        ),
        out_shape=[jax.ShapeDtypeStruct((2 * seq, half), BF16)]
        + [jax.ShapeDtypeStruct((n_z, cols, width), BF16)] * n_y,
        cost_estimate=LIGHT,
        compiler_params=limits(),
    )(place, near, far, ao, ao_other)


def head_kernel(heads, grads_ref, w_ref, probs_ref, probs_other_ref, own_ref, send_ref, dv_ref, dv_send_ref, sums):
    step = pl.program_id(0)

    @pl.when(step == 0)
    def _():
        sums[...] = jnp.zeros_like(sums)

    seq = own_ref.shape[0]
    both = jnp.dot(grads_ref[...], w_ref[...], preferred_element_type=F32)
    own_ref[...] = both[:seq]
    low = both.astype(BF16)
    send_ref[...] = low[seq:]
    for i, ref in enumerate((probs_ref, probs_other_ref)):
        total = sums[i]
        for h in range(heads):
            piece = low[i * seq : (i + 1) * seq, h * HEAD : (h + 1) * HEAD]
            total += jnp.dot(ref[h], piece, preferred_element_type=F32)
        sums[i] = total

    @pl.when(step == pl.num_programs(0) - 1)
    def _():
        dv_ref[...] = sums[...]
        dv_send_ref[...] = sums[...].astype(BF16)


def head_parts(grads, weights, probs, probs_other, width):
    tokens, half = grads.shape
    seq = tokens // 2
    heads = 2
    block = heads * HEAD
    pairs = pl.BlockSpec((heads, seq, seq), lambda i: (i, 0, 0))
    wide = pl.BlockSpec((seq, block), lambda i: (0, i))
    return pl.pallas_call(
        functools.partial(head_kernel, heads),
        grid=(width // block,),
        in_specs=[whole(grads.shape), pl.BlockSpec((half, block), lambda i: (0, i)), pairs, pairs],
        out_specs=[wide, wide, whole((2, seq, HEAD)), whole((2, seq, HEAD))],
        out_shape=[
            jax.ShapeDtypeStruct((seq, width), F32),
            jax.ShapeDtypeStruct((seq, width), BF16),
            jax.ShapeDtypeStruct((2, seq, HEAD), F32),
            jax.ShapeDtypeStruct((2, seq, HEAD), BF16),
        ],
        scratch_shapes=[pltpu.VMEM((2, seq, HEAD), F32)],
        cost_estimate=LIGHT,
        compiler_params=limits(),
    )(grads, weights, probs, probs_other)


def score_kernel(scale, heads, q_ref, k_ref, v_ref, ao_ref, own_ref, recv_ref, dq_ref, dk_ref, dk_sum):
    step = pl.program_id(0)

    @pl.when(step == 0)
    def _():
        dk_sum[...] = jnp.zeros_like(dk_sum)

    keys = k_ref[...]
    vals = v_ref[...]
    seq = keys.shape[0]
    rows = lax.broadcasted_iota(jnp.int32, (seq, seq), 0)
    cols = lax.broadcasted_iota(jnp.int32, (seq, seq), 1)
    dk_here = jnp.zeros(dk_sum.shape, F32)
    for h in range(heads):
        span = slice(h * HEAD, (h + 1) * HEAD)
        q = q_ref[:, span]
        grad = (own_ref[:, span] + recv_ref[:, span].astype(F32)).astype(BF16)
        scores = lax.dot_general(q, keys, LAST, preferred_element_type=F32) * scale
        scores = jnp.where(rows >= cols, scores, -jnp.inf)
        exponent = jnp.exp(scores - jnp.max(scores, axis=1, keepdims=True))
        probs = exponent / jnp.sum(exponent, axis=1, keepdims=True)
        prob_grad = lax.dot_general(grad, vals, LAST, preferred_element_type=F32)
        row_dot = jnp.sum(grad.astype(F32) * ao_ref[:, span].astype(F32), axis=1, keepdims=True)
        score_grad = (probs * (prob_grad - row_dot)).astype(BF16)
        dq_ref[:, span] = (jnp.dot(score_grad, keys, preferred_element_type=F32) * scale).astype(BF16)
        dk_here += lax.dot_general(score_grad, q, FIRST, preferred_element_type=F32)
    dk_sum[...] += dk_here

    @pl.when(step == pl.num_programs(0) - 1)
    def _():
        dk_ref[...] = (dk_sum[...] * scale).astype(BF16)


def score_gradients(q, k, v, ao, own, recv):
    seq, width = q.shape
    heads = 2
    count = width // HEAD
    wide = pl.BlockSpec((seq, heads * HEAD), lambda i: (0, i))
    narrow = whole((seq, HEAD))
    return pl.pallas_call(
        functools.partial(score_kernel, HEAD**-0.5, heads),
        grid=(count // heads,),
        in_specs=[wide, narrow, narrow, wide, wide, wide],
        out_specs=[wide, narrow],
        out_shape=[jax.ShapeDtypeStruct((seq, width), BF16), jax.ShapeDtypeStruct((seq, HEAD), BF16)],
        scratch_shapes=[pltpu.VMEM((seq, HEAD), F32)],
        cost_estimate=LIGHT,
        compiler_params=limits(),
    )(q, k, v, ao, own, recv)


def input_kernel(place, dv_ref, wv_ref, keep_ref, give_ref):
    xl, c = place[0], place[1]
    wv = wv_ref[...]
    for other in range(2):
        for xh in range(2):
            index = (xl + other) % 2 * 2 + xh
            keep_ref[index] = lax.dot_general(dv_ref[other, xh, c], wv, LAST, preferred_element_type=F32)
            give = lax.dot_general(dv_ref[other, xh, 1 - c], wv, LAST, preferred_element_type=F32)
            give_ref[index] = give.astype(BF16)


def input_parts(place, dv, wv):
    rows = dv.shape[3]
    half = wv.shape[0]
    shape = (4, rows, half)
    return pl.pallas_call(
        input_kernel,
        grid_spec=pltpu.PrefetchScalarGridSpec(
            num_scalar_prefetch=1,
            grid=(1,),
            in_specs=[whole(dv.shape), whole(wv.shape)],
            out_specs=[whole(shape), whole(shape)],
        ),
        out_shape=[jax.ShapeDtypeStruct(shape, F32), jax.ShapeDtypeStruct(shape, BF16)],
        cost_estimate=LIGHT,
        compiler_params=limits(),
    )(place, dv, wv)


def value_kernel(cols, place, near_ref, far_ref, dv_ref, part_ref, rows_ref):
    gather_rows(place[0], place[1], near_ref, far_ref, rows_ref)
    total = lax.dot_general(rows_ref[...], dv_ref[...], FIRST, preferred_element_type=F32)
    for i in range(part_ref.shape[0]):
        part_ref[i] = total[i * cols : (i + 1) * cols].astype(BF16)


def value_parts(place, near, far, dv, cols):
    tokens = dv.shape[0]
    half = near.shape[2]
    shape = (half // cols, cols, HEAD)
    return pl.pallas_call(
        functools.partial(value_kernel, cols),
        grid_spec=pltpu.PrefetchScalarGridSpec(
            num_scalar_prefetch=1,
            grid=(1,),
            in_specs=[whole(near.shape), whole(far.shape), whole(dv.shape)],
            out_specs=whole(shape),
            scratch_shapes=[pltpu.VMEM((tokens, half), BF16)],
        ),
        out_shape=jax.ShapeDtypeStruct(shape, BF16),
        cost_estimate=LIGHT,
        compiler_params=limits(),
    )(place, near, far, dv)


def pair_rows(array, n_xl):
    rows, feats = array.shape
    halves = array.reshape(rows, n_xl, 1, feats // n_xl).transpose(1, 2, 0, 3)
    return jnp.broadcast_to(halves, (n_xl, 2, rows, feats // n_xl)).reshape(n_xl * 2, rows, feats // n_xl)


def on_device(queries, keys, values, attn_out, layer_in, out_grad, w_out, w_value):
    xl, y, xh, c = (lax.axis_index(a) for a in ("xl", "y", "xh", "c"))
    place = jnp.stack([xl, c, y]).astype(jnp.int32)
    n_xl, n_z, n_y = SIZES["xl"], SIZES["z"], SIZES["y"]
    n_dp = n_xl * n_z * n_y
    q, k, v, ao, li, og = (a[0] for a in (queries, keys, values, attn_out, layer_in, out_grad))
    seq, width = q.shape
    rows, feats = og.shape
    half = feats // n_xl
    cols = feats // n_dp

    shard = jnp.concatenate([w_out.T, w_value], axis=1)
    pieces = [shift(shard, "y", step) for step in range(1, n_y)]
    near = lax.all_to_all(pair_rows(og, n_xl), ("xl", "xh"), 0, 0, tiled=True)
    pieces = [after(piece, near) for piece in [shard] + pieces]
    plane = in_order(place, pieces)

    weights = lax.all_gather(plane.reshape(n_y * cols, width + HEAD), "z", axis=0, tiled=True)

    ao_other = shift(ao, "xl", 1)
    far = shift(near, "c", 1)
    q_other = shift(after(q, ao_other), "xl", 1)
    k_other = shift(after(k, ao_other), "xl", 1)

    grads, *parts = out_parts(place, near, far, ao, ao_other, n_y, n_z, cols)
    parts = parts[:1] + [shift(parts[step], "y", step) for step in range(1, n_y)]

    li_near = lax.all_to_all(after(pair_rows(li, n_xl), grads), ("xl", "xh"), 0, 0, tiled=True)
    li_far = shift(li_near, "c", 1)

    probs = probabilities(after(q, near), k)
    probs_other = probabilities(q_other, k_other)

    part = sum(part.astype(F32) for part in parts).astype(BF16)
    weights, li_far, part = lax.optimization_barrier((weights, li_far, part))
    own, send, dv_own, dv_send = head_parts(grads, weights, probs, probs_other, width)
    dv_recv = shift(dv_send, "xl", 1)
    dv = (dv_own + dv_recv[::-1].astype(F32)).astype(BF16)
    value_grad = dv[0]
    recv = shift(after(send, dv_recv), "xl", 1)

    part = lax.psum_scatter(part.reshape(n_z * cols, width), "z", scatter_dimension=0, tiled=True)
    value_part = value_parts(place, li_near, li_far, dv.reshape(n_xl * seq, HEAD), cols)
    value_part = lax.all_to_all(value_part, ("z", "y"), 0, 0, tiled=True)

    keep, give = input_parts(place, dv.reshape(2, 2, 2, rows, HEAD), weights[:, width:])
    keep = (keep + shift(give, "c", 1).astype(F32)).reshape(n_xl, 2, rows, half)
    give = lax.dynamic_slice(keep, (0, 1 - xh, 0, 0), (n_xl, 1, rows, half)).astype(BF16)
    keep = lax.dynamic_slice(keep, (0, xh, 0, 0), (n_xl, 1, rows, half))
    give = shift(give, "xh", 1)

    part, value_part, recv, give = lax.optimization_barrier((part, value_part, recv, give))
    out_weight_grad = (part.astype(F32) / n_dp).T
    value_weight_grad = jnp.sum(value_part.astype(F32), axis=0) / n_dp
    keep = (keep + give.astype(F32)).astype(BF16).reshape(n_xl, rows, half)
    mine = lax.dynamic_index_in_dim(keep, xl, 0, False)
    other = shift(lax.dynamic_index_in_dim(keep, 1 - xl, 0, False), "xl", 1)
    input_grad = jnp.where(
        xl == 0, jnp.concatenate([mine, other], axis=1), jnp.concatenate([other, mine], axis=1)
    )
    query_grad, key_grad = score_gradients(q, k, v, ao, own, recv)

    return (
        query_grad[None],
        key_grad[None],
        value_grad[None],
        input_grad[None],
        out_weight_grad,
        value_weight_grad,
    )


def solution(mesh):
    fine = Mesh(mesh.devices.reshape(tuple(SIZES.values())), tuple(SIZES))
    heads = P(DP, None, TENSOR)
    tokens = P(DP, TENSOR, None)
    return jax.shard_map(
        on_device,
        mesh=fine,
        in_specs=(heads, heads, heads, heads, tokens, tokens, P(TENSOR, DP), P(DP, TENSOR)),
        out_specs=(heads, heads, heads, tokens, P(TENSOR, DP), P(DP, TENSOR)),
        check_vma=False,
    )
```

```python
import functools

import jax
import jax.numpy as jnp
from jax import lax
from jax.experimental import pallas as pl
from jax.experimental.pallas import tpu as pltpu
from jax.sharding import Mesh
from jax.sharding import PartitionSpec as P

HEAD = 128
SIZES = {"xl": 2, "z": 8, "y": 4, "xh": 2, "c": 2}
DP = ("xl", "z", "y")
TENSOR = ("xh", "c")
F32 = jnp.float32
BF16 = jnp.bfloat16


def shift(array, axis, by):
    count = SIZES[axis]
    return lax.ppermute(array, axis, [(i, (i + by) % count) for i in range(count)])


LAST = (((1,), (1,)), ((), ()))
FIRST = (((0,), (0,)), ((), ()))


def after(array, *earlier):
    return lax.optimization_barrier((array,) + earlier)[0]


LIGHT = pl.CostEstimate(flops=1, bytes_accessed=1, transcendentals=0)


def limits():
    return pltpu.CompilerParams(vmem_limit_bytes=16 * 1024 * 1024)


def whole(shape):
    return pl.BlockSpec(shape, lambda *_: (0,) * len(shape))


def probs_kernel(scale, heads, q_ref, k_ref, probs_ref):
    keys = k_ref[...]
    seq = keys.shape[0]
    rows = lax.broadcasted_iota(jnp.int32, (seq, seq), 0)
    cols = lax.broadcasted_iota(jnp.int32, (seq, seq), 1)
    for h in range(heads):
        q = q_ref[:, h * HEAD : (h + 1) * HEAD]
        scores = lax.dot_general(keys, q, LAST, preferred_element_type=F32) * scale
        scores = jnp.where(cols >= rows, scores, -jnp.inf)
        exponent = jnp.exp(scores - jnp.max(scores, axis=0, keepdims=True))
        probs_ref[h] = (exponent / jnp.sum(exponent, axis=0, keepdims=True)).astype(BF16)


def probabilities(q, k):
    seq, width = q.shape
    heads = 2
    count = width // HEAD
    return pl.pallas_call(
        functools.partial(probs_kernel, HEAD**-0.5, heads),
        grid=(count // heads,),
        in_specs=[pl.BlockSpec((seq, heads * HEAD), lambda i: (0, i)), whole((seq, HEAD))],
        out_specs=pl.BlockSpec((heads, seq, seq), lambda i: (i, 0, 0)),
        out_shape=jax.ShapeDtypeStruct((count, seq, seq), BF16),
        cost_estimate=LIGHT,
        compiler_params=limits(),
    )(q, k)


def plane_kernel(place, *refs):
    n_y = len(refs) - 1
    for k in range(n_y):
        refs[n_y][(place[2] + n_y - k) % n_y] = refs[k][...]


def in_order(place, pieces):
    shape = (len(pieces),) + pieces[0].shape
    return pl.pallas_call(
        plane_kernel,
        grid_spec=pltpu.PrefetchScalarGridSpec(
            num_scalar_prefetch=1,
            grid=(1,),
            in_specs=[whole(piece.shape) for piece in pieces],
            out_specs=whole(shape),
        ),
        out_shape=jax.ShapeDtypeStruct(shape, BF16),
        cost_estimate=LIGHT,
        compiler_params=limits(),
    )(place, *pieces)


def gather_rows(xl, c, near_ref, far_ref, rows_ref):
    rows = near_ref.shape[1]
    for other in range(2):
        for xh in range(2):
            index = (xl + other) % 2 * 2 + xh
            start = (other * 2 + xh) * 2 * rows
            rows_ref[pl.ds(pl.multiple_of(start + c * rows, rows), rows)] = near_ref[index]
            rows_ref[pl.ds(pl.multiple_of(start + (1 - c) * rows, rows), rows)] = far_ref[index]


def out_kernel(place, near_ref, far_ref, ao_ref, ao_other_ref, grads_ref, part_ref):
    step = pl.program_id(0)
    seq = ao_ref.shape[0]

    @pl.when(step == 0)
    def _():
        gather_rows(place[0], place[1], near_ref, far_ref, grads_ref)

    chunk = part_ref.shape[0]
    span = pl.ds(pl.multiple_of(step * chunk, chunk), chunk)
    total = lax.dot_general(grads_ref[:seq, span], ao_ref[...], FIRST, preferred_element_type=F32)
    total += lax.dot_general(grads_ref[seq:, span], ao_other_ref[...], FIRST, preferred_element_type=F32)
    part_ref[...] = total.astype(BF16)


def out_part(place, near, far, ao, ao_other):
    seq, width = ao.shape
    half = near.shape[2]
    chunk = half // 5
    return pl.pallas_call(
        out_kernel,
        grid_spec=pltpu.PrefetchScalarGridSpec(
            num_scalar_prefetch=1,
            grid=(half // chunk,),
            in_specs=[whole(near.shape), whole(far.shape), whole(ao.shape), whole(ao.shape)],
            out_specs=[whole((2 * seq, half)), pl.BlockSpec((chunk, width), lambda i, place: (i, 0))],
        ),
        out_shape=[jax.ShapeDtypeStruct((2 * seq, half), BF16), jax.ShapeDtypeStruct((half, width), BF16)],
        cost_estimate=LIGHT,
        compiler_params=limits(),
    )(place, near, far, ao, ao_other)


def head_kernel(heads, grads_ref, w_ref, probs_ref, probs_other_ref, own_ref, send_ref, dv_ref, dv_send_ref, sums):
    step = pl.program_id(0)

    @pl.when(step == 0)
    def _():
        sums[...] = jnp.zeros_like(sums)

    seq = own_ref.shape[0]
    both = jnp.dot(grads_ref[...], w_ref[...], preferred_element_type=F32)
    own_ref[...] = both[:seq]
    low = both.astype(BF16)
    send_ref[...] = low[seq:]
    for i, ref in enumerate((probs_ref, probs_other_ref)):
        total = sums[i]
        for h in range(heads):
            piece = low[i * seq : (i + 1) * seq, h * HEAD : (h + 1) * HEAD]
            total += jnp.dot(ref[h], piece, preferred_element_type=F32)
        sums[i] = total

    @pl.when(step == pl.num_programs(0) - 1)
    def _():
        dv_ref[...] = sums[...]
        dv_send_ref[...] = sums[...].astype(BF16)


def head_parts(grads, weights, probs, probs_other, width):
    tokens, half = grads.shape
    seq = tokens // 2
    heads = 2
    block = heads * HEAD
    pairs = pl.BlockSpec((heads, seq, seq), lambda i: (i, 0, 0))
    wide = pl.BlockSpec((seq, block), lambda i: (0, i))
    return pl.pallas_call(
        functools.partial(head_kernel, heads),
        grid=(width // block,),
        in_specs=[whole(grads.shape), pl.BlockSpec((half, block), lambda i: (0, i)), pairs, pairs],
        out_specs=[wide, wide, whole((2, seq, HEAD)), whole((2, seq, HEAD))],
        out_shape=[
            jax.ShapeDtypeStruct((seq, width), F32),
            jax.ShapeDtypeStruct((seq, width), BF16),
            jax.ShapeDtypeStruct((2, seq, HEAD), F32),
            jax.ShapeDtypeStruct((2, seq, HEAD), BF16),
        ],
        scratch_shapes=[pltpu.VMEM((2, seq, HEAD), F32)],
        cost_estimate=LIGHT,
        compiler_params=limits(),
    )(grads, weights, probs, probs_other)


def score_kernel(scale, heads, q_ref, k_ref, v_ref, ao_ref, own_ref, recv_ref, dq_ref, dk_ref, dk_sum):
    step = pl.program_id(0)

    @pl.when(step == 0)
    def _():
        dk_sum[...] = jnp.zeros_like(dk_sum)

    keys = k_ref[...]
    vals = v_ref[...]
    seq = keys.shape[0]
    rows = lax.broadcasted_iota(jnp.int32, (seq, seq), 0)
    cols = lax.broadcasted_iota(jnp.int32, (seq, seq), 1)
    dk_here = jnp.zeros(dk_sum.shape, F32)
    for h in range(heads):
        span = slice(h * HEAD, (h + 1) * HEAD)
        q = q_ref[:, span]
        grad = (own_ref[:, span] + recv_ref[:, span].astype(F32)).astype(BF16)
        scores = lax.dot_general(q, keys, LAST, preferred_element_type=F32) * scale
        scores = jnp.where(rows >= cols, scores, -jnp.inf)
        exponent = jnp.exp(scores - jnp.max(scores, axis=1, keepdims=True))
        probs = exponent / jnp.sum(exponent, axis=1, keepdims=True)
        prob_grad = lax.dot_general(grad, vals, LAST, preferred_element_type=F32)
        row_dot = jnp.sum(grad.astype(F32) * ao_ref[:, span].astype(F32), axis=1, keepdims=True)
        score_grad = (probs * (prob_grad - row_dot)).astype(BF16)
        dq_ref[:, span] = (jnp.dot(score_grad, keys, preferred_element_type=F32) * scale).astype(BF16)
        dk_here += lax.dot_general(score_grad, q, FIRST, preferred_element_type=F32)
    dk_sum[...] += dk_here

    @pl.when(step == pl.num_programs(0) - 1)
    def _():
        dk_ref[...] = (dk_sum[...] * scale).astype(BF16)


def score_gradients(q, k, v, ao, own, recv):
    seq, width = q.shape
    heads = 2
    count = width // HEAD
    wide = pl.BlockSpec((seq, heads * HEAD), lambda i: (0, i))
    narrow = whole((seq, HEAD))
    return pl.pallas_call(
        functools.partial(score_kernel, HEAD**-0.5, heads),
        grid=(count // heads,),
        in_specs=[wide, narrow, narrow, wide, wide, wide],
        out_specs=[wide, narrow],
        out_shape=[jax.ShapeDtypeStruct((seq, width), BF16), jax.ShapeDtypeStruct((seq, HEAD), BF16)],
        scratch_shapes=[pltpu.VMEM((seq, HEAD), F32)],
        cost_estimate=LIGHT,
        compiler_params=limits(),
    )(q, k, v, ao, own, recv)


def input_kernel(place, dv_ref, wv_ref, keep_ref, give_ref):
    xl, c = place[0], place[1]
    wv = wv_ref[...]
    for other in range(2):
        for xh in range(2):
            index = (xl + other) % 2 * 2 + xh
            keep_ref[index] = lax.dot_general(dv_ref[other, xh, c], wv, LAST, preferred_element_type=F32)
            give = lax.dot_general(dv_ref[other, xh, 1 - c], wv, LAST, preferred_element_type=F32)
            give_ref[index] = give.astype(BF16)


def input_parts(place, dv, wv):
    rows = dv.shape[3]
    half = wv.shape[0]
    shape = (4, rows, half)
    return pl.pallas_call(
        input_kernel,
        grid_spec=pltpu.PrefetchScalarGridSpec(
            num_scalar_prefetch=1,
            grid=(1,),
            in_specs=[whole(dv.shape), whole(wv.shape)],
            out_specs=[whole(shape), whole(shape)],
        ),
        out_shape=[jax.ShapeDtypeStruct(shape, F32), jax.ShapeDtypeStruct(shape, BF16)],
        cost_estimate=LIGHT,
        compiler_params=limits(),
    )(place, dv, wv)


def value_kernel(cols, place, near_ref, far_ref, dv_ref, part_ref, rows_ref):
    gather_rows(place[0], place[1], near_ref, far_ref, rows_ref)
    total = lax.dot_general(rows_ref[...], dv_ref[...], FIRST, preferred_element_type=F32)
    for i in range(part_ref.shape[0]):
        part_ref[i] = total[i * cols : (i + 1) * cols].astype(BF16)


def value_parts(place, near, far, dv, cols):
    tokens = dv.shape[0]
    half = near.shape[2]
    shape = (half // cols, cols, HEAD)
    return pl.pallas_call(
        functools.partial(value_kernel, cols),
        grid_spec=pltpu.PrefetchScalarGridSpec(
            num_scalar_prefetch=1,
            grid=(1,),
            in_specs=[whole(near.shape), whole(far.shape), whole(dv.shape)],
            out_specs=whole(shape),
            scratch_shapes=[pltpu.VMEM((tokens, half), BF16)],
        ),
        out_shape=jax.ShapeDtypeStruct(shape, BF16),
        cost_estimate=LIGHT,
        compiler_params=limits(),
    )(place, near, far, dv)


def pair_rows(array, n_xl):
    rows, feats = array.shape
    halves = array.reshape(rows, n_xl, 1, feats // n_xl).transpose(1, 2, 0, 3)
    return jnp.broadcast_to(halves, (n_xl, 2, rows, feats // n_xl)).reshape(n_xl * 2, rows, feats // n_xl)


def on_device(queries, keys, values, attn_out, layer_in, out_grad, w_out, w_value):
    xl, y, xh, c = (lax.axis_index(a) for a in ("xl", "y", "xh", "c"))
    place = jnp.stack([xl, c, y]).astype(jnp.int32)
    n_xl, n_z, n_y = SIZES["xl"], SIZES["z"], SIZES["y"]
    n_dp = n_xl * n_z * n_y
    q, k, v, ao, li, og = (a[0] for a in (queries, keys, values, attn_out, layer_in, out_grad))
    seq, width = q.shape
    rows, feats = og.shape
    half = feats // n_xl
    cols = feats // n_dp

    shard = jnp.concatenate([w_out.T, w_value], axis=1)
    plane = in_order(place, [shard] + [shift(shard, "y", step) for step in range(1, n_y)])
    weights = lax.all_gather(plane.reshape(n_y * cols, width + HEAD), "z", axis=0, tiled=True)

    ao_other = shift(ao, "xl", 1)
    near = lax.all_to_all(after(pair_rows(og, n_xl), ao_other, plane), ("xl", "xh"), 0, 0, tiled=True)
    far = shift(near, "c", 1)
    q_other = shift(after(q, near), "xl", 1)
    k_other = shift(after(k, near), "xl", 1)

    grads, part = out_part(place, near, far, ao, ao_other)
    part = lax.psum_scatter(part, "z", scatter_dimension=0, tiled=True)

    li_near = lax.all_to_all(after(pair_rows(li, n_xl), grads, k_other), ("xl", "xh"), 0, 0, tiled=True)
    li_far = shift(li_near, "c", 1)

    probs = probabilities(after(q, near), k)
    probs_other = probabilities(q_other, k_other)

    weights, li_far = lax.optimization_barrier((weights, li_far))
    own, send, dv_own, dv_send = head_parts(grads, weights, probs, probs_other, width)
    dv_recv = shift(dv_send, "xl", 1)
    dv = (dv_own + dv_recv[::-1].astype(F32)).astype(BF16)
    value_grad = dv[0]
    recv = shift(after(send, dv_recv), "xl", 1)

    value_part = value_parts(place, li_near, li_far, dv.reshape(n_xl * seq, HEAD), cols)
    value_part = lax.all_to_all(value_part, ("z", "y"), 0, 0, tiled=True)

    keep, give = input_parts(place, dv.reshape(2, 2, 2, rows, HEAD), weights[:, width:])
    keep = (keep + shift(give, "c", 1).astype(F32)).reshape(n_xl, 2, rows, half)
    give = lax.dynamic_slice(keep, (0, 1 - xh, 0, 0), (n_xl, 1, rows, half)).astype(BF16)
    keep = lax.dynamic_slice(keep, (0, xh, 0, 0), (n_xl, 1, rows, half))
    give = shift(give, "xh", 1)

    value_part, recv, give = lax.optimization_barrier((value_part, recv, give))
    part = lax.all_to_all(part.reshape(n_y, cols, width), "y", 0, 0, tiled=True)
    out_weight_grad = (jnp.sum(part.astype(F32), axis=0) / n_dp).T
    value_weight_grad = jnp.sum(value_part.astype(F32), axis=0) / n_dp
    keep = (keep + give.astype(F32)).astype(BF16).reshape(n_xl, rows, half)
    mine = lax.dynamic_index_in_dim(keep, xl, 0, False)
    other = shift(lax.dynamic_index_in_dim(keep, 1 - xl, 0, False), "xl", 1)
    input_grad = jnp.where(
        xl == 0, jnp.concatenate([mine, other], axis=1), jnp.concatenate([other, mine], axis=1)
    )
    query_grad, key_grad = score_gradients(q, k, v, ao, own, recv)

    return (
        query_grad[None],
        key_grad[None],
        value_grad[None],
        input_grad[None],
        out_weight_grad,
        value_weight_grad,
    )


def solution(mesh):
    fine = Mesh(mesh.devices.reshape(tuple(SIZES.values())), tuple(SIZES))
    heads = P(DP, None, TENSOR)
    tokens = P(DP, TENSOR, None)
    return jax.shard_map(
        on_device,
        mesh=fine,
        in_specs=(heads, heads, heads, heads, tokens, tokens, P(TENSOR, DP), P(DP, TENSOR)),
        out_specs=(heads, heads, heads, tokens, P(TENSOR, DP), P(DP, TENSOR)),
        check_vma=False,
    )
```

```python
import functools

import jax
import jax.numpy as jnp
from jax import lax
from jax.experimental import pallas as pl
from jax.experimental.pallas import tpu as pltpu
from jax.sharding import Mesh
from jax.sharding import PartitionSpec as P

HEAD = 128
SIZES = {"xl": 2, "z": 8, "y": 4, "xh": 2, "c": 2}
DP = ("xl", "z", "y")
TENSOR = ("xh", "c")
F32 = jnp.float32
BF16 = jnp.bfloat16


def shift(array, axis, by):
    count = SIZES[axis]
    return lax.ppermute(array, axis, [(i, (i + by) % count) for i in range(count)])


LAST = (((1,), (1,)), ((), ()))
FIRST = (((0,), (0,)), ((), ()))


def after(array, *earlier):
    return lax.optimization_barrier((array,) + earlier)[0]


LIGHT = pl.CostEstimate(flops=1, bytes_accessed=1, transcendentals=0)


def limits():
    return pltpu.CompilerParams(vmem_limit_bytes=56 * 1024 * 1024)


def whole(shape):
    return pl.BlockSpec(shape, lambda *_: (0,) * len(shape))


def probs_kernel(scale, heads, q_ref, k_ref, probs_ref):
    keys = k_ref[...]
    seq = keys.shape[0]
    rows = lax.broadcasted_iota(jnp.int32, (seq, seq), 0)
    cols = lax.broadcasted_iota(jnp.int32, (seq, seq), 1)
    for h in range(heads):
        q = q_ref[:, h * HEAD : (h + 1) * HEAD]
        scores = lax.dot_general(keys, q, LAST, preferred_element_type=F32) * scale
        scores = jnp.where(cols >= rows, scores, -jnp.inf)
        exponent = jnp.exp(scores - jnp.max(scores, axis=0, keepdims=True))
        probs_ref[h] = (exponent / jnp.sum(exponent, axis=0, keepdims=True)).astype(BF16)


def probabilities(q, k):
    seq, width = q.shape
    heads = 2
    count = width // HEAD
    return pl.pallas_call(
        functools.partial(probs_kernel, HEAD**-0.5, heads),
        grid=(count // heads,),
        in_specs=[pl.BlockSpec((seq, heads * HEAD), lambda i: (0, i)), whole((seq, HEAD))],
        out_specs=pl.BlockSpec((heads, seq, seq), lambda i: (i, 0, 0)),
        out_shape=jax.ShapeDtypeStruct((count, seq, seq), BF16),
        cost_estimate=LIGHT,
        compiler_params=limits(),
    )(q, k)


def plane_kernel(place, *refs):
    n_y = len(refs) - 1
    for k in range(n_y):
        refs[n_y][(place[2] + n_y - k) % n_y] = refs[k][...]


def in_order(place, pieces):
    shape = (len(pieces),) + pieces[0].shape
    return pl.pallas_call(
        plane_kernel,
        grid_spec=pltpu.PrefetchScalarGridSpec(
            num_scalar_prefetch=1,
            grid=(1,),
            in_specs=[whole(piece.shape) for piece in pieces],
            out_specs=whole(shape),
        ),
        out_shape=jax.ShapeDtypeStruct(shape, BF16),
        cost_estimate=LIGHT,
        compiler_params=limits(),
    )(place, *pieces)


def gather_rows(xl, c, near_ref, far_ref, rows_ref):
    rows = near_ref.shape[1]
    for other in range(2):
        for xh in range(2):
            index = (xl + other) % 2 * 2 + xh
            start = (other * 2 + xh) * 2 * rows
            rows_ref[pl.ds(pl.multiple_of(start + c * rows, rows), rows)] = near_ref[index]
            rows_ref[pl.ds(pl.multiple_of(start + (1 - c) * rows, rows), rows)] = far_ref[index]


def out_kernel(place, near_ref, far_ref, ao_ref, ao_other_ref, grads_ref, part_ref):
    step = pl.program_id(0)
    seq = ao_ref.shape[0]

    @pl.when(step == 0)
    def _():
        gather_rows(place[0], place[1], near_ref, far_ref, grads_ref)

    chunk = part_ref.shape[0]
    span = pl.ds(pl.multiple_of(step * chunk, chunk), chunk)
    total = lax.dot_general(grads_ref[:seq, span], ao_ref[...], FIRST, preferred_element_type=F32)
    total += lax.dot_general(grads_ref[seq:, span], ao_other_ref[...], FIRST, preferred_element_type=F32)
    part_ref[...] = total.astype(BF16)


def out_part(place, near, far, ao, ao_other):
    seq, width = ao.shape
    half = near.shape[2]
    chunk = half // 5
    return pl.pallas_call(
        out_kernel,
        grid_spec=pltpu.PrefetchScalarGridSpec(
            num_scalar_prefetch=1,
            grid=(half // chunk,),
            in_specs=[whole(near.shape), whole(far.shape), whole(ao.shape), whole(ao.shape)],
            out_specs=[whole((2 * seq, half)), pl.BlockSpec((chunk, width), lambda i, place: (i, 0))],
        ),
        out_shape=[jax.ShapeDtypeStruct((2 * seq, half), BF16), jax.ShapeDtypeStruct((half, width), BF16)],
        cost_estimate=LIGHT,
        compiler_params=limits(),
    )(place, near, far, ao, ao_other)


def head_kernel(heads, grads_ref, w_ref, probs_ref, probs_other_ref, own_ref, send_ref, dv_ref, dv_send_ref, sums):
    step = pl.program_id(0)

    @pl.when(step == 0)
    def _():
        sums[...] = jnp.zeros_like(sums)

    seq = own_ref.shape[0]
    both = jnp.dot(grads_ref[...], w_ref[...], preferred_element_type=F32)
    own_ref[...] = both[:seq]
    low = both.astype(BF16)
    send_ref[...] = low[seq:]
    for i, ref in enumerate((probs_ref, probs_other_ref)):
        total = sums[i]
        for h in range(heads):
            piece = low[i * seq : (i + 1) * seq, h * HEAD : (h + 1) * HEAD]
            total += jnp.dot(ref[h], piece, preferred_element_type=F32)
        sums[i] = total

    @pl.when(step == pl.num_programs(0) - 1)
    def _():
        dv_ref[...] = sums[...]
        dv_send_ref[...] = sums[...].astype(BF16)


def head_parts(grads, weights, probs, probs_other, width):
    tokens, half = grads.shape
    seq = tokens // 2
    heads = 2
    block = heads * HEAD
    pairs = pl.BlockSpec((heads, seq, seq), lambda i: (i, 0, 0))
    wide = pl.BlockSpec((seq, block), lambda i: (0, i))
    return pl.pallas_call(
        functools.partial(head_kernel, heads),
        grid=(width // block,),
        in_specs=[whole(grads.shape), pl.BlockSpec((half, block), lambda i: (0, i)), pairs, pairs],
        out_specs=[wide, wide, whole((2, seq, HEAD)), whole((2, seq, HEAD))],
        out_shape=[
            jax.ShapeDtypeStruct((seq, width), F32),
            jax.ShapeDtypeStruct((seq, width), BF16),
            jax.ShapeDtypeStruct((2, seq, HEAD), F32),
            jax.ShapeDtypeStruct((2, seq, HEAD), BF16),
        ],
        scratch_shapes=[pltpu.VMEM((2, seq, HEAD), F32)],
        cost_estimate=LIGHT,
        compiler_params=limits(),
    )(grads, weights, probs, probs_other)


def score_kernel(scale, heads, q_ref, k_ref, v_ref, ao_ref, own_ref, recv_ref, dq_ref, dk_ref, dk_sum):
    step = pl.program_id(0)

    @pl.when(step == 0)
    def _():
        dk_sum[...] = jnp.zeros_like(dk_sum)

    keys = k_ref[...]
    vals = v_ref[...]
    seq = keys.shape[0]
    rows = lax.broadcasted_iota(jnp.int32, (seq, seq), 0)
    cols = lax.broadcasted_iota(jnp.int32, (seq, seq), 1)
    dk_here = jnp.zeros(dk_sum.shape, F32)
    for h in range(heads):
        span = slice(h * HEAD, (h + 1) * HEAD)
        q = q_ref[:, span]
        grad = (own_ref[:, span] + recv_ref[:, span].astype(F32)).astype(BF16)
        scores = lax.dot_general(q, keys, LAST, preferred_element_type=F32) * scale
        scores = jnp.where(rows >= cols, scores, -jnp.inf)
        exponent = jnp.exp(scores - jnp.max(scores, axis=1, keepdims=True))
        probs = exponent / jnp.sum(exponent, axis=1, keepdims=True)
        prob_grad = lax.dot_general(grad, vals, LAST, preferred_element_type=F32)
        row_dot = jnp.sum(grad.astype(F32) * ao_ref[:, span].astype(F32), axis=1, keepdims=True)
        score_grad = (probs * (prob_grad - row_dot)).astype(BF16)
        dq_ref[:, span] = (jnp.dot(score_grad, keys, preferred_element_type=F32) * scale).astype(BF16)
        dk_here += lax.dot_general(score_grad, q, FIRST, preferred_element_type=F32)
    dk_sum[...] += dk_here

    @pl.when(step == pl.num_programs(0) - 1)
    def _():
        dk_ref[...] = (dk_sum[...] * scale).astype(BF16)


def score_gradients(q, k, v, ao, own, recv):
    seq, width = q.shape
    heads = 2
    count = width // HEAD
    wide = pl.BlockSpec((seq, heads * HEAD), lambda i: (0, i))
    narrow = whole((seq, HEAD))
    return pl.pallas_call(
        functools.partial(score_kernel, HEAD**-0.5, heads),
        grid=(count // heads,),
        in_specs=[wide, narrow, narrow, wide, wide, wide],
        out_specs=[wide, narrow],
        out_shape=[jax.ShapeDtypeStruct((seq, width), BF16), jax.ShapeDtypeStruct((seq, HEAD), BF16)],
        scratch_shapes=[pltpu.VMEM((seq, HEAD), F32)],
        cost_estimate=LIGHT,
        compiler_params=limits(),
    )(q, k, v, ao, own, recv)


def input_kernel(place, dv_ref, wv_ref, keep_ref, give_ref):
    xl, c = place[0], place[1]
    wv = wv_ref[...]
    for other in range(2):
        for xh in range(2):
            index = (xl + other) % 2 * 2 + xh
            keep_ref[index] = lax.dot_general(dv_ref[other, xh, c], wv, LAST, preferred_element_type=F32)
            give = lax.dot_general(dv_ref[other, xh, 1 - c], wv, LAST, preferred_element_type=F32)
            give_ref[index] = give.astype(BF16)


def input_parts(place, dv, wv):
    rows = dv.shape[3]
    half = wv.shape[0]
    shape = (4, rows, half)
    return pl.pallas_call(
        input_kernel,
        grid_spec=pltpu.PrefetchScalarGridSpec(
            num_scalar_prefetch=1,
            grid=(1,),
            in_specs=[whole(dv.shape), whole(wv.shape)],
            out_specs=[whole(shape), whole(shape)],
        ),
        out_shape=[jax.ShapeDtypeStruct(shape, F32), jax.ShapeDtypeStruct(shape, BF16)],
        cost_estimate=LIGHT,
        compiler_params=limits(),
    )(place, dv, wv)


def value_kernel(cols, place, near_ref, far_ref, dv_ref, part_ref, rows_ref):
    gather_rows(place[0], place[1], near_ref, far_ref, rows_ref)
    total = lax.dot_general(rows_ref[...], dv_ref[...], FIRST, preferred_element_type=F32)
    for i in range(part_ref.shape[0]):
        part_ref[i] = total[i * cols : (i + 1) * cols].astype(BF16)


def value_parts(place, near, far, dv, cols):
    tokens = dv.shape[0]
    half = near.shape[2]
    shape = (half // cols, cols, HEAD)
    return pl.pallas_call(
        functools.partial(value_kernel, cols),
        grid_spec=pltpu.PrefetchScalarGridSpec(
            num_scalar_prefetch=1,
            grid=(1,),
            in_specs=[whole(near.shape), whole(far.shape), whole(dv.shape)],
            out_specs=whole(shape),
            scratch_shapes=[pltpu.VMEM((tokens, half), BF16)],
        ),
        out_shape=jax.ShapeDtypeStruct(shape, BF16),
        cost_estimate=LIGHT,
        compiler_params=limits(),
    )(place, near, far, dv)


def pair_rows(array, n_xl):
    rows, feats = array.shape
    halves = array.reshape(rows, n_xl, 1, feats // n_xl).transpose(1, 2, 0, 3)
    return jnp.broadcast_to(halves, (n_xl, 2, rows, feats // n_xl)).reshape(n_xl * 2, rows, feats // n_xl)


def on_device(queries, keys, values, attn_out, layer_in, out_grad, w_out, w_value):
    xl, y, xh, c = (lax.axis_index(a) for a in ("xl", "y", "xh", "c"))
    place = jnp.stack([xl, c, y]).astype(jnp.int32)
    n_xl, n_z, n_y = SIZES["xl"], SIZES["z"], SIZES["y"]
    n_dp = n_xl * n_z * n_y
    q, k, v, ao, li, og = (a[0] for a in (queries, keys, values, attn_out, layer_in, out_grad))
    seq, width = q.shape
    rows, feats = og.shape
    half = feats // n_xl
    cols = feats // n_dp

    shard = jnp.concatenate([w_out.T, w_value], axis=1)
    plane = in_order(place, [shard] + [shift(shard, "y", step) for step in range(1, n_y)])
    weights = lax.all_gather(plane.reshape(n_y * cols, width + HEAD), "z", axis=0, tiled=True)

    ao_other = shift(ao, "xl", 1)
    near = lax.all_to_all(pair_rows(og, n_xl), ("xl", "xh"), 0, 0, tiled=True)
    near = after(near, ao_other, plane)
    far = shift(near, "c", 1)

    grads, part = out_part(place, near, far, ao, ao_other)
    part = lax.psum_scatter(part, "z", scatter_dimension=0, tiled=True)

    q_other = shift(after(q, grads), "xl", 1)
    k_other = shift(after(k, grads), "xl", 1)
    li_near = lax.all_to_all(after(pair_rows(li, n_xl), grads), ("xl", "xh"), 0, 0, tiled=True)
    li_near = after(li_near, q_other, k_other)
    li_far = shift(li_near, "c", 1)
    probs = probabilities(after(q, grads), k)
    probs_other = probabilities(q_other, k_other)

    weights, li_far = lax.optimization_barrier((weights, li_far))
    own, send, dv_own, dv_send = head_parts(grads, weights, probs, probs_other, width)
    dv_recv = shift(dv_send, "xl", 1)
    dv = (dv_own + dv_recv[::-1].astype(F32)).astype(BF16)
    value_grad = dv[0]
    recv = shift(send, "xl", 1)

    keep, give = input_parts(place, dv.reshape(2, 2, 2, rows, HEAD), weights[:, width:])
    keep = (keep + shift(give, "c", 1).astype(F32)).reshape(n_xl, 2, rows, half)
    give = lax.dynamic_slice(keep, (0, 1 - xh, 0, 0), (n_xl, 1, rows, half)).astype(BF16)
    keep = lax.dynamic_slice(keep, (0, xh, 0, 0), (n_xl, 1, rows, half))
    give, recv = lax.optimization_barrier((give, recv))

    value_part = value_parts(place, li_near, li_far, dv.reshape(n_xl * seq, HEAD), cols)
    value_part = lax.all_to_all(after(value_part, give), ("z", "y"), 0, 0, tiled=True)
    give = shift(give, "xh", 1)

    keep = (keep + give.astype(F32)).astype(BF16).reshape(n_xl, rows, half)
    mine = lax.dynamic_index_in_dim(keep, xl, 0, False)
    other = lax.dynamic_index_in_dim(keep, 1 - xl, 0, False)
    other = shift(other, "xl", 1)
    input_grad = jnp.where(
        xl == 0, jnp.concatenate([mine, other], axis=1), jnp.concatenate([other, mine], axis=1)
    )
    query_grad, key_grad = score_gradients(q, k, v, ao, own, recv)

    value_weight_grad = jnp.sum(value_part.astype(F32), axis=0) / n_dp
    part = lax.all_to_all(after(part, value_part, give).reshape(n_y, cols, width), "y", 0, 0, tiled=True)
    out_weight_grad = (jnp.sum(part.astype(F32), axis=0) / n_dp).T

    return (
        query_grad[None],
        key_grad[None],
        value_grad[None],
        input_grad[None],
        out_weight_grad,
        value_weight_grad,
    )


def solution(mesh):
    fine = Mesh(mesh.devices.reshape(tuple(SIZES.values())), tuple(SIZES))
    heads = P(DP, None, TENSOR)
    tokens = P(DP, TENSOR, None)
    return jax.shard_map(
        on_device,
        mesh=fine,
        in_specs=(heads, heads, heads, heads, tokens, tokens, P(TENSOR, DP), P(DP, TENSOR)),
        out_specs=(heads, heads, heads, tokens, P(TENSOR, DP), P(DP, TENSOR)),
        check_vma=False,
    )
```

```python
import functools

import jax
import jax.numpy as jnp
from jax import lax
from jax.experimental import pallas as pl
from jax.experimental.pallas import tpu as pltpu
from jax.sharding import Mesh
from jax.sharding import PartitionSpec as P

HEAD = 128
SIZES = {"xl": 2, "z": 8, "y": 4, "xh": 2, "c": 2}
DP = ("xl", "z", "y")
TENSOR = ("xh", "c")
F32 = jnp.float32
BF16 = jnp.bfloat16


def shift(array, axis, by):
    count = SIZES[axis]
    return lax.ppermute(array, axis, [(i, (i + by) % count) for i in range(count)])


LAST = (((1,), (1,)), ((), ()))
FIRST = (((0,), (0,)), ((), ()))


def after(array, *earlier):
    return lax.optimization_barrier((array,) + earlier)[0]


LIGHT = pl.CostEstimate(flops=1, bytes_accessed=1, transcendentals=0)


def limits():
    return pltpu.CompilerParams(vmem_limit_bytes=16 * 1024 * 1024)


def whole(shape):
    return pl.BlockSpec(shape, lambda *_: (0,) * len(shape))


def probs_kernel(scale, heads, q_ref, k_ref, probs_ref):
    keys = k_ref[...]
    seq = keys.shape[0]
    rows = lax.broadcasted_iota(jnp.int32, (seq, seq), 0)
    cols = lax.broadcasted_iota(jnp.int32, (seq, seq), 1)
    for h in range(heads):
        q = q_ref[:, h * HEAD : (h + 1) * HEAD]
        scores = lax.dot_general(keys, q, LAST, preferred_element_type=F32) * scale
        scores = jnp.where(cols >= rows, scores, -jnp.inf)
        exponent = jnp.exp(scores - jnp.max(scores, axis=0, keepdims=True))
        probs_ref[h] = (exponent / jnp.sum(exponent, axis=0, keepdims=True)).astype(BF16)


def probabilities(q, k):
    seq, width = q.shape
    heads = 2
    count = width // HEAD
    return pl.pallas_call(
        functools.partial(probs_kernel, HEAD**-0.5, heads),
        grid=(count // heads,),
        in_specs=[pl.BlockSpec((seq, heads * HEAD), lambda i: (0, i)), whole((seq, HEAD))],
        out_specs=pl.BlockSpec((heads, seq, seq), lambda i: (i, 0, 0)),
        out_shape=jax.ShapeDtypeStruct((count, seq, seq), BF16),
        cost_estimate=LIGHT,
        compiler_params=limits(),
    )(q, k)


def gather_rows(place, c, near_ref, far_ref, rows_ref):
    count = near_ref.shape[0] // 2
    rows = near_ref.shape[1]
    for k in range(count):
        for xh in range(2):
            index = (place + count - k) % count * 2 + xh
            start = (k * 2 + xh) * 2 * rows
            rows_ref[pl.ds(pl.multiple_of(start + c * rows, rows), rows)] = near_ref[index]
            rows_ref[pl.ds(pl.multiple_of(start + (1 - c) * rows, rows), rows)] = far_ref[index]


def out_kernel(place, near_ref, far_ref, *refs):
    ao_refs, (part_ref, grads_ref) = refs[:-2], refs[-2:]
    step = pl.program_id(0)
    seq = ao_refs[0].shape[0]

    @pl.when(step == 0)
    def _():
        gather_rows(place[2], place[1], near_ref, far_ref, grads_ref)

    chunk = part_ref.shape[0]
    span = pl.ds(pl.multiple_of(step * chunk, chunk), chunk)
    total = jnp.zeros(part_ref.shape, F32)
    for k, ao_ref in enumerate(ao_refs):
        total += lax.dot_general(
            grads_ref[k * seq : (k + 1) * seq, span], ao_ref[...], FIRST, preferred_element_type=F32
        )
    part_ref[...] = total.astype(BF16)


def out_part(place, near, far, aos):
    seq, width = aos[0].shape
    feats = near.shape[2]
    chunk = feats // 5
    return pl.pallas_call(
        out_kernel,
        grid_spec=pltpu.PrefetchScalarGridSpec(
            num_scalar_prefetch=1,
            grid=(feats // chunk,),
            in_specs=[whole(near.shape), whole(far.shape)] + [whole(ao.shape) for ao in aos],
            out_specs=pl.BlockSpec((chunk, width), lambda i, place: (i, 0)),
            scratch_shapes=[pltpu.VMEM((len(aos) * seq, feats), BF16)],
        ),
        out_shape=jax.ShapeDtypeStruct((feats, width), BF16),
        cost_estimate=LIGHT,
        compiler_params=limits(),
    )(place, near, far, *aos)


def head_kernel(place, near_ref, far_ref, w_ref, *refs):
    own_ref, send_refs, grads_ref = refs[0], refs[1:-1], refs[-1]

    @pl.when(pl.program_id(0) == 0)
    def _():
        gather_rows(place[2], place[1], near_ref, far_ref, grads_ref)

    seq = own_ref.shape[0]
    product = jnp.dot(grads_ref[...], w_ref[...], preferred_element_type=F32)
    own_ref[...] = product[:seq]
    for k, ref in enumerate(send_refs):
        ref[...] = product[(k + 1) * seq : (k + 2) * seq].astype(BF16)


def head_parts(place, near, far, weights, seq, width):
    feats = near.shape[2]
    count = near.shape[0] // 2
    block = 256
    wide = pl.BlockSpec((seq, block), lambda i, place: (0, i))
    return pl.pallas_call(
        head_kernel,
        grid_spec=pltpu.PrefetchScalarGridSpec(
            num_scalar_prefetch=1,
            grid=(width // block,),
            in_specs=[whole(near.shape), whole(far.shape), pl.BlockSpec((feats, block), lambda i, place: (0, i))],
            out_specs=[wide] * count,
            scratch_shapes=[pltpu.VMEM((count * seq, feats), BF16)],
        ),
        out_shape=[jax.ShapeDtypeStruct((seq, width), F32)]
        + [jax.ShapeDtypeStruct((seq, width), BF16)] * (count - 1),
        cost_estimate=LIGHT,
        compiler_params=limits(),
    )(place, near, far, weights)


def grad_kernel(heads, probs_ref, own_ref, *refs):
    recv_refs, (grad_ref, dv_ref) = refs[:-2], refs[-2:]
    total = jnp.zeros(dv_ref.shape, F32)
    for h in range(heads):
        span = slice(h * HEAD, (h + 1) * HEAD)
        grad = own_ref[:, span]
        for ref in recv_refs:
            grad += ref[:, span].astype(F32)
        grad = grad.astype(BF16)
        grad_ref[:, span] = grad
        total += jnp.dot(probs_ref[h], grad, preferred_element_type=F32)
    dv_ref[...] = total.astype(BF16)


def head_gradient(probs, own, recv):
    seq, width = own.shape
    return pl.pallas_call(
        functools.partial(grad_kernel, width // HEAD),
        out_shape=[jax.ShapeDtypeStruct((seq, width), BF16), jax.ShapeDtypeStruct((seq, HEAD), BF16)],
        cost_estimate=LIGHT,
        compiler_params=limits(),
    )(probs, own, *recv)


def score_kernel(scale, heads, q_ref, k_ref, v_ref, ao_ref, grad_ref, dq_ref, dk_ref, dk_sum):
    step = pl.program_id(0)

    @pl.when(step == 0)
    def _():
        dk_sum[...] = jnp.zeros_like(dk_sum)

    keys = k_ref[...]
    vals = v_ref[...]
    seq = keys.shape[0]
    rows = lax.broadcasted_iota(jnp.int32, (seq, seq), 0)
    cols = lax.broadcasted_iota(jnp.int32, (seq, seq), 1)
    dk_here = jnp.zeros(dk_sum.shape, F32)
    for h in range(heads):
        span = slice(h * HEAD, (h + 1) * HEAD)
        q = q_ref[:, span]
        grad = grad_ref[:, span]
        scores = lax.dot_general(q, keys, LAST, preferred_element_type=F32) * scale
        scores = jnp.where(rows >= cols, scores, -jnp.inf)
        exponent = jnp.exp(scores - jnp.max(scores, axis=1, keepdims=True))
        probs = exponent / jnp.sum(exponent, axis=1, keepdims=True)
        prob_grad = lax.dot_general(grad, vals, LAST, preferred_element_type=F32)
        row_dot = jnp.sum(grad.astype(F32) * ao_ref[:, span].astype(F32), axis=1, keepdims=True)
        score_grad = (probs * (prob_grad - row_dot)).astype(BF16)
        dq_ref[:, span] = (jnp.dot(score_grad, keys, preferred_element_type=F32) * scale).astype(BF16)
        dk_here += lax.dot_general(score_grad, q, FIRST, preferred_element_type=F32)
    dk_sum[...] += dk_here

    @pl.when(step == pl.num_programs(0) - 1)
    def _():
        dk_ref[...] = (dk_sum[...] * scale).astype(BF16)


def score_gradients(q, k, v, ao, grad):
    seq, width = q.shape
    heads = 2
    count = width // HEAD
    wide = pl.BlockSpec((seq, heads * HEAD), lambda i: (0, i))
    narrow = whole((seq, HEAD))
    return pl.pallas_call(
        functools.partial(score_kernel, HEAD**-0.5, heads),
        grid=(count // heads,),
        in_specs=[wide, narrow, narrow, wide, wide],
        out_specs=[wide, narrow],
        out_shape=[jax.ShapeDtypeStruct((seq, width), BF16), jax.ShapeDtypeStruct((seq, HEAD), BF16)],
        scratch_shapes=[pltpu.VMEM((seq, HEAD), F32)],
        cost_estimate=LIGHT,
        compiler_params=limits(),
    )(q, k, v, ao, grad)


def input_kernel(n_xl, n_z, cols, place, dv_ref, *refs):
    wv_refs, (keep_ref, give_ref, wv_all) = refs[:-3], refs[-3:]
    c, y, n_y = place[1], place[2], len(wv_refs)
    for k, ref in enumerate(wv_refs):
        from_y = (y + n_y - k) % n_y
        for z in range(n_z):
            for xl in range(n_xl):
                start = (xl * n_z + z) * n_y + from_y
                block = ref[(z * n_xl + xl) * cols : (z * n_xl + xl + 1) * cols].astype(F32)
                wv_all[pl.ds(pl.multiple_of(start * cols, 8), cols)] = block
    wv = wv_all[...].astype(BF16)
    for xh in range(2):
        keep_ref[xh] = lax.dot_general(dv_ref[xh, c], wv, LAST, preferred_element_type=F32)
        give = lax.dot_general(dv_ref[xh, 1 - c], wv, LAST, preferred_element_type=F32)
        give_ref[xh] = give.astype(BF16)


def input_parts(place, dv, wvs, n_xl, n_z, cols):
    rows = dv.shape[2]
    feats = len(wvs) * wvs[0].shape[0]
    shape = (2, rows, feats)
    return pl.pallas_call(
        functools.partial(input_kernel, n_xl, n_z, cols),
        grid_spec=pltpu.PrefetchScalarGridSpec(
            num_scalar_prefetch=1,
            grid=(1,),
            in_specs=[whole(dv.shape)] + [whole(wv.shape) for wv in wvs],
            out_specs=[whole(shape), whole(shape)],
            scratch_shapes=[pltpu.VMEM((feats, HEAD), F32)],
        ),
        out_shape=[jax.ShapeDtypeStruct(shape, F32), jax.ShapeDtypeStruct(shape, BF16)],
        cost_estimate=LIGHT,
        compiler_params=limits(),
    )(place, dv, *wvs)


def value_kernel(cols, place, near_ref, far_ref, dv_ref, part_ref, rows_ref):
    gather_rows(place[0], place[1], near_ref, far_ref, rows_ref)
    total = lax.dot_general(rows_ref[...], dv_ref[...], FIRST, preferred_element_type=F32)
    for i in range(part_ref.shape[0]):
        part_ref[i] = total[i * cols : (i + 1) * cols].astype(BF16)


def value_parts(place, near, far, dv, cols):
    tokens = dv.shape[0]
    half = near.shape[2]
    shape = (half // cols, cols, HEAD)
    return pl.pallas_call(
        functools.partial(value_kernel, cols),
        grid_spec=pltpu.PrefetchScalarGridSpec(
            num_scalar_prefetch=1,
            grid=(1,),
            in_specs=[whole(near.shape), whole(far.shape), whole(dv.shape)],
            out_specs=whole(shape),
            scratch_shapes=[pltpu.VMEM((tokens, half), BF16)],
        ),
        out_shape=jax.ShapeDtypeStruct(shape, BF16),
        cost_estimate=LIGHT,
        compiler_params=limits(),
    )(place, near, far, dv)


def for_each(parts):
    both = jnp.broadcast_to(parts[:, None], (parts.shape[0], 2) + parts.shape[1:])
    return both.reshape((parts.shape[0] * 2,) + parts.shape[1:])


def on_device(queries, keys, values, attn_out, layer_in, out_grad, w_out, w_value):
    xl, y, xh, c = (lax.axis_index(a) for a in ("xl", "y", "xh", "c"))
    place = jnp.stack([xl, c, y]).astype(jnp.int32)
    n_xl, n_z, n_y = SIZES["xl"], SIZES["z"], SIZES["y"]
    n_dp = n_xl * n_z * n_y
    q, k, v, ao, li, og = (a[0] for a in (queries, keys, values, attn_out, layer_in, out_grad))
    seq, width = q.shape
    rows, feats = og.shape
    half = feats // n_xl
    quarter = feats // n_y
    cols = feats // n_dp

    shard = jnp.concatenate([w_out.T, w_value], axis=1)
    other = shift(shard, "xl", 1)
    plane = jnp.where(xl == 0, jnp.concatenate([shard, other]), jnp.concatenate([other, shard]))
    weights = lax.all_gather(plane, "z", axis=0, tiled=True)

    by_xl = after(li, plane).reshape(rows, n_xl, half).transpose(1, 0, 2)
    li_near = lax.all_to_all(for_each(by_xl), ("xl", "xh"), 0, 0, tiled=True)
    li_far = shift(li_near, "c", 1)

    aos = [ao] + [shift(after(ao, plane), "y", step) for step in range(1, n_y)]
    by_y = og.reshape(rows, n_xl, n_z, n_y, cols).transpose(3, 0, 2, 1, 4).reshape(n_y, rows, quarter)
    by_y = after(for_each(by_y), li_near, aos[1], aos[n_y - 1])
    near = lax.all_to_all(by_y, ("y", "xh"), 0, 0, tiled=True)
    far = shift(near, "c", 1)

    own, *sends = head_parts(place, near, far, weights, seq, width)
    wv = weights[:, width:]
    wvs = [wv] + [shift(wv, "y", step) for step in range(1, n_y)]
    sends = [after(send, *wvs) for send in sends]
    recv = [shift(send, "y", -step - 1) for step, send in enumerate(sends)]
    probs = probabilities(after(q, near), k)

    part = out_part(place, near, far, aos)
    part = lax.psum_scatter(part, "z", scatter_dimension=0, tiled=True)

    li_far, *recv = lax.optimization_barrier((li_far, *recv))
    head_grad, value_grad = head_gradient(probs, own, recv)
    dv_other = shift(value_grad, "xl", 1)

    keep, give = input_parts(place, value_grad.reshape(2, 2, rows, HEAD), wvs, n_xl, n_z, cols)
    keep = keep + shift(after(give, dv_other), "c", 1).astype(F32)
    give = lax.dynamic_index_in_dim(keep, 1 - xh, 0, False).astype(BF16)
    keep = lax.dynamic_index_in_dim(keep, xh, 0, False)

    dv = jnp.concatenate([value_grad, dv_other])
    value_part = value_parts(place, li_near, li_far, dv, cols)
    value_part = lax.all_to_all(after(value_part, give, part), ("z", "y"), 0, 0, tiled=True)
    give = shift(give, "xh", 1)
    input_grad = (keep + give.astype(F32)).astype(BF16)

    query_grad, key_grad = score_gradients(q, k, v, ao, head_grad)

    part = after(part, give).reshape(n_xl, cols, width)
    mine = lax.dynamic_index_in_dim(part, xl, 0, False).astype(F32)
    other = shift(lax.dynamic_index_in_dim(part, 1 - xl, 0, False), "xl", 1)
    out_weight_grad = ((mine + other.astype(F32)) / n_dp).T
    value_weight_grad = jnp.sum(value_part.astype(F32), axis=0) / n_dp

    return (
        query_grad[None],
        key_grad[None],
        value_grad[None],
        input_grad[None],
        out_weight_grad,
        value_weight_grad,
    )


def solution(mesh):
    fine = Mesh(mesh.devices.reshape(tuple(SIZES.values())), tuple(SIZES))
    heads = P(DP, None, TENSOR)
    tokens = P(DP, TENSOR, None)
    return jax.shard_map(
        on_device,
        mesh=fine,
        in_specs=(heads, heads, heads, heads, tokens, tokens, P(TENSOR, DP), P(DP, TENSOR)),
        out_specs=(heads, heads, heads, tokens, P(TENSOR, DP), P(DP, TENSOR)),
        check_vma=False,
    )
```

```python
import functools

import jax
import jax.numpy as jnp
from jax import lax
from jax.experimental import pallas as pl
from jax.experimental.pallas import tpu as pltpu
from jax.sharding import Mesh
from jax.sharding import PartitionSpec as P

HEAD = 128
SIZES = {"xl": 2, "z": 8, "y": 4, "xh": 2, "c": 2}
DP = ("xl", "z", "y")
TENSOR = ("xh", "c")
F32 = jnp.float32
BF16 = jnp.bfloat16


def shift(array, axis, by):
    count = SIZES[axis]
    return lax.ppermute(array, axis, [(i, (i + by) % count) for i in range(count)])


LAST = (((1,), (1,)), ((), ()))
FIRST = (((0,), (0,)), ((), ()))


def after(array, *earlier):
    return lax.optimization_barrier((array,) + earlier)[0]


LIGHT = pl.CostEstimate(flops=1, bytes_accessed=1, transcendentals=0)


def limits():
    return pltpu.CompilerParams(vmem_limit_bytes=16 * 1024 * 1024)


def whole(shape):
    return pl.BlockSpec(shape, lambda *_: (0,) * len(shape))


def probs_kernel(scale, heads, q_ref, k_ref, probs_ref):
    keys = k_ref[...]
    seq = keys.shape[0]
    rows = lax.broadcasted_iota(jnp.int32, (seq, seq), 0)
    cols = lax.broadcasted_iota(jnp.int32, (seq, seq), 1)
    for h in range(heads):
        q = q_ref[:, h * HEAD : (h + 1) * HEAD]
        scores = lax.dot_general(keys, q, LAST, preferred_element_type=F32) * scale
        scores = jnp.where(cols >= rows, scores, -jnp.inf)
        exponent = jnp.exp(scores - jnp.max(scores, axis=0, keepdims=True))
        probs_ref[h] = (exponent / jnp.sum(exponent, axis=0, keepdims=True)).astype(BF16)


def probabilities(q, k):
    seq, width = q.shape
    heads = 2
    count = width // HEAD
    return pl.pallas_call(
        functools.partial(probs_kernel, HEAD**-0.5, heads),
        grid=(count // heads,),
        in_specs=[pl.BlockSpec((seq, heads * HEAD), lambda i: (0, i)), whole((seq, HEAD))],
        out_specs=pl.BlockSpec((heads, seq, seq), lambda i: (i, 0, 0)),
        out_shape=jax.ShapeDtypeStruct((count, seq, seq), BF16),
        cost_estimate=LIGHT,
        compiler_params=limits(),
    )(q, k)


def gather_rows(place, which, near_ref, far_ref, rows_ref):
    c, y = place[1], place[2]
    count = near_ref.shape[0] // 2
    rows = near_ref.shape[2]
    for k in range(count):
        for xh in range(2):
            index = (y + count - k) % count * 2 + xh
            start = (k * 2 + xh) * 2 * rows
            rows_ref[pl.ds(pl.multiple_of(start + c * rows, rows), rows)] = near_ref[index, which]
            rows_ref[pl.ds(pl.multiple_of(start + (1 - c) * rows, rows), rows)] = far_ref[index, which]


def out_kernel(place, near_ref, far_ref, *refs):
    ao_refs, (part_ref, grads_ref) = refs[:-2], refs[-2:]
    step = pl.program_id(0)
    seq = ao_refs[0].shape[0]

    @pl.when(step == 0)
    def _():
        gather_rows(place, 0, near_ref, far_ref, grads_ref)

    chunk = part_ref.shape[0]
    span = pl.ds(pl.multiple_of(step * chunk, chunk), chunk)
    total = jnp.zeros(part_ref.shape, F32)
    for k, ao_ref in enumerate(ao_refs):
        total += lax.dot_general(
            grads_ref[k * seq : (k + 1) * seq, span], ao_ref[...], FIRST, preferred_element_type=F32
        )
    part_ref[...] = total.astype(BF16)


def out_part(place, near, far, aos):
    seq, width = aos[0].shape
    feats = near.shape[3]
    chunk = feats // 5
    return pl.pallas_call(
        out_kernel,
        grid_spec=pltpu.PrefetchScalarGridSpec(
            num_scalar_prefetch=1,
            grid=(feats // chunk,),
            in_specs=[whole(near.shape), whole(far.shape)] + [whole(ao.shape) for ao in aos],
            out_specs=pl.BlockSpec((chunk, width), lambda i, place: (i, 0)),
            scratch_shapes=[pltpu.VMEM((len(aos) * seq, feats), BF16)],
        ),
        out_shape=jax.ShapeDtypeStruct((feats, width), BF16),
        cost_estimate=LIGHT,
        compiler_params=limits(),
    )(place, near, far, *aos)


def head_kernel(offsets, place, near_ref, far_ref, *refs):
    n_z = len(offsets)
    w_refs, wv_refs, refs = refs[:n_z], refs[n_z : 2 * n_z], refs[2 * n_z :]
    own_ref, send_refs, (wv_ref, grads_ref, w_all) = refs[0], refs[1:-3], refs[-3:]
    depth = w_refs[0].shape[0]

    def in_order(pieces, ref):
        for offset, piece in zip(offsets, pieces):
            start = (place[3] + offset + n_z) % n_z * depth
            ref[pl.ds(pl.multiple_of(start, depth), depth)] = piece[...]

    @pl.when(pl.program_id(0) == 0)
    def _():
        gather_rows(place, 0, near_ref, far_ref, grads_ref)
        in_order(wv_refs, wv_ref)

    in_order(w_refs, w_all)
    seq = own_ref.shape[0]
    product = jnp.dot(grads_ref[...], w_all[...], preferred_element_type=F32)
    own_ref[...] = product[:seq]
    for k, ref in enumerate(send_refs):
        ref[...] = product[(k + 1) * seq : (k + 2) * seq].astype(BF16)


def head_parts(place, near, far, pieces, seq, width):
    feats = near.shape[3]
    count = near.shape[0] // 2
    block = 256
    depth = feats // len(pieces)
    wide = pl.BlockSpec((seq, block), lambda i, place: (0, i))
    return pl.pallas_call(
        functools.partial(head_kernel, tuple(pieces)),
        grid_spec=pltpu.PrefetchScalarGridSpec(
            num_scalar_prefetch=1,
            grid=(width // block,),
            in_specs=[whole(near.shape), whole(far.shape)]
            + [pl.BlockSpec((depth, block), lambda i, place: (0, i))] * len(pieces)
            + [pl.BlockSpec((depth, HEAD), lambda i, place: (0, width // HEAD))] * len(pieces),
            out_specs=[wide] * count + [whole((feats, HEAD))],
            scratch_shapes=[pltpu.VMEM((count * seq, feats), BF16), pltpu.VMEM((feats, block), BF16)],
        ),
        out_shape=[jax.ShapeDtypeStruct((seq, width), F32)]
        + [jax.ShapeDtypeStruct((seq, width), BF16)] * (count - 1)
        + [jax.ShapeDtypeStruct((feats, HEAD), BF16)],
        cost_estimate=LIGHT,
        compiler_params=limits(),
    )(place, near, far, *pieces.values(), *pieces.values())


def grad_kernel(heads, probs_ref, own_ref, *refs):
    recv_refs, (grad_ref, dv_ref) = refs[:-2], refs[-2:]
    total = jnp.zeros(dv_ref.shape, F32)
    for h in range(heads):
        span = slice(h * HEAD, (h + 1) * HEAD)
        grad = own_ref[:, span]
        for ref in recv_refs:
            grad += ref[:, span].astype(F32)
        grad = grad.astype(BF16)
        grad_ref[:, span] = grad
        total += jnp.dot(probs_ref[h], grad, preferred_element_type=F32)
    dv_ref[...] = total.astype(BF16)


def head_gradient(probs, own, recv):
    seq, width = own.shape
    return pl.pallas_call(
        functools.partial(grad_kernel, width // HEAD),
        out_shape=[jax.ShapeDtypeStruct((seq, width), BF16), jax.ShapeDtypeStruct((seq, HEAD), BF16)],
        cost_estimate=LIGHT,
        compiler_params=limits(),
    )(probs, own, *recv)


def score_kernel(scale, heads, q_ref, k_ref, v_ref, ao_ref, grad_ref, dq_ref, dk_ref, dk_sum):
    step = pl.program_id(0)

    @pl.when(step == 0)
    def _():
        dk_sum[...] = jnp.zeros_like(dk_sum)

    keys = k_ref[...]
    vals = v_ref[...]
    seq = keys.shape[0]
    rows = lax.broadcasted_iota(jnp.int32, (seq, seq), 0)
    cols = lax.broadcasted_iota(jnp.int32, (seq, seq), 1)
    dk_here = jnp.zeros(dk_sum.shape, F32)
    for h in range(heads):
        span = slice(h * HEAD, (h + 1) * HEAD)
        q = q_ref[:, span]
        grad = grad_ref[:, span]
        scores = lax.dot_general(q, keys, LAST, preferred_element_type=F32) * scale
        scores = jnp.where(rows >= cols, scores, -jnp.inf)
        exponent = jnp.exp(scores - jnp.max(scores, axis=1, keepdims=True))
        probs = exponent / jnp.sum(exponent, axis=1, keepdims=True)
        prob_grad = lax.dot_general(grad, vals, LAST, preferred_element_type=F32)
        row_dot = jnp.sum(grad.astype(F32) * ao_ref[:, span].astype(F32), axis=1, keepdims=True)
        score_grad = (probs * (prob_grad - row_dot)).astype(BF16)
        dq_ref[:, span] = (jnp.dot(score_grad, keys, preferred_element_type=F32) * scale).astype(BF16)
        dk_here += lax.dot_general(score_grad, q, FIRST, preferred_element_type=F32)
    dk_sum[...] += dk_here

    @pl.when(step == pl.num_programs(0) - 1)
    def _():
        dk_ref[...] = (dk_sum[...] * scale).astype(BF16)


def score_gradients(q, k, v, ao, grad):
    seq, width = q.shape
    heads = 2
    count = width // HEAD
    wide = pl.BlockSpec((seq, heads * HEAD), lambda i: (0, i))
    narrow = whole((seq, HEAD))
    return pl.pallas_call(
        functools.partial(score_kernel, HEAD**-0.5, heads),
        grid=(count // heads,),
        in_specs=[wide, narrow, narrow, wide, wide],
        out_specs=[wide, narrow],
        out_shape=[jax.ShapeDtypeStruct((seq, width), BF16), jax.ShapeDtypeStruct((seq, HEAD), BF16)],
        scratch_shapes=[pltpu.VMEM((seq, HEAD), F32)],
        cost_estimate=LIGHT,
        compiler_params=limits(),
    )(q, k, v, ao, grad)


def input_kernel(n_xl, n_z, cols, place, dv_ref, *refs):
    wv_refs, (keep_ref, give_ref, wv_all) = refs[:-3], refs[-3:]
    c, y, n_y = place[1], place[2], len(wv_refs)
    for k, ref in enumerate(wv_refs):
        from_y = (y + n_y - k) % n_y
        for z in range(n_z):
            for xl in range(n_xl):
                start = (xl * n_z + z) * n_y + from_y
                block = ref[(z * n_xl + xl) * cols : (z * n_xl + xl + 1) * cols].astype(F32)
                wv_all[pl.ds(pl.multiple_of(start * cols, 8), cols)] = block
    wv = wv_all[...].astype(BF16)
    for xh in range(2):
        keep_ref[xh] = lax.dot_general(dv_ref[xh, c], wv, LAST, preferred_element_type=F32)
        give = lax.dot_general(dv_ref[xh, 1 - c], wv, LAST, preferred_element_type=F32)
        give_ref[xh] = give.astype(BF16)


def input_parts(place, dv, wvs, n_xl, n_z, cols):
    rows = dv.shape[2]
    feats = len(wvs) * wvs[0].shape[0]
    shape = (2, rows, feats)
    return pl.pallas_call(
        functools.partial(input_kernel, n_xl, n_z, cols),
        grid_spec=pltpu.PrefetchScalarGridSpec(
            num_scalar_prefetch=1,
            grid=(1,),
            in_specs=[whole(dv.shape)] + [whole(wv.shape) for wv in wvs],
            out_specs=[whole(shape), whole(shape)],
            scratch_shapes=[pltpu.VMEM((feats, HEAD), F32)],
        ),
        out_shape=[jax.ShapeDtypeStruct(shape, F32), jax.ShapeDtypeStruct(shape, BF16)],
        cost_estimate=LIGHT,
        compiler_params=limits(),
    )(place, dv, *wvs)


def value_kernel(n_xl, cols, place, near_ref, far_ref, *refs):
    dv_refs, (part_ref, rows_ref) = refs[:-2], refs[-2:]
    gather_rows(place, 1, near_ref, far_ref, rows_ref)
    seq = dv_refs[0].shape[0]
    total = jnp.zeros((rows_ref.shape[1], HEAD), F32)
    for k, ref in enumerate(dv_refs):
        total += lax.dot_general(rows_ref[k * seq : (k + 1) * seq], ref[...], FIRST, preferred_element_type=F32)
    count = part_ref.shape[0]
    for i in range(count):
        part_ref[i % n_xl * (count // n_xl) + i // n_xl] = total[i * cols : (i + 1) * cols].astype(BF16)


def value_parts(place, near, far, dvs, n_xl, cols):
    feats = near.shape[3]
    shape = (feats // cols, cols, HEAD)
    return pl.pallas_call(
        functools.partial(value_kernel, n_xl, cols),
        grid_spec=pltpu.PrefetchScalarGridSpec(
            num_scalar_prefetch=1,
            grid=(1,),
            in_specs=[whole(near.shape), whole(far.shape)] + [whole(dv.shape) for dv in dvs],
            out_specs=whole(shape),
            scratch_shapes=[pltpu.VMEM((len(dvs) * dvs[0].shape[0], feats), BF16)],
        ),
        out_shape=jax.ShapeDtypeStruct(shape, BF16),
        cost_estimate=LIGHT,
        compiler_params=limits(),
    )(place, near, far, *dvs)


def for_each(parts):
    both = jnp.broadcast_to(parts[:, None], (parts.shape[0], 2) + parts.shape[1:])
    return both.reshape((parts.shape[0] * 2,) + parts.shape[1:])


def on_device(queries, keys, values, attn_out, layer_in, out_grad, w_out, w_value):
    xl, z, y, xh, c = (lax.axis_index(a) for a in ("xl", "z", "y", "xh", "c"))
    place = jnp.stack([xl, c, y, z]).astype(jnp.int32)
    n_xl, n_z, n_y = SIZES["xl"], SIZES["z"], SIZES["y"]
    n_dp = n_xl * n_z * n_y
    q, k, v, ao, li, og = (a[0] for a in (queries, keys, values, attn_out, layer_in, out_grad))
    seq, width = q.shape
    rows, feats = og.shape
    quarter = feats // n_y
    cols = feats // n_dp

    shard = jnp.concatenate([w_out.T, w_value], axis=1)
    other = shift(shard, "xl", 1)
    plane = jnp.where(xl == 0, jnp.concatenate([shard, other]), jnp.concatenate([other, shard]))
    aos = [ao] + [shift(ao, "y", step) for step in range(1, n_y)]
    pieces = {0: plane}
    for step in range(1, n_z // 2):
        if step == 3:
            pieces[-2], pieces[2], _, _ = lax.optimization_barrier((pieces[-2], pieces[2], aos[1], aos[3]))
        pieces[-step] = shift(pieces[1 - step], "z", 1)
        pieces[step] = shift(pieces[step - 1], "z", -1)
    pieces[-n_z // 2] = shift(after(pieces[1 - n_z // 2], aos[2]), "z", 1)

    by_y = jnp.stack([og, li]).reshape(2, rows, n_xl, n_z, n_y, cols)
    by_y = by_y.transpose(4, 0, 1, 3, 2, 5).reshape(n_y, 2, rows, quarter)
    near = lax.all_to_all(for_each(by_y), ("y", "xh"), 0, 0, tiled=True)
    near = after(near, pieces[-2], pieces[2])
    far = shift(near, "c", 1)

    part = out_part(place, near, far, aos)
    near = after(near, part)
    part = lax.all_to_all(part.reshape(n_z, n_xl * cols, width), "z", 0, 0, tiled=True)
    part = jnp.sum(part.astype(F32), axis=0).astype(BF16)

    own, *sends, wv = head_parts(place, near, far, pieces, seq, width)
    recv = [shift(send, "y", -step - 1) for step, send in enumerate(sends)]
    probs = probabilities(after(q, sends[0]), k)
    wv, probs, *recv = lax.optimization_barrier((wv, probs, *recv))
    wvs = [wv] + [shift(wv, "y", step) for step in range(1, n_y)]
    head_grad, value_grad = head_gradient(probs, own, recv)
    dvs = [value_grad] + [shift(value_grad, "y", step) for step in range(1, n_y)]

    value_part = value_parts(place, near, far, dvs, n_xl, cols)
    value_part = lax.all_to_all(after(value_part, part), ("xl", "z"), 0, 0, tiled=True)

    keep, give = input_parts(place, value_grad.reshape(2, 2, rows, HEAD), wvs, n_xl, n_z, cols)
    keep = keep + shift(after(give, *dvs), "c", 1).astype(F32)
    give = lax.dynamic_index_in_dim(keep, 1 - xh, 0, False).astype(BF16)
    keep = lax.dynamic_index_in_dim(keep, xh, 0, False)
    give = shift(give, "xh", 1)
    head_grad = after(head_grad, give)
    input_grad = (keep + give.astype(F32)).astype(BF16)

    query_grad, key_grad = score_gradients(q, k, v, ao, head_grad)

    part = part.reshape(n_xl, cols, width)
    mine = lax.dynamic_index_in_dim(part, xl, 0, False).astype(F32)
    other = shift(lax.dynamic_index_in_dim(part, 1 - xl, 0, False), "xl", 1)
    out_weight_grad = ((mine + other.astype(F32)) / n_dp).T
    value_weight_grad = jnp.sum(value_part.astype(F32), axis=0) / n_dp

    return (
        query_grad[None],
        key_grad[None],
        value_grad[None],
        input_grad[None],
        out_weight_grad,
        value_weight_grad,
    )


def solution(mesh):
    fine = Mesh(mesh.devices.reshape(tuple(SIZES.values())), tuple(SIZES))
    heads = P(DP, None, TENSOR)
    tokens = P(DP, TENSOR, None)
    return jax.shard_map(
        on_device,
        mesh=fine,
        in_specs=(heads, heads, heads, heads, tokens, tokens, P(TENSOR, DP), P(DP, TENSOR)),
        out_specs=(heads, heads, heads, tokens, P(TENSOR, DP), P(DP, TENSOR)),
        check_vma=False,
    )
```

```python
import functools

import jax
import jax.numpy as jnp
from jax import lax
from jax.experimental import pallas as pl
from jax.experimental.pallas import tpu as pltpu
from jax.sharding import Mesh
from jax.sharding import PartitionSpec as P

HEAD = 128
SIZES = {"xl": 2, "z": 8, "y": 4, "xh": 2, "c": 2}
DP = ("xl", "z", "y")
TENSOR = ("xh", "c")
F32 = jnp.float32
BF16 = jnp.bfloat16


def shift(array, axis, by):
    count = SIZES[axis]
    return lax.ppermute(array, axis, [(i, (i + by) % count) for i in range(count)])


LAST = (((1,), (1,)), ((), ()))
FIRST = (((0,), (0,)), ((), ()))


def after(array, *earlier):
    return lax.optimization_barrier((array,) + earlier)[0]


LIGHT = pl.CostEstimate(flops=1, bytes_accessed=1, transcendentals=0)


def limits():
    return pltpu.CompilerParams(vmem_limit_bytes=16 * 1024 * 1024)


def whole(shape):
    return pl.BlockSpec(shape, lambda *_: (0,) * len(shape))


def probs_kernel(scale, heads, q_ref, k_ref, probs_ref):
    keys = k_ref[...]
    seq = keys.shape[0]
    rows = lax.broadcasted_iota(jnp.int32, (seq, seq), 0)
    cols = lax.broadcasted_iota(jnp.int32, (seq, seq), 1)
    for h in range(heads):
        q = q_ref[:, h * HEAD : (h + 1) * HEAD]
        scores = lax.dot_general(keys, q, LAST, preferred_element_type=F32) * scale
        scores = jnp.where(cols >= rows, scores, -jnp.inf)
        exponent = jnp.exp(scores - jnp.max(scores, axis=0, keepdims=True))
        probs_ref[h] = (exponent / jnp.sum(exponent, axis=0, keepdims=True)).astype(BF16)


def probabilities(q, k):
    seq, width = q.shape
    heads = 2
    count = width // HEAD
    return pl.pallas_call(
        functools.partial(probs_kernel, HEAD**-0.5, heads),
        grid=(count // heads,),
        in_specs=[pl.BlockSpec((seq, heads * HEAD), lambda i: (0, i)), whole((seq, HEAD))],
        out_specs=pl.BlockSpec((heads, seq, seq), lambda i: (i, 0, 0)),
        out_shape=jax.ShapeDtypeStruct((count, seq, seq), BF16),
        cost_estimate=LIGHT,
        compiler_params=limits(),
    )(q, k)


def gather_rows(position, c, near_ref, far_ref, rows_ref):
    count = near_ref.shape[0] // 2
    rows = near_ref.shape[1]
    for k in range(count):
        for xh in range(2):
            index = (position + count - k) % count * 2 + xh
            start = (k * 2 + xh) * 2 * rows
            rows_ref[pl.ds(pl.multiple_of(start + c * rows, rows), rows)] = near_ref[index]
            rows_ref[pl.ds(pl.multiple_of(start + (1 - c) * rows, rows), rows)] = far_ref[index]


def out_kernel(place, near_ref, far_ref, *refs):
    ao_refs, (part_ref, grads_ref) = refs[:-2], refs[-2:]
    step = pl.program_id(0)
    seq = ao_refs[0].shape[0]

    @pl.when(step == 0)
    def _():
        gather_rows(place[2], place[1], near_ref, far_ref, grads_ref)

    chunk = part_ref.shape[0]
    span = pl.ds(pl.multiple_of(step * chunk, chunk), chunk)
    total = jnp.zeros(part_ref.shape, F32)
    for k, ao_ref in enumerate(ao_refs):
        total += lax.dot_general(
            grads_ref[k * seq : (k + 1) * seq, span], ao_ref[...], FIRST, preferred_element_type=F32
        )
    part_ref[...] = total.astype(BF16)


def out_part(place, near, far, aos):
    seq, width = aos[0].shape
    feats = near.shape[2]
    chunk = feats // 5
    return pl.pallas_call(
        out_kernel,
        grid_spec=pltpu.PrefetchScalarGridSpec(
            num_scalar_prefetch=1,
            grid=(feats // chunk,),
            in_specs=[whole(near.shape), whole(far.shape)] + [whole(ao.shape) for ao in aos],
            out_specs=pl.BlockSpec((chunk, width), lambda i, place: (i, 0)),
            scratch_shapes=[pltpu.VMEM((len(aos) * seq, feats), BF16)],
        ),
        out_shape=jax.ShapeDtypeStruct((feats, width), BF16),
        cost_estimate=LIGHT,
        compiler_params=limits(),
    )(place, near, far, *aos)


def head_kernel(offsets, place, near_ref, far_ref, *refs):
    n_z = len(offsets)
    w_refs, wv_refs, refs = refs[:n_z], refs[n_z : 2 * n_z], refs[2 * n_z :]
    own_ref, send_refs, (wv_ref, grads_ref, w_all) = refs[0], refs[1:-3], refs[-3:]
    depth = w_refs[0].shape[0]

    def in_order(pieces, ref):
        for offset, piece in zip(offsets, pieces):
            start = (place[3] + offset + n_z) % n_z * depth
            ref[pl.ds(pl.multiple_of(start, depth), depth)] = piece[...]

    @pl.when(pl.program_id(0) == 0)
    def _():
        gather_rows(place[2], place[1], near_ref, far_ref, grads_ref)
        in_order(wv_refs, wv_ref)

    in_order(w_refs, w_all)
    seq = own_ref.shape[0]
    product = jnp.dot(grads_ref[...], w_all[...], preferred_element_type=F32)
    own_ref[...] = product[:seq]
    for k, ref in enumerate(send_refs):
        ref[...] = product[(k + 1) * seq : (k + 2) * seq].astype(BF16)


def head_parts(place, near, far, pieces, seq, width):
    feats = near.shape[2]
    count = near.shape[0] // 2
    block = 256
    depth = feats // len(pieces)
    wide = pl.BlockSpec((seq, block), lambda i, place: (0, i))
    return pl.pallas_call(
        functools.partial(head_kernel, tuple(pieces)),
        grid_spec=pltpu.PrefetchScalarGridSpec(
            num_scalar_prefetch=1,
            grid=(width // block,),
            in_specs=[whole(near.shape), whole(far.shape)]
            + [pl.BlockSpec((depth, block), lambda i, place: (0, i))] * len(pieces)
            + [pl.BlockSpec((depth, HEAD), lambda i, place: (0, width // HEAD))] * len(pieces),
            out_specs=[wide] * count + [whole((feats, HEAD))],
            scratch_shapes=[pltpu.VMEM((count * seq, feats), BF16), pltpu.VMEM((feats, block), BF16)],
        ),
        out_shape=[jax.ShapeDtypeStruct((seq, width), F32)]
        + [jax.ShapeDtypeStruct((seq, width), BF16)] * (count - 1)
        + [jax.ShapeDtypeStruct((feats, HEAD), BF16)],
        cost_estimate=LIGHT,
        compiler_params=limits(),
    )(place, near, far, *pieces.values(), *pieces.values())


def grad_kernel(heads, probs_ref, own_ref, *refs):
    recv_refs, (grad_ref, dv_ref) = refs[:-2], refs[-2:]
    total = jnp.zeros(dv_ref.shape, F32)
    for h in range(heads):
        span = slice(h * HEAD, (h + 1) * HEAD)
        grad = own_ref[:, span]
        for ref in recv_refs:
            grad += ref[:, span].astype(F32)
        grad = grad.astype(BF16)
        grad_ref[:, span] = grad
        total += jnp.dot(probs_ref[h], grad, preferred_element_type=F32)
    dv_ref[...] = total.astype(BF16)


def head_gradient(probs, own, recv):
    seq, width = own.shape
    return pl.pallas_call(
        functools.partial(grad_kernel, width // HEAD),
        out_shape=[jax.ShapeDtypeStruct((seq, width), BF16), jax.ShapeDtypeStruct((seq, HEAD), BF16)],
        cost_estimate=LIGHT,
        compiler_params=limits(),
    )(probs, own, *recv)


def score_kernel(scale, heads, q_ref, k_ref, v_ref, ao_ref, grad_ref, dq_ref, dk_ref, dk_sum):
    step = pl.program_id(0)

    @pl.when(step == 0)
    def _():
        dk_sum[...] = jnp.zeros_like(dk_sum)

    keys = k_ref[...]
    vals = v_ref[...]
    seq = keys.shape[0]
    rows = lax.broadcasted_iota(jnp.int32, (seq, seq), 0)
    cols = lax.broadcasted_iota(jnp.int32, (seq, seq), 1)
    dk_here = jnp.zeros(dk_sum.shape, F32)
    for h in range(heads):
        span = slice(h * HEAD, (h + 1) * HEAD)
        q = q_ref[:, span]
        grad = grad_ref[:, span]
        scores = lax.dot_general(q, keys, LAST, preferred_element_type=F32) * scale
        scores = jnp.where(rows >= cols, scores, -jnp.inf)
        exponent = jnp.exp(scores - jnp.max(scores, axis=1, keepdims=True))
        probs = exponent / jnp.sum(exponent, axis=1, keepdims=True)
        prob_grad = lax.dot_general(grad, vals, LAST, preferred_element_type=F32)
        row_dot = jnp.sum(grad.astype(F32) * ao_ref[:, span].astype(F32), axis=1, keepdims=True)
        score_grad = (probs * (prob_grad - row_dot)).astype(BF16)
        dq_ref[:, span] = (jnp.dot(score_grad, keys, preferred_element_type=F32) * scale).astype(BF16)
        dk_here += lax.dot_general(score_grad, q, FIRST, preferred_element_type=F32)
    dk_sum[...] += dk_here

    @pl.when(step == pl.num_programs(0) - 1)
    def _():
        dk_ref[...] = (dk_sum[...] * scale).astype(BF16)


def score_gradients(q, k, v, ao, grad):
    seq, width = q.shape
    heads = 2
    count = width // HEAD
    wide = pl.BlockSpec((seq, heads * HEAD), lambda i: (0, i))
    narrow = whole((seq, HEAD))
    return pl.pallas_call(
        functools.partial(score_kernel, HEAD**-0.5, heads),
        grid=(count // heads,),
        in_specs=[wide, narrow, narrow, wide, wide],
        out_specs=[wide, narrow],
        out_shape=[jax.ShapeDtypeStruct((seq, width), BF16), jax.ShapeDtypeStruct((seq, HEAD), BF16)],
        scratch_shapes=[pltpu.VMEM((seq, HEAD), F32)],
        cost_estimate=LIGHT,
        compiler_params=limits(),
    )(q, k, v, ao, grad)


def input_kernel(n_xl, n_z, cols, place, dv_ref, *refs):
    wv_refs, (keep_ref, give_ref, wv_all) = refs[:-3], refs[-3:]
    c, y, n_y = place[1], place[2], len(wv_refs)
    for k, ref in enumerate(wv_refs):
        from_y = (y + n_y - k) % n_y
        for z in range(n_z):
            for xl in range(n_xl):
                start = (xl * n_z + z) * n_y + from_y
                block = ref[(z * n_xl + xl) * cols : (z * n_xl + xl + 1) * cols].astype(F32)
                wv_all[pl.ds(pl.multiple_of(start * cols, 8), cols)] = block
    wv = wv_all[...].astype(BF16)
    for xh in range(2):
        keep_ref[xh] = lax.dot_general(dv_ref[xh, c], wv, LAST, preferred_element_type=F32)
        give = lax.dot_general(dv_ref[xh, 1 - c], wv, LAST, preferred_element_type=F32)
        give_ref[xh] = give.astype(BF16)


def input_parts(place, dv, wvs, n_xl, n_z, cols):
    rows = dv.shape[2]
    feats = len(wvs) * wvs[0].shape[0]
    shape = (2, rows, feats)
    return pl.pallas_call(
        functools.partial(input_kernel, n_xl, n_z, cols),
        grid_spec=pltpu.PrefetchScalarGridSpec(
            num_scalar_prefetch=1,
            grid=(1,),
            in_specs=[whole(dv.shape)] + [whole(wv.shape) for wv in wvs],
            out_specs=[whole(shape), whole(shape)],
            scratch_shapes=[pltpu.VMEM((feats, HEAD), F32)],
        ),
        out_shape=[jax.ShapeDtypeStruct(shape, F32), jax.ShapeDtypeStruct(shape, BF16)],
        cost_estimate=LIGHT,
        compiler_params=limits(),
    )(place, dv, *wvs)


def value_kernel(cols, place, near_ref, far_ref, *refs):
    dv_refs, (part_ref, rows_ref) = refs[:-2], refs[-2:]
    gather_rows(place[0], place[1], near_ref, far_ref, rows_ref)
    seq = dv_refs[0].shape[0]
    total = jnp.zeros((rows_ref.shape[1], HEAD), F32)
    for k, ref in enumerate(dv_refs):
        total += lax.dot_general(rows_ref[k * seq : (k + 1) * seq], ref[...], FIRST, preferred_element_type=F32)
    for i in range(part_ref.shape[0]):
        part_ref[i] = total[i * cols : (i + 1) * cols].astype(BF16)


def value_parts(place, near, far, dvs, cols):
    feats = near.shape[2]
    shape = (feats // cols, cols, HEAD)
    return pl.pallas_call(
        functools.partial(value_kernel, cols),
        grid_spec=pltpu.PrefetchScalarGridSpec(
            num_scalar_prefetch=1,
            grid=(1,),
            in_specs=[whole(near.shape), whole(far.shape)] + [whole(dv.shape) for dv in dvs],
            out_specs=whole(shape),
            scratch_shapes=[pltpu.VMEM((len(dvs) * dvs[0].shape[0], feats), BF16)],
        ),
        out_shape=jax.ShapeDtypeStruct(shape, BF16),
        cost_estimate=LIGHT,
        compiler_params=limits(),
    )(place, near, far, *dvs)


def for_each(parts):
    both = jnp.broadcast_to(parts[:, None], (parts.shape[0], 2) + parts.shape[1:])
    return both.reshape((parts.shape[0] * 2,) + parts.shape[1:])


def on_device(queries, keys, values, attn_out, layer_in, out_grad, w_out, w_value):
    xl, z, y, xh, c = (lax.axis_index(a) for a in ("xl", "z", "y", "xh", "c"))
    place = jnp.stack([xl, c, y, z]).astype(jnp.int32)
    n_xl, n_z, n_y = SIZES["xl"], SIZES["z"], SIZES["y"]
    n_dp = n_xl * n_z * n_y
    q, k, v, ao, li, og = (a[0] for a in (queries, keys, values, attn_out, layer_in, out_grad))
    seq, width = q.shape
    rows, feats = og.shape
    quarter = feats // n_y
    cols = feats // n_dp

    shard = jnp.concatenate([w_out.T, w_value], axis=1)
    other = shift(shard, "xl", 1)
    plane = jnp.where(xl == 0, jnp.concatenate([shard, other]), jnp.concatenate([other, shard]))
    aos = [ao] + [shift(ao, "y", step) for step in range(1, n_y)]
    pieces = {0: plane}
    for step in range(1, n_z // 2):
        if step == 3:
            pieces[-2], pieces[2], _, _ = lax.optimization_barrier((pieces[-2], pieces[2], aos[1], aos[3]))
        pieces[-step] = shift(pieces[1 - step], "z", 1)
        pieces[step] = shift(pieces[step - 1], "z", -1)
    pieces[-n_z // 2] = shift(pieces[1 - n_z // 2], "z", 1)

    by_y = og.reshape(rows, n_xl, n_z, n_y, cols).transpose(3, 0, 2, 1, 4).reshape(n_y, rows, quarter)
    near = lax.all_to_all(after(for_each(by_y), plane), ("y", "xh"), 0, 0, tiled=True)
    near = after(near, pieces[-1], pieces[1])
    far = shift(near, "c", 1)

    by_xl = li.reshape(rows, n_xl, feats // n_xl).transpose(1, 0, 2)
    li_near = lax.all_to_all(after(for_each(by_xl), near), ("xl", "xh"), 0, 0, tiled=True)
    li_near = after(li_near, pieces[-3], pieces[3])
    li_far = shift(li_near, "c", 1)

    own, *sends, wv = head_parts(place, after(near, aos[2], li_far), far, pieces, seq, width)
    recv = [shift(send, "y", -step - 1) for step, send in enumerate(sends)]
    probs = probabilities(after(q, sends[0]), k)

    part = out_part(place, after(near, sends[0]), far, aos)
    part = lax.all_to_all(part.reshape(n_z, n_xl * cols, width), "z", 0, 0, tiled=True)
    part = jnp.sum(part.astype(F32), axis=0).astype(BF16)
    wv, probs, *recv = lax.optimization_barrier((wv, probs, *recv))
    wvs = [wv] + [shift(wv, "y", step) for step in range(1, n_y)]
    head_grad, value_grad = head_gradient(probs, own, recv)
    dvs = [value_grad, shift(value_grad, "xl", 1)]

    value_part = value_parts(place, li_near, li_far, dvs, cols)

    keep, give = input_parts(place, value_grad.reshape(2, 2, rows, HEAD), wvs, n_xl, n_z, cols)
    keep = keep + shift(after(give, value_part), "c", 1).astype(F32)
    give = lax.dynamic_index_in_dim(keep, 1 - xh, 0, False).astype(BF16)
    keep = lax.dynamic_index_in_dim(keep, xh, 0, False)
    give = shift(give, "xh", 1)
    head_grad = after(head_grad, give)
    input_grad = (keep + give.astype(F32)).astype(BF16)

    value_part = lax.all_to_all(after(value_part, part), ("z", "y"), 0, 0, tiled=True)
    query_grad, key_grad = score_gradients(q, k, v, ao, head_grad)

    part = part.reshape(n_xl, cols, width)
    mine = lax.dynamic_index_in_dim(part, xl, 0, False).astype(F32)
    other = shift(lax.dynamic_index_in_dim(part, 1 - xl, 0, False), "xl", 1)
    out_weight_grad = ((mine + other.astype(F32)) / n_dp).T
    value_weight_grad = jnp.sum(value_part.astype(F32), axis=0) / n_dp

    return (
        query_grad[None],
        key_grad[None],
        value_grad[None],
        input_grad[None],
        out_weight_grad,
        value_weight_grad,
    )


def solution(mesh):
    fine = Mesh(mesh.devices.reshape(tuple(SIZES.values())), tuple(SIZES))
    heads = P(DP, None, TENSOR)
    tokens = P(DP, TENSOR, None)
    return jax.shard_map(
        on_device,
        mesh=fine,
        in_specs=(heads, heads, heads, heads, tokens, tokens, P(TENSOR, DP), P(DP, TENSOR)),
        out_specs=(heads, heads, heads, tokens, P(TENSOR, DP), P(DP, TENSOR)),
        check_vma=False,
    )
```

```python
import functools

import jax
import jax.numpy as jnp
from jax import lax
from jax.experimental import pallas as pl
from jax.experimental.pallas import tpu as pltpu
from jax.sharding import Mesh
from jax.sharding import PartitionSpec as P

HEAD = 128
SIZES = {"xl": 2, "z": 8, "y": 4, "xh": 2, "c": 2}
DP = ("xl", "z", "y")
TENSOR = ("xh", "c")
F32 = jnp.float32
BF16 = jnp.bfloat16


def shift(array, axis, by):
    count = SIZES[axis]
    return lax.ppermute(array, axis, [(i, (i + by) % count) for i in range(count)])


LAST = (((1,), (1,)), ((), ()))
FIRST = (((0,), (0,)), ((), ()))


def after(array, *earlier):
    return lax.optimization_barrier((array,) + earlier)[0]


LIGHT = pl.CostEstimate(flops=1, bytes_accessed=1, transcendentals=0)


def limits():
    return pltpu.CompilerParams(vmem_limit_bytes=16 * 1024 * 1024)


def whole(shape):
    return pl.BlockSpec(shape, lambda *_: (0,) * len(shape))


def probs_kernel(scale, heads, q_ref, k_ref, probs_ref):
    keys = k_ref[...]
    seq = keys.shape[0]
    rows = lax.broadcasted_iota(jnp.int32, (seq, seq), 0)
    cols = lax.broadcasted_iota(jnp.int32, (seq, seq), 1)
    for h in range(heads):
        q = q_ref[:, h * HEAD : (h + 1) * HEAD]
        scores = lax.dot_general(keys, q, LAST, preferred_element_type=F32) * scale
        scores = jnp.where(cols >= rows, scores, -jnp.inf)
        exponent = jnp.exp(scores - jnp.max(scores, axis=0, keepdims=True))
        probs_ref[h] = (exponent / jnp.sum(exponent, axis=0, keepdims=True)).astype(BF16)


def probabilities(q, k):
    seq, width = q.shape
    heads = 2
    count = width // HEAD
    return pl.pallas_call(
        functools.partial(probs_kernel, HEAD**-0.5, heads),
        grid=(count // heads,),
        in_specs=[pl.BlockSpec((seq, heads * HEAD), lambda i: (0, i)), whole((seq, HEAD))],
        out_specs=pl.BlockSpec((heads, seq, seq), lambda i: (i, 0, 0)),
        out_shape=jax.ShapeDtypeStruct((count, seq, seq), BF16),
        cost_estimate=LIGHT,
        compiler_params=limits(),
    )(q, k)


def gather_rows(position, c, near_ref, far_ref, rows_ref):
    count = near_ref.shape[0] // 2
    rows = near_ref.shape[1]
    for k in range(count):
        for xh in range(2):
            index = (position + count - k) % count * 2 + xh
            start = (k * 2 + xh) * 2 * rows
            rows_ref[pl.ds(pl.multiple_of(start + c * rows, rows), rows)] = near_ref[index]
            rows_ref[pl.ds(pl.multiple_of(start + (1 - c) * rows, rows), rows)] = far_ref[index]


def out_kernel(place, near_ref, far_ref, *refs):
    ao_refs, (part_ref, grads_ref) = refs[:-2], refs[-2:]
    step = pl.program_id(0)
    seq = ao_refs[0].shape[0]

    @pl.when(step == 0)
    def _():
        gather_rows(place[2], place[1], near_ref, far_ref, grads_ref)

    chunk = part_ref.shape[0]
    span = pl.ds(pl.multiple_of(step * chunk, chunk), chunk)
    total = jnp.zeros(part_ref.shape, F32)
    for k, ao_ref in enumerate(ao_refs):
        total += lax.dot_general(
            grads_ref[k * seq : (k + 1) * seq, span], ao_ref[...], FIRST, preferred_element_type=F32
        )
    part_ref[...] = total.astype(BF16)


def out_part(place, near, far, aos):
    seq, width = aos[0].shape
    feats = near.shape[2]
    chunk = feats // 5
    return pl.pallas_call(
        out_kernel,
        grid_spec=pltpu.PrefetchScalarGridSpec(
            num_scalar_prefetch=1,
            grid=(feats // chunk,),
            in_specs=[whole(near.shape), whole(far.shape)] + [whole(ao.shape) for ao in aos],
            out_specs=pl.BlockSpec((chunk, width), lambda i, place: (i, 0)),
            scratch_shapes=[pltpu.VMEM((len(aos) * seq, feats), BF16)],
        ),
        out_shape=jax.ShapeDtypeStruct((feats, width), BF16),
        cost_estimate=LIGHT,
        compiler_params=limits(),
    )(place, near, far, *aos)


def head_kernel(offsets, place, near_ref, far_ref, *refs):
    n_z = len(offsets)
    w_refs, wv_refs, refs = refs[:n_z], refs[n_z : 2 * n_z], refs[2 * n_z :]
    own_ref, send_refs, (wv_ref, grads_ref, w_all) = refs[0], refs[1:-3], refs[-3:]
    depth = w_refs[0].shape[0]

    def in_order(pieces, ref):
        for offset, piece in zip(offsets, pieces):
            start = (place[3] + offset + n_z) % n_z * depth
            ref[pl.ds(pl.multiple_of(start, depth), depth)] = piece[...]

    @pl.when(pl.program_id(0) == 0)
    def _():
        gather_rows(place[2], place[1], near_ref, far_ref, grads_ref)
        in_order(wv_refs, wv_ref)

    in_order(w_refs, w_all)
    seq = own_ref.shape[0]
    product = jnp.dot(grads_ref[...], w_all[...], preferred_element_type=F32)
    own_ref[...] = product[:seq]
    for k, ref in enumerate(send_refs):
        ref[...] = product[(k + 1) * seq : (k + 2) * seq].astype(BF16)


def head_parts(place, near, far, pieces, seq, width):
    feats = near.shape[2]
    count = near.shape[0] // 2
    block = 256
    depth = feats // len(pieces)
    wide = pl.BlockSpec((seq, block), lambda i, place: (0, i))
    return pl.pallas_call(
        functools.partial(head_kernel, tuple(pieces)),
        grid_spec=pltpu.PrefetchScalarGridSpec(
            num_scalar_prefetch=1,
            grid=(width // block,),
            in_specs=[whole(near.shape), whole(far.shape)]
            + [pl.BlockSpec((depth, block), lambda i, place: (0, i))] * len(pieces)
            + [pl.BlockSpec((depth, HEAD), lambda i, place: (0, width // HEAD))] * len(pieces),
            out_specs=[wide] * count + [whole((feats, HEAD))],
            scratch_shapes=[pltpu.VMEM((count * seq, feats), BF16), pltpu.VMEM((feats, block), BF16)],
        ),
        out_shape=[jax.ShapeDtypeStruct((seq, width), F32)]
        + [jax.ShapeDtypeStruct((seq, width), BF16)] * (count - 1)
        + [jax.ShapeDtypeStruct((feats, HEAD), BF16)],
        cost_estimate=LIGHT,
        compiler_params=limits(),
    )(place, near, far, *pieces.values(), *pieces.values())


def grad_kernel(heads, probs_ref, own_ref, *refs):
    recv_refs, (grad_ref, dv_ref) = refs[:-2], refs[-2:]
    total = jnp.zeros(dv_ref.shape, F32)
    for h in range(heads):
        span = slice(h * HEAD, (h + 1) * HEAD)
        grad = own_ref[:, span]
        for ref in recv_refs:
            grad += ref[:, span].astype(F32)
        grad = grad.astype(BF16)
        grad_ref[:, span] = grad
        total += jnp.dot(probs_ref[h], grad, preferred_element_type=F32)
    dv_ref[...] = total.astype(BF16)


def head_gradient(probs, own, recv):
    seq, width = own.shape
    return pl.pallas_call(
        functools.partial(grad_kernel, width // HEAD),
        out_shape=[jax.ShapeDtypeStruct((seq, width), BF16), jax.ShapeDtypeStruct((seq, HEAD), BF16)],
        cost_estimate=LIGHT,
        compiler_params=limits(),
    )(probs, own, *recv)


def score_kernel(scale, heads, q_ref, k_ref, v_ref, ao_ref, grad_ref, dq_ref, dk_ref, dk_sum):
    step = pl.program_id(0)

    @pl.when(step == 0)
    def _():
        dk_sum[...] = jnp.zeros_like(dk_sum)

    keys = k_ref[...]
    vals = v_ref[...]
    seq = keys.shape[0]
    rows = lax.broadcasted_iota(jnp.int32, (seq, seq), 0)
    cols = lax.broadcasted_iota(jnp.int32, (seq, seq), 1)
    dk_here = jnp.zeros(dk_sum.shape, F32)
    for h in range(heads):
        span = slice(h * HEAD, (h + 1) * HEAD)
        q = q_ref[:, span]
        grad = grad_ref[:, span]
        scores = lax.dot_general(q, keys, LAST, preferred_element_type=F32) * scale
        scores = jnp.where(rows >= cols, scores, -jnp.inf)
        exponent = jnp.exp(scores - jnp.max(scores, axis=1, keepdims=True))
        probs = exponent / jnp.sum(exponent, axis=1, keepdims=True)
        prob_grad = lax.dot_general(grad, vals, LAST, preferred_element_type=F32)
        row_dot = jnp.sum(grad.astype(F32) * ao_ref[:, span].astype(F32), axis=1, keepdims=True)
        score_grad = (probs * (prob_grad - row_dot)).astype(BF16)
        dq_ref[:, span] = (jnp.dot(score_grad, keys, preferred_element_type=F32) * scale).astype(BF16)
        dk_here += lax.dot_general(score_grad, q, FIRST, preferred_element_type=F32)
    dk_sum[...] += dk_here

    @pl.when(step == pl.num_programs(0) - 1)
    def _():
        dk_ref[...] = (dk_sum[...] * scale).astype(BF16)


def score_gradients(q, k, v, ao, grad):
    seq, width = q.shape
    heads = 2
    count = width // HEAD
    wide = pl.BlockSpec((seq, heads * HEAD), lambda i: (0, i))
    narrow = whole((seq, HEAD))
    return pl.pallas_call(
        functools.partial(score_kernel, HEAD**-0.5, heads),
        grid=(count // heads,),
        in_specs=[wide, narrow, narrow, wide, wide],
        out_specs=[wide, narrow],
        out_shape=[jax.ShapeDtypeStruct((seq, width), BF16), jax.ShapeDtypeStruct((seq, HEAD), BF16)],
        scratch_shapes=[pltpu.VMEM((seq, HEAD), F32)],
        cost_estimate=LIGHT,
        compiler_params=limits(),
    )(q, k, v, ao, grad)


def input_kernel(n_xl, n_z, cols, place, dv_ref, *refs):
    wv_refs, (keep_ref, give_ref, wv_all) = refs[:-3], refs[-3:]
    c, y, n_y = place[1], place[2], len(wv_refs)
    for k, ref in enumerate(wv_refs):
        from_y = (y + n_y - k) % n_y
        for z in range(n_z):
            for xl in range(n_xl):
                start = (xl * n_z + z) * n_y + from_y
                block = ref[(z * n_xl + xl) * cols : (z * n_xl + xl + 1) * cols].astype(F32)
                wv_all[pl.ds(pl.multiple_of(start * cols, 8), cols)] = block
    wv = wv_all[...].astype(BF16)
    for xh in range(2):
        keep_ref[xh] = lax.dot_general(dv_ref[xh, c], wv, LAST, preferred_element_type=F32)
        give = lax.dot_general(dv_ref[xh, 1 - c], wv, LAST, preferred_element_type=F32)
        give_ref[xh] = give.astype(BF16)


def input_parts(place, dv, wvs, n_xl, n_z, cols):
    rows = dv.shape[2]
    feats = len(wvs) * wvs[0].shape[0]
    shape = (2, rows, feats)
    return pl.pallas_call(
        functools.partial(input_kernel, n_xl, n_z, cols),
        grid_spec=pltpu.PrefetchScalarGridSpec(
            num_scalar_prefetch=1,
            grid=(1,),
            in_specs=[whole(dv.shape)] + [whole(wv.shape) for wv in wvs],
            out_specs=[whole(shape), whole(shape)],
            scratch_shapes=[pltpu.VMEM((feats, HEAD), F32)],
        ),
        out_shape=[jax.ShapeDtypeStruct(shape, F32), jax.ShapeDtypeStruct(shape, BF16)],
        cost_estimate=LIGHT,
        compiler_params=limits(),
    )(place, dv, *wvs)


def value_kernel(cols, place, near_ref, far_ref, *refs):
    dv_refs, part_refs, rows_ref = refs[:2], refs[2:-1], refs[-1]
    y = place[2]
    gather_rows(place[0], place[1], near_ref, far_ref, rows_ref)
    seq = dv_refs[0].shape[0]
    total = jnp.zeros((rows_ref.shape[1], HEAD), F32)
    for k, ref in enumerate(dv_refs):
        total += lax.dot_general(rows_ref[k * seq : (k + 1) * seq], ref[...], FIRST, preferred_element_type=F32)
    n_y = len(part_refs)
    for to_y in range(n_y):
        for k, ref in enumerate(part_refs):

            @pl.when((y + k) % n_y == to_y)
            def _():
                for z in range(ref.shape[0]):
                    start = (z * n_y + to_y) * cols
                    ref[z] = total[start : start + cols].astype(BF16)


def value_parts(place, near, far, dvs, n_y, cols):
    half = near.shape[2]
    shape = (half // cols // n_y, cols, HEAD)
    return pl.pallas_call(
        functools.partial(value_kernel, cols),
        grid_spec=pltpu.PrefetchScalarGridSpec(
            num_scalar_prefetch=1,
            grid=(1,),
            in_specs=[whole(array.shape) for array in [near, far] + dvs],
            out_specs=[whole(shape)] * n_y,
            scratch_shapes=[pltpu.VMEM((len(dvs) * dvs[0].shape[0], half), BF16)],
        ),
        out_shape=[jax.ShapeDtypeStruct(shape, BF16)] * n_y,
        cost_estimate=LIGHT,
        compiler_params=limits(),
    )(place, near, far, *dvs)


def for_each(parts):
    both = jnp.broadcast_to(parts[:, None], (parts.shape[0], 2) + parts.shape[1:])
    return both.reshape((parts.shape[0] * 2,) + parts.shape[1:])


def on_device(queries, keys, values, attn_out, layer_in, out_grad, w_out, w_value):
    xl, z, y, xh, c = (lax.axis_index(a) for a in ("xl", "z", "y", "xh", "c"))
    place = jnp.stack([xl, c, y, z, xh]).astype(jnp.int32)
    n_xl, n_z, n_y = SIZES["xl"], SIZES["z"], SIZES["y"]
    n_dp = n_xl * n_z * n_y
    q, k, v, ao, li, og = (a[0] for a in (queries, keys, values, attn_out, layer_in, out_grad))
    seq, width = q.shape
    rows, feats = og.shape
    quarter = feats // n_y
    cols = feats // n_dp

    shard = jnp.concatenate([w_out.T, w_value], axis=1)
    other = shift(shard, "xl", 1)
    plane = jnp.where(xl == 0, jnp.concatenate([shard, other]), jnp.concatenate([other, shard]))
    aos = [ao] + [shift(ao, "y", step) for step in range(1, n_y)]
    pieces = {0: plane}
    for step in range(1, n_z // 2):
        if step == 3:
            pieces[-2], pieces[2], _, _ = lax.optimization_barrier((pieces[-2], pieces[2], aos[1], aos[3]))
        pieces[-step] = shift(pieces[1 - step], "z", 1)
        pieces[step] = shift(pieces[step - 1], "z", -1)
    pieces[-n_z // 2] = shift(after(pieces[1 - n_z // 2], aos[2]), "z", 1)

    by_y = og.reshape(rows, n_xl, n_z, n_y, cols).transpose(3, 0, 2, 1, 4).reshape(n_y, rows, quarter)
    near = lax.all_to_all(after(for_each(by_y), pieces[1], pieces[-1]), ("y", "xh"), 0, 0, tiled=True)
    near = after(near, pieces[-2], pieces[2])
    far = shift(near, "c", 1)

    by_xl = li.reshape(rows, n_xl, feats // n_xl).transpose(1, 0, 2)
    li_near = lax.all_to_all(after(for_each(by_xl), near), ("xl", "xh"), 0, 0, tiled=True)

    own, *sends, wv = head_parts(place, after(near, li_near), far, pieces, seq, width)
    recv = [shift(send, "y", -step - 1) for step, send in enumerate(sends)]
    probs = probabilities(after(q, sends[0]), k)

    part = out_part(place, after(near, sends[0]), far, aos)
    part = part.reshape(n_z, n_xl * cols, width)
    parts = lax.all_to_all(part, "z", 0, 0, tiled=True)

    li_far = shift(after(li_near, sends[0]), "c", 1)
    probs, recv, li_far, part = lax.optimization_barrier((probs, recv, li_far, part))
    head_grad, value_grad = head_gradient(probs, own, recv)
    wv = after(wv, value_grad)
    wvs = [wv] + [shift(wv, "y", step) for step in range(1, n_y)]
    dvs = [value_grad, shift(value_grad, "xl", 1)]

    value_part = value_parts(place, li_near, li_far, dvs, n_y, cols)
    value_part = [value_part[0]] + [shift(value_part[step], "y", step) for step in range(1, n_y)]
    value_part = sum(piece.astype(F32) for piece in value_part).astype(BF16)

    keep, give = input_parts(place, value_grad.reshape(2, 2, rows, HEAD), wvs, n_xl, n_z, cols)
    keep = keep + shift(after(give, value_part), "c", 1).astype(F32)
    part = jnp.sum(parts.astype(F32), axis=0).astype(BF16)
    give = after(lax.dynamic_index_in_dim(keep, 1 - xh, 0, False).astype(BF16), part)
    keep = lax.dynamic_index_in_dim(keep, xh, 0, False)
    give = shift(give, "xh", 1)
    head_grad = after(head_grad, part)
    input_grad = (keep + give.astype(F32)).astype(BF16)

    value_part = lax.all_to_all(after(value_part, part), "z", 0, 0, tiled=True)
    query_grad, key_grad = score_gradients(q, k, v, ao, head_grad)

    part = part.reshape(n_xl, cols, width)
    mine = lax.dynamic_index_in_dim(part, xl, 0, False).astype(F32)
    other = shift(lax.dynamic_index_in_dim(part, 1 - xl, 0, False), "xl", 1)
    out_weight_grad = ((mine + other.astype(F32)) / n_dp).T
    value_weight_grad = jnp.sum(value_part.astype(F32), axis=0) / n_dp

    return (
        query_grad[None],
        key_grad[None],
        value_grad[None],
        input_grad[None],
        out_weight_grad,
        value_weight_grad,
    )


def solution(mesh):
    fine = Mesh(mesh.devices.reshape(tuple(SIZES.values())), tuple(SIZES))
    heads = P(DP, None, TENSOR)
    tokens = P(DP, TENSOR, None)
    return jax.shard_map(
        on_device,
        mesh=fine,
        in_specs=(heads, heads, heads, heads, tokens, tokens, P(TENSOR, DP), P(DP, TENSOR)),
        out_specs=(heads, heads, heads, tokens, P(TENSOR, DP), P(DP, TENSOR)),
        check_vma=False,
    )
```

```python
import functools

import jax
import jax.numpy as jnp
from jax import lax
from jax.experimental import pallas as pl
from jax.experimental.pallas import tpu as pltpu
from jax.sharding import Mesh
from jax.sharding import PartitionSpec as P

HEAD = 128
SIZES = {"xl": 2, "z": 8, "y": 4, "xh": 2, "c": 2}
DP = ("xl", "z", "y")
TENSOR = ("xh", "c")
F32 = jnp.float32
BF16 = jnp.bfloat16


def shift(array, axis, by):
    count = SIZES[axis]
    return lax.ppermute(array, axis, [(i, (i + by) % count) for i in range(count)])


LAST = (((1,), (1,)), ((), ()))
FIRST = (((0,), (0,)), ((), ()))


def after(array, *earlier):
    return lax.optimization_barrier((array,) + earlier)[0]


LIGHT = pl.CostEstimate(flops=1, bytes_accessed=1, transcendentals=0)


def limits():
    return pltpu.CompilerParams(vmem_limit_bytes=16 * 1024 * 1024)


def whole(shape):
    return pl.BlockSpec(shape, lambda *_: (0,) * len(shape))


def probs_kernel(scale, heads, q_ref, k_ref, probs_ref):
    keys = k_ref[...]
    seq = keys.shape[0]
    rows = lax.broadcasted_iota(jnp.int32, (seq, seq), 0)
    cols = lax.broadcasted_iota(jnp.int32, (seq, seq), 1)
    for h in range(heads):
        q = q_ref[:, h * HEAD : (h + 1) * HEAD]
        scores = lax.dot_general(keys, q, LAST, preferred_element_type=F32) * scale
        scores = jnp.where(cols >= rows, scores, -jnp.inf)
        exponent = jnp.exp(scores - jnp.max(scores, axis=0, keepdims=True))
        probs_ref[h] = (exponent / jnp.sum(exponent, axis=0, keepdims=True)).astype(BF16)


def probabilities(q, k):
    seq, width = q.shape
    heads = 2
    count = width // HEAD
    return pl.pallas_call(
        functools.partial(probs_kernel, HEAD**-0.5, heads),
        grid=(count // heads,),
        in_specs=[pl.BlockSpec((seq, heads * HEAD), lambda i: (0, i)), whole((seq, HEAD))],
        out_specs=pl.BlockSpec((heads, seq, seq), lambda i: (i, 0, 0)),
        out_shape=jax.ShapeDtypeStruct((count, seq, seq), BF16),
        cost_estimate=LIGHT,
        compiler_params=limits(),
    )(q, k)


def gather_rows(position, c, near_ref, far_ref, rows_ref):
    count = near_ref.shape[0] // 2
    rows = near_ref.shape[1]
    for k in range(count):
        for xh in range(2):
            index = (position + count - k) % count * 2 + xh
            start = (k * 2 + xh) * 2 * rows
            rows_ref[pl.ds(pl.multiple_of(start + c * rows, rows), rows)] = near_ref[index]
            rows_ref[pl.ds(pl.multiple_of(start + (1 - c) * rows, rows), rows)] = far_ref[index]


def out_kernel(place, near_ref, far_ref, *refs):
    ao_refs, (part_ref, grads_ref) = refs[:-2], refs[-2:]
    step = pl.program_id(0)
    seq = ao_refs[0].shape[0]

    @pl.when(step == 0)
    def _():
        gather_rows(place[2], place[1], near_ref, far_ref, grads_ref)

    chunk = part_ref.shape[0]
    span = pl.ds(pl.multiple_of(step * chunk, chunk), chunk)
    total = jnp.zeros(part_ref.shape, F32)
    for k, ao_ref in enumerate(ao_refs):
        total += lax.dot_general(
            grads_ref[k * seq : (k + 1) * seq, span], ao_ref[...], FIRST, preferred_element_type=F32
        )
    part_ref[...] = total.astype(BF16)


def out_part(place, near, far, aos):
    seq, width = aos[0].shape
    feats = near.shape[2]
    chunk = feats // 5
    return pl.pallas_call(
        out_kernel,
        grid_spec=pltpu.PrefetchScalarGridSpec(
            num_scalar_prefetch=1,
            grid=(feats // chunk,),
            in_specs=[whole(near.shape), whole(far.shape)] + [whole(ao.shape) for ao in aos],
            out_specs=pl.BlockSpec((chunk, width), lambda i, place: (i, 0)),
            scratch_shapes=[pltpu.VMEM((len(aos) * seq, feats), BF16)],
        ),
        out_shape=jax.ShapeDtypeStruct((feats, width), BF16),
        cost_estimate=LIGHT,
        compiler_params=limits(),
    )(place, near, far, *aos)


def head_kernel(offsets, place, near_ref, far_ref, *refs):
    n_z = len(offsets)
    w_refs, wv_refs, refs = refs[:n_z], refs[n_z : 2 * n_z], refs[2 * n_z :]
    own_ref, send_refs, (wv_ref, grads_ref, w_all) = refs[0], refs[1:-3], refs[-3:]
    depth = w_refs[0].shape[0]

    def in_order(pieces, ref):
        for offset, piece in zip(offsets, pieces):
            start = (place[3] + offset + n_z) % n_z * depth
            ref[pl.ds(pl.multiple_of(start, depth), depth)] = piece[...]

    @pl.when(pl.program_id(0) == 0)
    def _():
        gather_rows(place[2], place[1], near_ref, far_ref, grads_ref)
        in_order(wv_refs, wv_ref)

    in_order(w_refs, w_all)
    seq = own_ref.shape[0]
    product = jnp.dot(grads_ref[...], w_all[...], preferred_element_type=F32)
    own_ref[...] = product[:seq]
    for k, ref in enumerate(send_refs):
        ref[...] = product[(k + 1) * seq : (k + 2) * seq].astype(BF16)


def head_parts(place, near, far, pieces, seq, width):
    feats = near.shape[2]
    count = near.shape[0] // 2
    block = 256
    depth = feats // len(pieces)
    wide = pl.BlockSpec((seq, block), lambda i, place: (0, i))
    return pl.pallas_call(
        functools.partial(head_kernel, tuple(pieces)),
        grid_spec=pltpu.PrefetchScalarGridSpec(
            num_scalar_prefetch=1,
            grid=(width // block,),
            in_specs=[whole(near.shape), whole(far.shape)]
            + [pl.BlockSpec((depth, block), lambda i, place: (0, i))] * len(pieces)
            + [pl.BlockSpec((depth, HEAD), lambda i, place: (0, width // HEAD))] * len(pieces),
            out_specs=[wide] * count + [whole((feats, HEAD))],
            scratch_shapes=[pltpu.VMEM((count * seq, feats), BF16), pltpu.VMEM((feats, block), BF16)],
        ),
        out_shape=[jax.ShapeDtypeStruct((seq, width), F32)]
        + [jax.ShapeDtypeStruct((seq, width), BF16)] * (count - 1)
        + [jax.ShapeDtypeStruct((feats, HEAD), BF16)],
        cost_estimate=LIGHT,
        compiler_params=limits(),
    )(place, near, far, *pieces.values(), *pieces.values())


def grad_kernel(heads, probs_ref, own_ref, *refs):
    recv_refs, (grad_ref, dv_ref) = refs[:-2], refs[-2:]
    total = jnp.zeros(dv_ref.shape, F32)
    for h in range(heads):
        span = slice(h * HEAD, (h + 1) * HEAD)
        grad = own_ref[:, span]
        for ref in recv_refs:
            grad += ref[:, span].astype(F32)
        grad = grad.astype(BF16)
        grad_ref[:, span] = grad
        total += jnp.dot(probs_ref[h], grad, preferred_element_type=F32)
    dv_ref[...] = total.astype(BF16)


def head_gradient(probs, own, recv):
    seq, width = own.shape
    return pl.pallas_call(
        functools.partial(grad_kernel, width // HEAD),
        out_shape=[jax.ShapeDtypeStruct((seq, width), BF16), jax.ShapeDtypeStruct((seq, HEAD), BF16)],
        cost_estimate=LIGHT,
        compiler_params=limits(),
    )(probs, own, *recv)


def score_kernel(scale, heads, q_ref, k_ref, v_ref, ao_ref, grad_ref, dq_ref, dk_ref, dk_sum):
    step = pl.program_id(0)

    @pl.when(step == 0)
    def _():
        dk_sum[...] = jnp.zeros_like(dk_sum)

    keys = k_ref[...]
    vals = v_ref[...]
    seq = keys.shape[0]
    rows = lax.broadcasted_iota(jnp.int32, (seq, seq), 0)
    cols = lax.broadcasted_iota(jnp.int32, (seq, seq), 1)
    dk_here = jnp.zeros(dk_sum.shape, F32)
    for h in range(heads):
        span = slice(h * HEAD, (h + 1) * HEAD)
        q = q_ref[:, span]
        grad = grad_ref[:, span]
        scores = lax.dot_general(q, keys, LAST, preferred_element_type=F32) * scale
        scores = jnp.where(rows >= cols, scores, -jnp.inf)
        exponent = jnp.exp(scores - jnp.max(scores, axis=1, keepdims=True))
        probs = exponent / jnp.sum(exponent, axis=1, keepdims=True)
        prob_grad = lax.dot_general(grad, vals, LAST, preferred_element_type=F32)
        row_dot = jnp.sum(grad.astype(F32) * ao_ref[:, span].astype(F32), axis=1, keepdims=True)
        score_grad = (probs * (prob_grad - row_dot)).astype(BF16)
        dq_ref[:, span] = (jnp.dot(score_grad, keys, preferred_element_type=F32) * scale).astype(BF16)
        dk_here += lax.dot_general(score_grad, q, FIRST, preferred_element_type=F32)
    dk_sum[...] += dk_here

    @pl.when(step == pl.num_programs(0) - 1)
    def _():
        dk_ref[...] = (dk_sum[...] * scale).astype(BF16)


def score_gradients(q, k, v, ao, grad):
    seq, width = q.shape
    heads = 2
    count = width // HEAD
    wide = pl.BlockSpec((seq, heads * HEAD), lambda i: (0, i))
    narrow = whole((seq, HEAD))
    return pl.pallas_call(
        functools.partial(score_kernel, HEAD**-0.5, heads),
        grid=(count // heads,),
        in_specs=[wide, narrow, narrow, wide, wide],
        out_specs=[wide, narrow],
        out_shape=[jax.ShapeDtypeStruct((seq, width), BF16), jax.ShapeDtypeStruct((seq, HEAD), BF16)],
        scratch_shapes=[pltpu.VMEM((seq, HEAD), F32)],
        cost_estimate=LIGHT,
        compiler_params=limits(),
    )(q, k, v, ao, grad)


def input_kernel(n_xl, n_z, cols, place, dv_ref, *refs):
    wv_refs, (keep_ref, give_ref, wv_all) = refs[:-3], refs[-3:]
    c, y, n_y = place[1], place[2], len(wv_refs)
    for k, ref in enumerate(wv_refs):
        from_y = (y + n_y - k) % n_y
        for z in range(n_z):
            for xl in range(n_xl):
                start = (xl * n_z + z) * n_y + from_y
                block = ref[(z * n_xl + xl) * cols : (z * n_xl + xl + 1) * cols].astype(F32)
                wv_all[pl.ds(pl.multiple_of(start * cols, 8), cols)] = block
    wv = wv_all[...].astype(BF16)
    for xh in range(2):
        keep_ref[xh] = lax.dot_general(dv_ref[xh, c], wv, LAST, preferred_element_type=F32)
        give = lax.dot_general(dv_ref[xh, 1 - c], wv, LAST, preferred_element_type=F32)
        give_ref[xh] = give.astype(BF16)


def input_parts(place, dv, wvs, n_xl, n_z, cols):
    rows = dv.shape[2]
    feats = len(wvs) * wvs[0].shape[0]
    shape = (2, rows, feats)
    return pl.pallas_call(
        functools.partial(input_kernel, n_xl, n_z, cols),
        grid_spec=pltpu.PrefetchScalarGridSpec(
            num_scalar_prefetch=1,
            grid=(1,),
            in_specs=[whole(dv.shape)] + [whole(wv.shape) for wv in wvs],
            out_specs=[whole(shape), whole(shape)],
            scratch_shapes=[pltpu.VMEM((feats, HEAD), F32)],
        ),
        out_shape=[jax.ShapeDtypeStruct(shape, F32), jax.ShapeDtypeStruct(shape, BF16)],
        cost_estimate=LIGHT,
        compiler_params=limits(),
    )(place, dv, *wvs)


def value_kernel(cols, place, near_ref, far_ref, *refs):
    dv_refs, (part_ref, rows_ref) = refs[:-2], refs[-2:]
    gather_rows(place[0], place[1], near_ref, far_ref, rows_ref)
    seq = dv_refs[0].shape[0]
    total = jnp.zeros((rows_ref.shape[1], HEAD), F32)
    for k, ref in enumerate(dv_refs):
        total += lax.dot_general(rows_ref[k * seq : (k + 1) * seq], ref[...], FIRST, preferred_element_type=F32)
    for i in range(part_ref.shape[0]):
        part_ref[i] = total[i * cols : (i + 1) * cols].astype(BF16)


def value_parts(place, near, far, dvs, cols):
    feats = near.shape[2]
    shape = (feats // cols, cols, HEAD)
    return pl.pallas_call(
        functools.partial(value_kernel, cols),
        grid_spec=pltpu.PrefetchScalarGridSpec(
            num_scalar_prefetch=1,
            grid=(1,),
            in_specs=[whole(near.shape), whole(far.shape)] + [whole(dv.shape) for dv in dvs],
            out_specs=whole(shape),
            scratch_shapes=[pltpu.VMEM((len(dvs) * dvs[0].shape[0], feats), BF16)],
        ),
        out_shape=jax.ShapeDtypeStruct(shape, BF16),
        cost_estimate=LIGHT,
        compiler_params=limits(),
    )(place, near, far, *dvs)


def for_each(parts):
    both = jnp.broadcast_to(parts[:, None], (parts.shape[0], 2) + parts.shape[1:])
    return both.reshape((parts.shape[0] * 2,) + parts.shape[1:])


def on_device(queries, keys, values, attn_out, layer_in, out_grad, w_out, w_value):
    xl, z, y, xh, c = (lax.axis_index(a) for a in ("xl", "z", "y", "xh", "c"))
    place = jnp.stack([xl, c, y, z]).astype(jnp.int32)
    n_xl, n_z, n_y = SIZES["xl"], SIZES["z"], SIZES["y"]
    n_dp = n_xl * n_z * n_y
    q, k, v, ao, li, og = (a[0] for a in (queries, keys, values, attn_out, layer_in, out_grad))
    seq, width = q.shape
    rows, feats = og.shape
    quarter = feats // n_y
    cols = feats // n_dp

    shard = jnp.concatenate([w_out.T, w_value], axis=1)
    other = shift(shard, "xl", 1)
    plane = jnp.where(xl == 0, jnp.concatenate([shard, other]), jnp.concatenate([other, shard]))
    aos = [ao] + [shift(ao, "y", step) for step in range(1, n_y)]
    pieces = {0: plane}
    for step in range(1, n_z // 2):
        if step == 3:
            pieces[-2], pieces[2], _, _ = lax.optimization_barrier((pieces[-2], pieces[2], aos[1], aos[3]))
        pieces[-step] = shift(pieces[1 - step], "z", 1)
        pieces[step] = shift(pieces[step - 1], "z", -1)
    pieces[-n_z // 2] = shift(after(pieces[1 - n_z // 2], aos[2]), "z", 1)

    by_y = og.reshape(rows, n_xl, n_z, n_y, cols).transpose(3, 0, 2, 1, 4).reshape(n_y, rows, quarter)
    near = lax.all_to_all(after(for_each(by_y), plane), ("y", "xh"), 0, 0, tiled=True)
    near = after(near, pieces[-1], pieces[1])
    far = shift(near, "c", 1)

    by_xl = li.reshape(rows, n_xl, feats // n_xl).transpose(1, 0, 2)
    li_near = lax.all_to_all(after(for_each(by_xl), near), ("xl", "xh"), 0, 0, tiled=True)
    li_near = after(li_near, pieces[-3], pieces[3])
    li_far = shift(li_near, "c", 1)

    own, *sends, wv = head_parts(place, after(near, li_far), far, pieces, seq, width)
    recv = [shift(send, "y", -step - 1) for step, send in enumerate(sends)]
    probs = probabilities(after(q, sends[0]), k)

    part = out_part(place, after(near, sends[0]), far, aos)
    part = lax.all_to_all(part.reshape(n_z, n_xl * cols, width), "z", 0, 0, tiled=True)
    part = jnp.sum(part.astype(F32), axis=0).astype(BF16)
    wv, probs, *recv = lax.optimization_barrier((wv, probs, *recv))
    wvs = [wv] + [shift(wv, "y", step) for step in range(1, n_y)]
    head_grad, value_grad = head_gradient(probs, own, recv)
    dvs = [value_grad, shift(value_grad, "xl", 1)]

    value_part = value_parts(place, li_near, li_far, dvs, cols)

    keep, give = input_parts(place, value_grad.reshape(2, 2, rows, HEAD), wvs, n_xl, n_z, cols)
    keep = keep + shift(after(give, value_part), "c", 1).astype(F32)
    give = lax.dynamic_index_in_dim(keep, 1 - xh, 0, False).astype(BF16)
    keep = lax.dynamic_index_in_dim(keep, xh, 0, False)
    give = shift(give, "xh", 1)
    head_grad = after(head_grad, give)
    input_grad = (keep + give.astype(F32)).astype(BF16)

    value_part = lax.all_to_all(after(value_part, part), ("z", "y"), 0, 0, tiled=True)
    query_grad, key_grad = score_gradients(q, k, v, ao, head_grad)

    part = part.reshape(n_xl, cols, width)
    mine = lax.dynamic_index_in_dim(part, xl, 0, False).astype(F32)
    other = shift(lax.dynamic_index_in_dim(part, 1 - xl, 0, False), "xl", 1)
    out_weight_grad = ((mine + other.astype(F32)) / n_dp).T
    value_weight_grad = jnp.sum(value_part.astype(F32), axis=0) / n_dp

    return (
        query_grad[None],
        key_grad[None],
        value_grad[None],
        input_grad[None],
        out_weight_grad,
        value_weight_grad,
    )


def solution(mesh):
    fine = Mesh(mesh.devices.reshape(tuple(SIZES.values())), tuple(SIZES))
    heads = P(DP, None, TENSOR)
    tokens = P(DP, TENSOR, None)
    return jax.shard_map(
        on_device,
        mesh=fine,
        in_specs=(heads, heads, heads, heads, tokens, tokens, P(TENSOR, DP), P(DP, TENSOR)),
        out_specs=(heads, heads, heads, tokens, P(TENSOR, DP), P(DP, TENSOR)),
        check_vma=False,
    )
```

```python
import functools

import jax
import jax.numpy as jnp
from jax import lax
from jax.experimental import pallas as pl
from jax.experimental.pallas import tpu as pltpu
from jax.sharding import Mesh
from jax.sharding import PartitionSpec as P

HEAD = 128
SIZES = {"xl": 2, "z": 8, "y": 4, "xh": 2, "c": 2}
DP = ("xl", "z", "y")
TENSOR = ("xh", "c")
F32 = jnp.float32
BF16 = jnp.bfloat16


def shift(array, axis, by):
    count = SIZES[axis]
    return lax.ppermute(array, axis, [(i, (i + by) % count) for i in range(count)])


LAST = (((1,), (1,)), ((), ()))
FIRST = (((0,), (0,)), ((), ()))


def after(array, *earlier):
    return lax.optimization_barrier((array,) + earlier)[0]


LIGHT = pl.CostEstimate(flops=1, bytes_accessed=1, transcendentals=0)
SHORT = pl.CostEstimate(flops=4 * 10**9, bytes_accessed=10**7, transcendentals=0)


def limits():
    return pltpu.CompilerParams(vmem_limit_bytes=16 * 1024 * 1024)


def whole(shape):
    return pl.BlockSpec(shape, lambda *_: (0,) * len(shape))


def probs_kernel(scale, heads, q_ref, k_ref, probs_ref):
    keys = k_ref[...]
    seq = keys.shape[0]
    rows = lax.broadcasted_iota(jnp.int32, (seq, seq), 0)
    cols = lax.broadcasted_iota(jnp.int32, (seq, seq), 1)
    for h in range(heads):
        q = q_ref[:, h * HEAD : (h + 1) * HEAD]
        scores = lax.dot_general(keys, q, LAST, preferred_element_type=F32) * scale
        scores = jnp.where(cols >= rows, scores, -jnp.inf)
        exponent = jnp.exp(scores - jnp.max(scores, axis=0, keepdims=True))
        probs_ref[h] = (exponent / jnp.sum(exponent, axis=0, keepdims=True)).astype(BF16)


def probabilities(q, k):
    seq, width = q.shape
    heads = 2
    count = width // HEAD
    return pl.pallas_call(
        functools.partial(probs_kernel, HEAD**-0.5, heads),
        grid=(count // heads,),
        in_specs=[pl.BlockSpec((seq, heads * HEAD), lambda i: (0, i)), whole((seq, HEAD))],
        out_specs=pl.BlockSpec((heads, seq, seq), lambda i: (i, 0, 0)),
        out_shape=jax.ShapeDtypeStruct((count, seq, seq), BF16),
        cost_estimate=LIGHT,
        compiler_params=limits(),
    )(q, k)


def gather_rows(position, c, near_ref, far_ref, rows_ref):
    count = near_ref.shape[0] // 2
    rows = near_ref.shape[1]
    for k in range(count):
        for xh in range(2):
            index = (position + count - k) % count * 2 + xh
            start = (k * 2 + xh) * 2 * rows
            rows_ref[pl.ds(pl.multiple_of(start + c * rows, rows), rows)] = near_ref[index]
            rows_ref[pl.ds(pl.multiple_of(start + (1 - c) * rows, rows), rows)] = far_ref[index]


def out_kernel(place, near_ref, far_ref, *refs):
    ao_refs, (part_ref, grads_ref) = refs[:-2], refs[-2:]
    step = pl.program_id(0)
    seq = ao_refs[0].shape[0]

    @pl.when(step == 0)
    def _():
        gather_rows(place[2], place[1], near_ref, far_ref, grads_ref)

    chunk = part_ref.shape[0]
    span = pl.ds(pl.multiple_of(step * chunk, chunk), chunk)
    total = jnp.zeros(part_ref.shape, F32)
    for k, ao_ref in enumerate(ao_refs):
        total += lax.dot_general(
            grads_ref[k * seq : (k + 1) * seq, span], ao_ref[...], FIRST, preferred_element_type=F32
        )
    part_ref[...] = total.astype(BF16)


def out_part(place, near, far, aos):
    seq, width = aos[0].shape
    feats = near.shape[2]
    chunk = feats // 5
    return pl.pallas_call(
        out_kernel,
        grid_spec=pltpu.PrefetchScalarGridSpec(
            num_scalar_prefetch=1,
            grid=(feats // chunk,),
            in_specs=[whole(near.shape), whole(far.shape)] + [whole(ao.shape) for ao in aos],
            out_specs=pl.BlockSpec((chunk, width), lambda i, place: (i, 0)),
            scratch_shapes=[pltpu.VMEM((len(aos) * seq, feats), BF16)],
        ),
        out_shape=jax.ShapeDtypeStruct((feats, width), BF16),
        cost_estimate=LIGHT,
        compiler_params=limits(),
    )(place, near, far, *aos)


def head_kernel(offsets, place, near_ref, far_ref, *refs):
    n_z = len(offsets)
    w_refs, wv_refs, refs = refs[:n_z], refs[n_z : 2 * n_z], refs[2 * n_z :]
    own_ref, send_refs, (wv_ref, grads_ref, w_all) = refs[0], refs[1:-3], refs[-3:]
    depth = w_refs[0].shape[0]

    def in_order(pieces, ref):
        for offset, piece in zip(offsets, pieces):
            start = (place[3] + offset + n_z) % n_z * depth
            ref[pl.ds(pl.multiple_of(start, depth), depth)] = piece[...]

    @pl.when(pl.program_id(0) == 0)
    def _():
        gather_rows(place[2], place[1], near_ref, far_ref, grads_ref)
        in_order(wv_refs, wv_ref)

    in_order(w_refs, w_all)
    seq = own_ref.shape[0]
    product = jnp.dot(grads_ref[...], w_all[...], preferred_element_type=F32)
    own_ref[...] = product[:seq]
    for k, ref in enumerate(send_refs):
        ref[...] = product[(k + 1) * seq : (k + 2) * seq].astype(BF16)


def head_parts(place, near, far, pieces, seq, width):
    feats = near.shape[2]
    count = near.shape[0] // 2
    block = 256
    depth = feats // len(pieces)
    wide = pl.BlockSpec((seq, block), lambda i, place: (0, i))
    return pl.pallas_call(
        functools.partial(head_kernel, tuple(pieces)),
        grid_spec=pltpu.PrefetchScalarGridSpec(
            num_scalar_prefetch=1,
            grid=(width // block,),
            in_specs=[whole(near.shape), whole(far.shape)]
            + [pl.BlockSpec((depth, block), lambda i, place: (0, i))] * len(pieces)
            + [pl.BlockSpec((depth, HEAD), lambda i, place: (0, width // HEAD))] * len(pieces),
            out_specs=[wide] * count + [whole((feats, HEAD))],
            scratch_shapes=[pltpu.VMEM((count * seq, feats), BF16), pltpu.VMEM((feats, block), BF16)],
        ),
        out_shape=[jax.ShapeDtypeStruct((seq, width), F32)]
        + [jax.ShapeDtypeStruct((seq, width), BF16)] * (count - 1)
        + [jax.ShapeDtypeStruct((feats, HEAD), BF16)],
        cost_estimate=LIGHT,
        compiler_params=limits(),
    )(place, near, far, *pieces.values(), *pieces.values())


def grad_kernel(heads, probs_ref, own_ref, *refs):
    recv_refs, (grad_ref, dv_ref) = refs[:-2], refs[-2:]
    total = jnp.zeros(dv_ref.shape, F32)
    for h in range(heads):
        span = slice(h * HEAD, (h + 1) * HEAD)
        grad = own_ref[:, span]
        for ref in recv_refs:
            grad += ref[:, span].astype(F32)
        grad = grad.astype(BF16)
        grad_ref[:, span] = grad
        total += jnp.dot(probs_ref[h], grad, preferred_element_type=F32)
    dv_ref[...] = total.astype(BF16)


def head_gradient(probs, own, recv):
    seq, width = own.shape
    return pl.pallas_call(
        functools.partial(grad_kernel, width // HEAD),
        out_shape=[jax.ShapeDtypeStruct((seq, width), BF16), jax.ShapeDtypeStruct((seq, HEAD), BF16)],
        cost_estimate=SHORT,
        compiler_params=limits(),
    )(probs, own, *recv)


def score_kernel(scale, heads, q_ref, k_ref, v_ref, ao_ref, grad_ref, dq_ref, dk_ref, dk_sum):
    step = pl.program_id(0)

    @pl.when(step == 0)
    def _():
        dk_sum[...] = jnp.zeros_like(dk_sum)

    keys = k_ref[...]
    vals = v_ref[...]
    seq = keys.shape[0]
    rows = lax.broadcasted_iota(jnp.int32, (seq, seq), 0)
    cols = lax.broadcasted_iota(jnp.int32, (seq, seq), 1)
    dk_here = jnp.zeros(dk_sum.shape, F32)
    for h in range(heads):
        span = slice(h * HEAD, (h + 1) * HEAD)
        q = q_ref[:, span]
        grad = grad_ref[:, span]
        scores = lax.dot_general(q, keys, LAST, preferred_element_type=F32) * scale
        scores = jnp.where(rows >= cols, scores, -jnp.inf)
        exponent = jnp.exp(scores - jnp.max(scores, axis=1, keepdims=True))
        probs = exponent / jnp.sum(exponent, axis=1, keepdims=True)
        prob_grad = lax.dot_general(grad, vals, LAST, preferred_element_type=F32)
        row_dot = jnp.sum(grad.astype(F32) * ao_ref[:, span].astype(F32), axis=1, keepdims=True)
        score_grad = (probs * (prob_grad - row_dot)).astype(BF16)
        dq_ref[:, span] = (jnp.dot(score_grad, keys, preferred_element_type=F32) * scale).astype(BF16)
        dk_here += lax.dot_general(score_grad, q, FIRST, preferred_element_type=F32)
    dk_sum[...] += dk_here

    @pl.when(step == pl.num_programs(0) - 1)
    def _():
        dk_ref[...] = (dk_sum[...] * scale).astype(BF16)


def score_gradients(q, k, v, ao, grad):
    seq, width = q.shape
    heads = 2
    count = width // HEAD
    wide = pl.BlockSpec((seq, heads * HEAD), lambda i: (0, i))
    narrow = whole((seq, HEAD))
    return pl.pallas_call(
        functools.partial(score_kernel, HEAD**-0.5, heads),
        grid=(count // heads,),
        in_specs=[wide, narrow, narrow, wide, wide],
        out_specs=[wide, narrow],
        out_shape=[jax.ShapeDtypeStruct((seq, width), BF16), jax.ShapeDtypeStruct((seq, HEAD), BF16)],
        scratch_shapes=[pltpu.VMEM((seq, HEAD), F32)],
        cost_estimate=LIGHT,
        compiler_params=limits(),
    )(q, k, v, ao, grad)


def input_kernel(n_xl, n_z, cols, place, dv_ref, *refs):
    wv_refs, (keep_ref, give_ref, wv_all) = refs[:-3], refs[-3:]
    c, y, n_y = place[1], place[2], len(wv_refs)
    for k, ref in enumerate(wv_refs):
        from_y = (y + n_y - k) % n_y
        for z in range(n_z):
            for xl in range(n_xl):
                start = (xl * n_z + z) * n_y + from_y
                block = ref[(z * n_xl + xl) * cols : (z * n_xl + xl + 1) * cols].astype(F32)
                wv_all[pl.ds(pl.multiple_of(start * cols, 8), cols)] = block
    wv = wv_all[...].astype(BF16)
    for xh in range(2):
        keep_ref[xh] = lax.dot_general(dv_ref[xh, c], wv, LAST, preferred_element_type=F32)
        give = lax.dot_general(dv_ref[xh, 1 - c], wv, LAST, preferred_element_type=F32)
        give_ref[xh] = give.astype(BF16)


def input_parts(place, dv, wvs, n_xl, n_z, cols):
    rows = dv.shape[2]
    feats = len(wvs) * wvs[0].shape[0]
    shape = (2, rows, feats)
    return pl.pallas_call(
        functools.partial(input_kernel, n_xl, n_z, cols),
        grid_spec=pltpu.PrefetchScalarGridSpec(
            num_scalar_prefetch=1,
            grid=(1,),
            in_specs=[whole(dv.shape)] + [whole(wv.shape) for wv in wvs],
            out_specs=[whole(shape), whole(shape)],
            scratch_shapes=[pltpu.VMEM((feats, HEAD), F32)],
        ),
        out_shape=[jax.ShapeDtypeStruct(shape, F32), jax.ShapeDtypeStruct(shape, BF16)],
        cost_estimate=SHORT,
        compiler_params=limits(),
    )(place, dv, *wvs)


def value_kernel(cols, place, near_ref, far_ref, *refs):
    dv_refs, part_refs, rows_ref = refs[:2], refs[2:-1], refs[-1]
    y = place[2]
    gather_rows(place[0], place[1], near_ref, far_ref, rows_ref)
    seq = dv_refs[0].shape[0]
    total = jnp.zeros((rows_ref.shape[1], HEAD), F32)
    for k, ref in enumerate(dv_refs):
        total += lax.dot_general(rows_ref[k * seq : (k + 1) * seq], ref[...], FIRST, preferred_element_type=F32)
    n_y = len(part_refs)
    for to_y in range(n_y):
        for k, ref in enumerate(part_refs):

            @pl.when((y + k) % n_y == to_y)
            def _():
                for z in range(ref.shape[0]):
                    start = (z * n_y + to_y) * cols
                    ref[z] = total[start : start + cols].astype(BF16)


def value_parts(place, near, far, dvs, n_y, cols):
    half = near.shape[2]
    shape = (half // cols // n_y, cols, HEAD)
    return pl.pallas_call(
        functools.partial(value_kernel, cols),
        grid_spec=pltpu.PrefetchScalarGridSpec(
            num_scalar_prefetch=1,
            grid=(1,),
            in_specs=[whole(array.shape) for array in [near, far] + dvs],
            out_specs=[whole(shape)] * n_y,
            scratch_shapes=[pltpu.VMEM((len(dvs) * dvs[0].shape[0], half), BF16)],
        ),
        out_shape=[jax.ShapeDtypeStruct(shape, BF16)] * n_y,
        cost_estimate=SHORT,
        compiler_params=limits(),
    )(place, near, far, *dvs)


def for_each(parts):
    both = jnp.broadcast_to(parts[:, None], (parts.shape[0], 2) + parts.shape[1:])
    return both.reshape((parts.shape[0] * 2,) + parts.shape[1:])


def on_device(queries, keys, values, attn_out, layer_in, out_grad, w_out, w_value):
    xl, z, y, xh, c = (lax.axis_index(a) for a in ("xl", "z", "y", "xh", "c"))
    place = jnp.stack([xl, c, y, z]).astype(jnp.int32)
    n_xl, n_z, n_y = SIZES["xl"], SIZES["z"], SIZES["y"]
    n_dp = n_xl * n_z * n_y
    q, k, v, ao, li, og = (a[0] for a in (queries, keys, values, attn_out, layer_in, out_grad))
    seq, width = q.shape
    rows, feats = og.shape
    quarter = feats // n_y
    cols = feats // n_dp

    shard = jnp.concatenate([w_out.T, w_value], axis=1)
    other = shift(shard, "xl", 1)
    plane = jnp.where(xl == 0, jnp.concatenate([shard, other]), jnp.concatenate([other, shard]))
    aos = [ao] + [shift(ao, "y", step) for step in range(1, n_y)]
    pieces = {0: plane}
    for step in range(1, n_z // 2):
        if step == 3:
            pieces[-2], pieces[2], _, _ = lax.optimization_barrier((pieces[-2], pieces[2], aos[1], aos[3]))
        pieces[-step] = shift(pieces[1 - step], "z", 1)
        pieces[step] = shift(pieces[step - 1], "z", -1)
    pieces[-n_z // 2] = shift(after(pieces[1 - n_z // 2], aos[2]), "z", 1)

    by_y = og.reshape(rows, n_xl, n_z, n_y, cols).transpose(3, 0, 2, 1, 4).reshape(n_y, rows, quarter)
    near = lax.all_to_all(after(for_each(by_y), plane), ("y", "xh"), 0, 0, tiled=True)
    near = after(near, pieces[-1], pieces[1])
    far = shift(near, "c", 1)

    by_xl = li.reshape(rows, n_xl, feats // n_xl).transpose(1, 0, 2)
    li_near = lax.all_to_all(after(for_each(by_xl), near), ("xl", "xh"), 0, 0, tiled=True)
    li_near = after(li_near, pieces[-3], pieces[3])
    li_far = shift(li_near, "c", 1)

    own, *sends, wv = head_parts(place, after(near, li_far), far, pieces, seq, width)
    recv = [shift(send, "y", -step - 1) for step, send in enumerate(sends)]
    probs = probabilities(after(q, sends[0]), k)

    part = out_part(place, after(near, sends[0]), far, aos)
    part = lax.all_to_all(part.reshape(n_z, n_xl * cols, width), "z", 0, 0, tiled=True)
    part = jnp.sum(part.astype(F32), axis=0).astype(BF16)
    wv, probs, *recv = lax.optimization_barrier((wv, probs, *recv))
    wvs = [wv] + [shift(wv, "y", step) for step in range(1, n_y)]
    head_grad, value_grad = head_gradient(probs, own, recv)
    dvs = [value_grad, shift(value_grad, "xl", 1)]

    value_part = value_parts(place, li_near, li_far, dvs, n_y, cols)
    first_part = value_part[0]
    value_part = [value_part[0]] + [shift(value_part[step], "y", step) for step in range(1, n_y)]
    value_part = sum(piece.astype(F32) for piece in value_part).astype(BF16)

    keep, give = input_parts(place, value_grad.reshape(2, 2, rows, HEAD), wvs, n_xl, n_z, cols)
    give = shift(after(give, first_part), "c", 1)

    def sum_of(i):
        return lax.dynamic_index_in_dim(keep, i, 0, False) + lax.dynamic_index_in_dim(give, i, 0, False).astype(F32)

    last = shift(sum_of(1 - xh).astype(BF16), "xh", 1)
    input_grad = (sum_of(xh) + last.astype(F32)).astype(BF16)

    value_part = lax.all_to_all(after(value_part, part), "z", 0, 0, tiled=True)

    part = part.reshape(n_xl, cols, width)
    mine = lax.dynamic_index_in_dim(part, xl, 0, False).astype(F32)
    other = shift(lax.dynamic_index_in_dim(part, 1 - xl, 0, False), "xl", 1)

    query_grad, key_grad = score_gradients(q, k, v, ao, after(head_grad, other))
    out_weight_grad = ((mine + other.astype(F32)) / n_dp).T
    value_weight_grad = jnp.sum(value_part.astype(F32), axis=0) / n_dp

    return (
        query_grad[None],
        key_grad[None],
        value_grad[None],
        input_grad[None],
        out_weight_grad,
        value_weight_grad,
    )


def solution(mesh):
    fine = Mesh(mesh.devices.reshape(tuple(SIZES.values())), tuple(SIZES))
    heads = P(DP, None, TENSOR)
    tokens = P(DP, TENSOR, None)
    return jax.shard_map(
        on_device,
        mesh=fine,
        in_specs=(heads, heads, heads, heads, tokens, tokens, P(TENSOR, DP), P(DP, TENSOR)),
        out_specs=(heads, heads, heads, tokens, P(TENSOR, DP), P(DP, TENSOR)),
        check_vma=False,
    )
```

```python
import functools

import jax
import jax.numpy as jnp
from jax import lax
from jax.experimental import pallas as pl
from jax.experimental.pallas import tpu as pltpu
from jax.sharding import Mesh
from jax.sharding import PartitionSpec as P

HEAD = 128
SIZES = {"xl": 2, "z": 8, "y": 4, "xh": 2, "c": 2}
DP = ("xl", "z", "y")
TENSOR = ("xh", "c")
F32 = jnp.float32
BF16 = jnp.bfloat16


def shift(array, axis, by):
    count = SIZES[axis]
    return lax.ppermute(array, axis, [(i, (i + by) % count) for i in range(count)])


LAST = (((1,), (1,)), ((), ()))
FIRST = (((0,), (0,)), ((), ()))


def after(array, *earlier):
    return lax.optimization_barrier((array,) + earlier)[0]


LIGHT = pl.CostEstimate(flops=1, bytes_accessed=1, transcendentals=0)
SHORT = pl.CostEstimate(flops=4 * 10**9, bytes_accessed=10**7, transcendentals=0)


def limits():
    return pltpu.CompilerParams(vmem_limit_bytes=16 * 1024 * 1024)


def whole(shape):
    return pl.BlockSpec(shape, lambda *_: (0,) * len(shape))


def probs_kernel(scale, heads, q_ref, k_ref, probs_ref):
    keys = k_ref[...]
    seq = keys.shape[0]
    rows = lax.broadcasted_iota(jnp.int32, (seq, seq), 0)
    cols = lax.broadcasted_iota(jnp.int32, (seq, seq), 1)
    for h in range(heads):
        q = q_ref[:, h * HEAD : (h + 1) * HEAD]
        scores = lax.dot_general(keys, q, LAST, preferred_element_type=F32) * scale
        scores = jnp.where(cols >= rows, scores, -jnp.inf)
        exponent = jnp.exp(scores - jnp.max(scores, axis=0, keepdims=True))
        probs_ref[h] = (exponent / jnp.sum(exponent, axis=0, keepdims=True)).astype(BF16)


def probabilities(q, k):
    seq, width = q.shape
    heads = 2
    count = width // HEAD
    return pl.pallas_call(
        functools.partial(probs_kernel, HEAD**-0.5, heads),
        grid=(count // heads,),
        in_specs=[pl.BlockSpec((seq, heads * HEAD), lambda i: (0, i)), whole((seq, HEAD))],
        out_specs=pl.BlockSpec((heads, seq, seq), lambda i: (i, 0, 0)),
        out_shape=jax.ShapeDtypeStruct((count, seq, seq), BF16),
        cost_estimate=LIGHT,
        compiler_params=limits(),
    )(q, k)


def gather_rows(position, c, near_ref, far_ref, rows_ref):
    count = near_ref.shape[0] // 2
    rows = near_ref.shape[1]
    for k in range(count):
        for xh in range(2):
            index = (position + count - k) % count * 2 + xh
            start = (k * 2 + xh) * 2 * rows
            rows_ref[pl.ds(pl.multiple_of(start + c * rows, rows), rows)] = near_ref[index]
            rows_ref[pl.ds(pl.multiple_of(start + (1 - c) * rows, rows), rows)] = far_ref[index]


def out_kernel(place, near_ref, far_ref, *refs):
    ao_refs, (part_ref, grads_ref) = refs[:-2], refs[-2:]
    step = pl.program_id(0)
    seq = ao_refs[0].shape[0]

    @pl.when(step == 0)
    def _():
        gather_rows(place[2], place[1], near_ref, far_ref, grads_ref)

    chunk = part_ref.shape[0]
    span = pl.ds(pl.multiple_of(step * chunk, chunk), chunk)
    total = jnp.zeros(part_ref.shape, F32)
    for k, ao_ref in enumerate(ao_refs):
        total += lax.dot_general(
            grads_ref[k * seq : (k + 1) * seq, span], ao_ref[...], FIRST, preferred_element_type=F32
        )
    part_ref[...] = total.astype(BF16)


def out_part(place, near, far, aos):
    seq, width = aos[0].shape
    feats = near.shape[2]
    chunk = feats // 5
    return pl.pallas_call(
        out_kernel,
        grid_spec=pltpu.PrefetchScalarGridSpec(
            num_scalar_prefetch=1,
            grid=(feats // chunk,),
            in_specs=[whole(near.shape), whole(far.shape)] + [whole(ao.shape) for ao in aos],
            out_specs=pl.BlockSpec((chunk, width), lambda i, place: (i, 0)),
            scratch_shapes=[pltpu.VMEM((len(aos) * seq, feats), BF16)],
        ),
        out_shape=jax.ShapeDtypeStruct((feats, width), BF16),
        cost_estimate=LIGHT,
        compiler_params=limits(),
    )(place, near, far, *aos)


def head_kernel(offsets, place, near_ref, far_ref, *refs):
    n_z = len(offsets)
    w_refs, wv_refs, refs = refs[:n_z], refs[n_z : 2 * n_z], refs[2 * n_z :]
    own_ref, send_refs, (wv_ref, grads_ref, w_all) = refs[0], refs[1:-3], refs[-3:]
    depth = w_refs[0].shape[0]

    def in_order(pieces, ref):
        for offset, piece in zip(offsets, pieces):
            start = (place[3] + offset + n_z) % n_z * depth
            ref[pl.ds(pl.multiple_of(start, depth), depth)] = piece[...]

    @pl.when(pl.program_id(0) == 0)
    def _():
        gather_rows(place[2], place[1], near_ref, far_ref, grads_ref)
        in_order(wv_refs, wv_ref)

    in_order(w_refs, w_all)
    seq = own_ref.shape[0]
    product = jnp.dot(grads_ref[...], w_all[...], preferred_element_type=F32)
    own_ref[...] = product[:seq]
    for k, ref in enumerate(send_refs):
        ref[...] = product[(k + 1) * seq : (k + 2) * seq].astype(BF16)


def head_parts(place, near, far, pieces, seq, width):
    feats = near.shape[2]
    count = near.shape[0] // 2
    block = 256
    depth = feats // len(pieces)
    wide = pl.BlockSpec((seq, block), lambda i, place: (0, i))
    return pl.pallas_call(
        functools.partial(head_kernel, tuple(pieces)),
        grid_spec=pltpu.PrefetchScalarGridSpec(
            num_scalar_prefetch=1,
            grid=(width // block,),
            in_specs=[whole(near.shape), whole(far.shape)]
            + [pl.BlockSpec((depth, block), lambda i, place: (0, i))] * len(pieces)
            + [pl.BlockSpec((depth, HEAD), lambda i, place: (0, width // HEAD))] * len(pieces),
            out_specs=[wide] * count + [whole((feats, HEAD))],
            scratch_shapes=[pltpu.VMEM((count * seq, feats), BF16), pltpu.VMEM((feats, block), BF16)],
        ),
        out_shape=[jax.ShapeDtypeStruct((seq, width), F32)]
        + [jax.ShapeDtypeStruct((seq, width), BF16)] * (count - 1)
        + [jax.ShapeDtypeStruct((feats, HEAD), BF16)],
        cost_estimate=LIGHT,
        compiler_params=limits(),
    )(place, near, far, *pieces.values(), *pieces.values())


def grad_kernel(heads, probs_ref, own_ref, *refs):
    recv_refs, (grad_ref, dv_ref, sums) = refs[:-3], refs[-3:]
    step = pl.program_id(0)

    @pl.when(step == 0)
    def _():
        sums[...] = jnp.zeros_like(sums)

    total = sums[...]
    for h in range(heads):
        span = slice(h * HEAD, (h + 1) * HEAD)
        grad = own_ref[:, span]
        for ref in recv_refs:
            grad += ref[:, span].astype(F32)
        grad = grad.astype(BF16)
        grad_ref[:, span] = grad
        total += jnp.dot(probs_ref[h], grad, preferred_element_type=F32)
    sums[...] = total

    @pl.when(step == pl.num_programs(0) - 1)
    def _():
        dv_ref[...] = total.astype(BF16)


def head_gradient(probs, own, recv):
    seq, width = own.shape
    heads = 2
    wide = pl.BlockSpec((seq, heads * HEAD), lambda i: (0, i))
    return pl.pallas_call(
        functools.partial(grad_kernel, heads),
        grid=(width // HEAD // heads,),
        in_specs=[pl.BlockSpec((heads, seq, seq), lambda i: (i, 0, 0))] + [wide] * (1 + len(recv)),
        out_specs=[wide, whole((seq, HEAD))],
        out_shape=[jax.ShapeDtypeStruct((seq, width), BF16), jax.ShapeDtypeStruct((seq, HEAD), BF16)],
        scratch_shapes=[pltpu.VMEM((seq, HEAD), F32)],
        cost_estimate=SHORT,
        compiler_params=limits(),
    )(probs, own, *recv)


def score_kernel(scale, heads, q_ref, k_ref, v_ref, ao_ref, grad_ref, dq_ref, dk_ref, dk_sum):
    step = pl.program_id(0)

    @pl.when(step == 0)
    def _():
        dk_sum[...] = jnp.zeros_like(dk_sum)

    keys = k_ref[...]
    vals = v_ref[...]
    seq = keys.shape[0]
    rows = lax.broadcasted_iota(jnp.int32, (seq, seq), 0)
    cols = lax.broadcasted_iota(jnp.int32, (seq, seq), 1)
    dk_here = jnp.zeros(dk_sum.shape, F32)
    for h in range(heads):
        span = slice(h * HEAD, (h + 1) * HEAD)
        q = q_ref[:, span]
        grad = grad_ref[:, span]
        scores = lax.dot_general(q, keys, LAST, preferred_element_type=F32) * scale
        scores = jnp.where(rows >= cols, scores, -jnp.inf)
        exponent = jnp.exp(scores - jnp.max(scores, axis=1, keepdims=True))
        probs = exponent / jnp.sum(exponent, axis=1, keepdims=True)
        prob_grad = lax.dot_general(grad, vals, LAST, preferred_element_type=F32)
        row_dot = jnp.sum(grad.astype(F32) * ao_ref[:, span].astype(F32), axis=1, keepdims=True)
        score_grad = (probs * (prob_grad - row_dot)).astype(BF16)
        dq_ref[:, span] = (jnp.dot(score_grad, keys, preferred_element_type=F32) * scale).astype(BF16)
        dk_here += lax.dot_general(score_grad, q, FIRST, preferred_element_type=F32)
    dk_sum[...] += dk_here

    @pl.when(step == pl.num_programs(0) - 1)
    def _():
        dk_ref[...] = (dk_sum[...] * scale).astype(BF16)


def score_gradients(q, k, v, ao, grad):
    seq, width = q.shape
    heads = 2
    count = width // HEAD
    wide = pl.BlockSpec((seq, heads * HEAD), lambda i: (0, i))
    narrow = whole((seq, HEAD))
    return pl.pallas_call(
        functools.partial(score_kernel, HEAD**-0.5, heads),
        grid=(count // heads,),
        in_specs=[wide, narrow, narrow, wide, wide],
        out_specs=[wide, narrow],
        out_shape=[jax.ShapeDtypeStruct((seq, width), BF16), jax.ShapeDtypeStruct((seq, HEAD), BF16)],
        scratch_shapes=[pltpu.VMEM((seq, HEAD), F32)],
        cost_estimate=LIGHT,
        compiler_params=limits(),
    )(q, k, v, ao, grad)


def input_kernel(n_xl, n_z, cols, place, dv_ref, *refs):
    wv_refs, (keep_ref, give_ref, wv_all) = refs[:-3], refs[-3:]
    c, y, n_y = place[1], place[2], len(wv_refs)
    for k, ref in enumerate(wv_refs):
        from_y = (y + n_y - k) % n_y
        for z in range(n_z):
            for xl in range(n_xl):
                start = (xl * n_z + z) * n_y + from_y
                block = ref[(z * n_xl + xl) * cols : (z * n_xl + xl + 1) * cols].astype(F32)
                wv_all[pl.ds(pl.multiple_of(start * cols, 8), cols)] = block
    wv = wv_all[...].astype(BF16)
    for xh in range(2):
        keep_ref[xh] = lax.dot_general(dv_ref[xh, c], wv, LAST, preferred_element_type=F32)
        give = lax.dot_general(dv_ref[xh, 1 - c], wv, LAST, preferred_element_type=F32)
        give_ref[xh] = give.astype(BF16)


def input_parts(place, dv, wvs, n_xl, n_z, cols):
    rows = dv.shape[2]
    feats = len(wvs) * wvs[0].shape[0]
    shape = (2, rows, feats)
    return pl.pallas_call(
        functools.partial(input_kernel, n_xl, n_z, cols),
        grid_spec=pltpu.PrefetchScalarGridSpec(
            num_scalar_prefetch=1,
            grid=(1,),
            in_specs=[whole(dv.shape)] + [whole(wv.shape) for wv in wvs],
            out_specs=[whole(shape), whole(shape)],
            scratch_shapes=[pltpu.VMEM((feats, HEAD), F32)],
        ),
        out_shape=[jax.ShapeDtypeStruct(shape, F32), jax.ShapeDtypeStruct(shape, BF16)],
        cost_estimate=SHORT,
        compiler_params=limits(),
    )(place, dv, *wvs)


def value_kernel(cols, place, near_ref, far_ref, *refs):
    dv_refs, part_refs, rows_ref = refs[:2], refs[2:-1], refs[-1]
    y = place[2]
    gather_rows(place[0], place[1], near_ref, far_ref, rows_ref)
    seq = dv_refs[0].shape[0]
    total = jnp.zeros((rows_ref.shape[1], HEAD), F32)
    for k, ref in enumerate(dv_refs):
        total += lax.dot_general(rows_ref[k * seq : (k + 1) * seq], ref[...], FIRST, preferred_element_type=F32)
    n_y = len(part_refs)
    for to_y in range(n_y):
        for k, ref in enumerate(part_refs):

            @pl.when((y + k) % n_y == to_y)
            def _():
                for z in range(ref.shape[0]):
                    start = (z * n_y + to_y) * cols
                    ref[z] = total[start : start + cols].astype(BF16)


def value_parts(place, near, far, dvs, n_y, cols):
    half = near.shape[2]
    shape = (half // cols // n_y, cols, HEAD)
    return pl.pallas_call(
        functools.partial(value_kernel, cols),
        grid_spec=pltpu.PrefetchScalarGridSpec(
            num_scalar_prefetch=1,
            grid=(1,),
            in_specs=[whole(array.shape) for array in [near, far] + dvs],
            out_specs=[whole(shape)] * n_y,
            scratch_shapes=[pltpu.VMEM((len(dvs) * dvs[0].shape[0], half), BF16)],
        ),
        out_shape=[jax.ShapeDtypeStruct(shape, BF16)] * n_y,
        cost_estimate=SHORT,
        compiler_params=limits(),
    )(place, near, far, *dvs)


def split_kernel(rows_ref, halves_ref):
    half = halves_ref.shape[2]
    for i in range(halves_ref.shape[0]):
        halves_ref[i] = rows_ref[:, i // 2 * half : (i // 2 + 1) * half]


def split(array, count):
    rows, feats = array.shape
    shape = (2 * count, rows, feats // count)
    return pl.pallas_call(
        split_kernel,
        in_specs=[whole(array.shape)],
        out_specs=whole(shape),
        out_shape=jax.ShapeDtypeStruct(shape, BF16),
        cost_estimate=LIGHT,
        compiler_params=limits(),
    )(array)


def for_each(parts):
    both = jnp.broadcast_to(parts[:, None], (parts.shape[0], 2) + parts.shape[1:])
    return both.reshape((parts.shape[0] * 2,) + parts.shape[1:])


def on_device(queries, keys, values, attn_out, layer_in, out_grad, w_out, w_value):
    xl, z, y, xh, c = (lax.axis_index(a) for a in ("xl", "z", "y", "xh", "c"))
    place = jnp.stack([xl, c, y, z]).astype(jnp.int32)
    n_xl, n_z, n_y = SIZES["xl"], SIZES["z"], SIZES["y"]
    n_dp = n_xl * n_z * n_y
    q, k, v, ao, li, og = (a[0] for a in (queries, keys, values, attn_out, layer_in, out_grad))
    seq, width = q.shape
    rows, feats = og.shape
    quarter = feats // n_y
    cols = feats // n_dp

    shard = jnp.concatenate([w_out.T, w_value], axis=1)
    other = shift(shard, "xl", 1)
    plane = jnp.where(xl == 0, jnp.concatenate([shard, other]), jnp.concatenate([other, shard]))
    aos = [ao] + [shift(ao, "y", step) for step in range(1, n_y)]
    pieces = {0: plane}
    for step in range(1, n_z // 2):
        if step == 3:
            pieces[-2], pieces[2], _, _ = lax.optimization_barrier((pieces[-2], pieces[2], aos[1], aos[3]))
        pieces[-step] = shift(pieces[1 - step], "z", 1)
        pieces[step] = shift(pieces[step - 1], "z", -1)
    pieces[-n_z // 2] = shift(after(pieces[1 - n_z // 2], aos[2]), "z", 1)

    by_y = og.reshape(rows, n_xl, n_z, n_y, cols).transpose(3, 0, 2, 1, 4).reshape(n_y, rows, quarter)
    near = lax.all_to_all(after(for_each(by_y), plane), ("y", "xh"), 0, 0, tiled=True)
    near = after(near, pieces[-1], pieces[1])
    far = shift(near, "c", 1)

    li_near = lax.all_to_all(after(split(li, n_xl), near), ("xl", "xh"), 0, 0, tiled=True)
    li_near = after(li_near, pieces[-3], pieces[3])
    li_far = shift(li_near, "c", 1)

    own, *sends, wv = head_parts(place, after(near, li_far), far, pieces, seq, width)
    recv = [shift(send, "y", -step - 1) for step, send in enumerate(sends)]
    probs = probabilities(after(q, sends[0]), k)

    part = out_part(place, after(near, sends[0]), far, aos)
    part = lax.all_to_all(part.reshape(n_z, n_xl * cols, width), "z", 0, 0, tiled=True)
    part = jnp.sum(part.astype(F32), axis=0).astype(BF16)
    wv, probs, *recv = lax.optimization_barrier((wv, probs, *recv))
    wvs = [wv] + [shift(wv, "y", step) for step in range(1, n_y)]
    head_grad, value_grad = head_gradient(probs, own, recv)
    dvs = [value_grad, shift(value_grad, "xl", 1)]

    value_part = value_parts(place, li_near, li_far, dvs, n_y, cols)
    first_part = value_part[0]
    value_part = [value_part[0]] + [shift(value_part[step], "y", step) for step in range(1, n_y)]
    value_part = sum(piece.astype(F32) for piece in value_part).astype(BF16)

    keep, give = input_parts(place, value_grad.reshape(2, 2, rows, HEAD), wvs, n_xl, n_z, cols)
    give = shift(after(give, first_part), "c", 1)

    def sum_of(i):
        return lax.dynamic_index_in_dim(keep, i, 0, False) + lax.dynamic_index_in_dim(give, i, 0, False).astype(F32)

    last = shift(sum_of(1 - xh).astype(BF16), "xh", 1)
    value_part = lax.all_to_all(after(value_part, part), "z", 0, 0, tiled=True)

    part = part.reshape(n_xl, cols, width)
    mine = lax.dynamic_index_in_dim(part, xl, 0, False).astype(F32)
    other = shift(lax.dynamic_index_in_dim(part, 1 - xl, 0, False), "xl", 1)

    query_grad, key_grad = score_gradients(q, k, v, ao, after(head_grad, other))
    input_grad = (sum_of(xh) + after(last, key_grad).astype(F32)).astype(BF16)
    out_weight_grad = ((mine + other.astype(F32)) / n_dp).T
    value_weight_grad = jnp.sum(value_part.astype(F32), axis=0) / n_dp

    return (
        query_grad[None],
        key_grad[None],
        value_grad[None],
        input_grad[None],
        out_weight_grad,
        value_weight_grad,
    )


def solution(mesh):
    fine = Mesh(mesh.devices.reshape(tuple(SIZES.values())), tuple(SIZES))
    heads = P(DP, None, TENSOR)
    tokens = P(DP, TENSOR, None)
    return jax.shard_map(
        on_device,
        mesh=fine,
        in_specs=(heads, heads, heads, heads, tokens, tokens, P(TENSOR, DP), P(DP, TENSOR)),
        out_specs=(heads, heads, heads, tokens, P(TENSOR, DP), P(DP, TENSOR)),
        check_vma=False,
    )
```

```python
import functools

import jax
import jax.numpy as jnp
from jax import lax
from jax.experimental import pallas as pl
from jax.experimental.pallas import tpu as pltpu
from jax.sharding import Mesh
from jax.sharding import PartitionSpec as P

HEAD = 128
SIZES = {"xl": 2, "z": 8, "y": 4, "xh": 2, "c": 2}
DP = ("xl", "z", "y")
TENSOR = ("xh", "c")
F32 = jnp.float32
BF16 = jnp.bfloat16


def shift(array, axis, by):
    count = SIZES[axis]
    return lax.ppermute(array, axis, [(i, (i + by) % count) for i in range(count)])


LAST = (((1,), (1,)), ((), ()))
FIRST = (((0,), (0,)), ((), ()))


def after(array, *earlier):
    return lax.optimization_barrier((array,) + earlier)[0]


LIGHT = pl.CostEstimate(flops=1, bytes_accessed=1, transcendentals=0)
SHORT = pl.CostEstimate(flops=4 * 10**9, bytes_accessed=10**7, transcendentals=0)


def limits():
    return pltpu.CompilerParams(vmem_limit_bytes=16 * 1024 * 1024)


def whole(shape):
    return pl.BlockSpec(shape, lambda *_: (0,) * len(shape))


def probs_kernel(scale, heads, q_ref, k_ref, probs_ref):
    keys = k_ref[...]
    seq = keys.shape[0]
    rows = lax.broadcasted_iota(jnp.int32, (seq, seq), 0)
    cols = lax.broadcasted_iota(jnp.int32, (seq, seq), 1)
    for h in range(heads):
        q = q_ref[:, h * HEAD : (h + 1) * HEAD]
        scores = lax.dot_general(keys, q, LAST, preferred_element_type=F32) * scale
        scores = jnp.where(cols >= rows, scores, -jnp.inf)
        exponent = jnp.exp(scores - jnp.max(scores, axis=0, keepdims=True))
        probs_ref[h] = (exponent / jnp.sum(exponent, axis=0, keepdims=True)).astype(BF16)


def probabilities(q, k):
    seq, width = q.shape
    heads = 2
    count = width // HEAD
    return pl.pallas_call(
        functools.partial(probs_kernel, HEAD**-0.5, heads),
        grid=(count // heads,),
        in_specs=[pl.BlockSpec((seq, heads * HEAD), lambda i: (0, i)), whole((seq, HEAD))],
        out_specs=pl.BlockSpec((heads, seq, seq), lambda i: (i, 0, 0)),
        out_shape=jax.ShapeDtypeStruct((count, seq, seq), BF16),
        cost_estimate=LIGHT,
        compiler_params=limits(),
    )(q, k)


def gather_rows(position, c, near_ref, far_ref, rows_ref):
    count = near_ref.shape[0] // 2
    rows = near_ref.shape[1]
    for k in range(count):
        for xh in range(2):
            index = (position + count - k) % count * 2 + xh
            start = (k * 2 + xh) * 2 * rows
            rows_ref[pl.ds(pl.multiple_of(start + c * rows, rows), rows)] = near_ref[index]
            rows_ref[pl.ds(pl.multiple_of(start + (1 - c) * rows, rows), rows)] = far_ref[index]


def out_kernel(place, near_ref, far_ref, *refs):
    ao_refs, (part_ref, grads_ref) = refs[:-2], refs[-2:]
    step = pl.program_id(0)
    seq = ao_refs[0].shape[0]

    @pl.when(step == 0)
    def _():
        gather_rows(place[2], place[1], near_ref, far_ref, grads_ref)

    chunk = part_ref.shape[0]
    span = pl.ds(pl.multiple_of(step * chunk, chunk), chunk)
    total = jnp.zeros(part_ref.shape, F32)
    for k, ao_ref in enumerate(ao_refs):
        total += lax.dot_general(
            grads_ref[k * seq : (k + 1) * seq, span], ao_ref[...], FIRST, preferred_element_type=F32
        )
    part_ref[...] = total.astype(BF16)


def out_part(place, near, far, aos):
    seq, width = aos[0].shape
    feats = near.shape[2]
    chunk = feats // 5
    return pl.pallas_call(
        out_kernel,
        grid_spec=pltpu.PrefetchScalarGridSpec(
            num_scalar_prefetch=1,
            grid=(feats // chunk,),
            in_specs=[whole(near.shape), whole(far.shape)] + [whole(ao.shape) for ao in aos],
            out_specs=pl.BlockSpec((chunk, width), lambda i, place: (i, 0)),
            scratch_shapes=[pltpu.VMEM((len(aos) * seq, feats), BF16)],
        ),
        out_shape=jax.ShapeDtypeStruct((feats, width), BF16),
        cost_estimate=LIGHT,
        compiler_params=limits(),
    )(place, near, far, *aos)


def head_kernel(offsets, place, near_ref, far_ref, *refs):
    n_z = len(offsets)
    w_refs, wv_refs, refs = refs[:n_z], refs[n_z : 2 * n_z], refs[2 * n_z :]
    own_ref, send_refs, (wv_ref, grads_ref, w_all) = refs[0], refs[1:-3], refs[-3:]
    depth = w_refs[0].shape[0]

    def in_order(pieces, ref):
        for offset, piece in zip(offsets, pieces):
            start = (place[3] + offset + n_z) % n_z * depth
            ref[pl.ds(pl.multiple_of(start, depth), depth)] = piece[...]

    @pl.when(pl.program_id(0) == 0)
    def _():
        gather_rows(place[2], place[1], near_ref, far_ref, grads_ref)
        in_order(wv_refs, wv_ref)

    in_order(w_refs, w_all)
    seq = own_ref.shape[0]
    product = jnp.dot(grads_ref[...], w_all[...], preferred_element_type=F32)
    own_ref[...] = product[:seq]
    for k, ref in enumerate(send_refs):
        ref[...] = product[(k + 1) * seq : (k + 2) * seq].astype(BF16)


def head_parts(place, near, far, pieces, seq, width):
    feats = near.shape[2]
    count = near.shape[0] // 2
    block = 256
    depth = feats // len(pieces)
    wide = pl.BlockSpec((seq, block), lambda i, place: (0, i))
    return pl.pallas_call(
        functools.partial(head_kernel, tuple(pieces)),
        grid_spec=pltpu.PrefetchScalarGridSpec(
            num_scalar_prefetch=1,
            grid=(width // block,),
            in_specs=[whole(near.shape), whole(far.shape)]
            + [pl.BlockSpec((depth, block), lambda i, place: (0, i))] * len(pieces)
            + [pl.BlockSpec((depth, HEAD), lambda i, place: (0, width // HEAD))] * len(pieces),
            out_specs=[wide] * count + [whole((feats, HEAD))],
            scratch_shapes=[pltpu.VMEM((count * seq, feats), BF16), pltpu.VMEM((feats, block), BF16)],
        ),
        out_shape=[jax.ShapeDtypeStruct((seq, width), F32)]
        + [jax.ShapeDtypeStruct((seq, width), BF16)] * (count - 1)
        + [jax.ShapeDtypeStruct((feats, HEAD), BF16)],
        cost_estimate=LIGHT,
        compiler_params=limits(),
    )(place, near, far, *pieces.values(), *pieces.values())


def grad_kernel(heads, probs_ref, own_ref, *refs):
    recv_refs, (grad_ref, dv_ref) = refs[:-2], refs[-2:]
    total = jnp.zeros(dv_ref.shape, F32)
    for h in range(heads):
        span = slice(h * HEAD, (h + 1) * HEAD)
        grad = own_ref[:, span]
        for ref in recv_refs:
            grad += ref[:, span].astype(F32)
        grad = grad.astype(BF16)
        grad_ref[:, span] = grad
        total += jnp.dot(probs_ref[h], grad, preferred_element_type=F32)
    dv_ref[...] = total.astype(BF16)


def head_gradient(probs, own, recv):
    seq, width = own.shape
    return pl.pallas_call(
        functools.partial(grad_kernel, width // HEAD),
        out_shape=[jax.ShapeDtypeStruct((seq, width), BF16), jax.ShapeDtypeStruct((seq, HEAD), BF16)],
        cost_estimate=SHORT,
        compiler_params=limits(),
    )(probs, own, *recv)


def score_kernel(scale, heads, q_ref, k_ref, v_ref, ao_ref, grad_ref, dq_ref, dk_ref, dk_sum):
    step = pl.program_id(0)

    @pl.when(step == 0)
    def _():
        dk_sum[...] = jnp.zeros_like(dk_sum)

    keys = k_ref[...]
    vals = v_ref[...]
    seq = keys.shape[0]
    rows = lax.broadcasted_iota(jnp.int32, (seq, seq), 0)
    cols = lax.broadcasted_iota(jnp.int32, (seq, seq), 1)
    dk_here = jnp.zeros(dk_sum.shape, F32)
    for h in range(heads):
        span = slice(h * HEAD, (h + 1) * HEAD)
        q = q_ref[:, span]
        grad = grad_ref[:, span]
        scores = lax.dot_general(q, keys, LAST, preferred_element_type=F32) * scale
        scores = jnp.where(rows >= cols, scores, -jnp.inf)
        exponent = jnp.exp(scores - jnp.max(scores, axis=1, keepdims=True))
        probs = exponent / jnp.sum(exponent, axis=1, keepdims=True)
        prob_grad = lax.dot_general(grad, vals, LAST, preferred_element_type=F32)
        row_dot = jnp.sum(grad.astype(F32) * ao_ref[:, span].astype(F32), axis=1, keepdims=True)
        score_grad = (probs * (prob_grad - row_dot)).astype(BF16)
        dq_ref[:, span] = (jnp.dot(score_grad, keys, preferred_element_type=F32) * scale).astype(BF16)
        dk_here += lax.dot_general(score_grad, q, FIRST, preferred_element_type=F32)
    dk_sum[...] += dk_here

    @pl.when(step == pl.num_programs(0) - 1)
    def _():
        dk_ref[...] = (dk_sum[...] * scale).astype(BF16)


def score_gradients(q, k, v, ao, grad):
    seq, width = q.shape
    heads = 2
    count = width // HEAD
    wide = pl.BlockSpec((seq, heads * HEAD), lambda i: (0, i))
    narrow = whole((seq, HEAD))
    return pl.pallas_call(
        functools.partial(score_kernel, HEAD**-0.5, heads),
        grid=(count // heads,),
        in_specs=[wide, narrow, narrow, wide, wide],
        out_specs=[wide, narrow],
        out_shape=[jax.ShapeDtypeStruct((seq, width), BF16), jax.ShapeDtypeStruct((seq, HEAD), BF16)],
        scratch_shapes=[pltpu.VMEM((seq, HEAD), F32)],
        cost_estimate=LIGHT,
        compiler_params=limits(),
    )(q, k, v, ao, grad)


def input_kernel(n_xl, n_z, cols, place, dv_ref, *refs):
    wv_refs, (keep_ref, give_ref, wv_all) = refs[:-3], refs[-3:]
    c, y, n_y = place[1], place[2], len(wv_refs)
    for k, ref in enumerate(wv_refs):
        from_y = (y + n_y - k) % n_y
        for z in range(n_z):
            for xl in range(n_xl):
                start = (xl * n_z + z) * n_y + from_y
                block = ref[(z * n_xl + xl) * cols : (z * n_xl + xl + 1) * cols].astype(F32)
                wv_all[pl.ds(pl.multiple_of(start * cols, 8), cols)] = block
    wv = wv_all[...].astype(BF16)
    for xh in range(2):
        keep_ref[xh] = lax.dot_general(dv_ref[xh, c], wv, LAST, preferred_element_type=F32)
        give = lax.dot_general(dv_ref[xh, 1 - c], wv, LAST, preferred_element_type=F32)
        give_ref[xh] = give.astype(BF16)


def input_parts(place, dv, wvs, n_xl, n_z, cols):
    rows = dv.shape[2]
    feats = len(wvs) * wvs[0].shape[0]
    shape = (2, rows, feats)
    return pl.pallas_call(
        functools.partial(input_kernel, n_xl, n_z, cols),
        grid_spec=pltpu.PrefetchScalarGridSpec(
            num_scalar_prefetch=1,
            grid=(1,),
            in_specs=[whole(dv.shape)] + [whole(wv.shape) for wv in wvs],
            out_specs=[whole(shape), whole(shape)],
            scratch_shapes=[pltpu.VMEM((feats, HEAD), F32)],
        ),
        out_shape=[jax.ShapeDtypeStruct(shape, F32), jax.ShapeDtypeStruct(shape, BF16)],
        cost_estimate=SHORT,
        compiler_params=limits(),
    )(place, dv, *wvs)


def value_kernel(cols, place, near_ref, far_ref, *refs):
    dv_refs, part_refs, rows_ref = refs[:2], refs[2:-1], refs[-1]
    y = place[2]
    gather_rows(place[0], place[1], near_ref, far_ref, rows_ref)
    seq = dv_refs[0].shape[0]
    total = jnp.zeros((rows_ref.shape[1], HEAD), F32)
    for k, ref in enumerate(dv_refs):
        total += lax.dot_general(rows_ref[k * seq : (k + 1) * seq], ref[...], FIRST, preferred_element_type=F32)
    n_y = len(part_refs)
    for to_y in range(n_y):
        for k, ref in enumerate(part_refs):

            @pl.when((y + k) % n_y == to_y)
            def _():
                for z in range(ref.shape[0]):
                    start = (z * n_y + to_y) * cols
                    ref[z] = total[start : start + cols].astype(BF16)


def value_parts(place, near, far, dvs, n_y, cols):
    half = near.shape[2]
    shape = (half // cols // n_y, cols, HEAD)
    return pl.pallas_call(
        functools.partial(value_kernel, cols),
        grid_spec=pltpu.PrefetchScalarGridSpec(
            num_scalar_prefetch=1,
            grid=(1,),
            in_specs=[whole(array.shape) for array in [near, far] + dvs],
            out_specs=[whole(shape)] * n_y,
            scratch_shapes=[pltpu.VMEM((len(dvs) * dvs[0].shape[0], half), BF16)],
        ),
        out_shape=[jax.ShapeDtypeStruct(shape, BF16)] * n_y,
        cost_estimate=SHORT,
        compiler_params=limits(),
    )(place, near, far, *dvs)


def split_kernel(rows_ref, halves_ref):
    half = halves_ref.shape[2]
    for i in range(halves_ref.shape[0]):
        halves_ref[i] = rows_ref[:, i // 2 * half : (i // 2 + 1) * half]


def split(array, count):
    rows, feats = array.shape
    shape = (2 * count, rows, feats // count)
    return pl.pallas_call(
        split_kernel,
        in_specs=[whole(array.shape)],
        out_specs=whole(shape),
        out_shape=jax.ShapeDtypeStruct(shape, BF16),
        cost_estimate=LIGHT,
        compiler_params=limits(),
    )(array)


def for_each(parts):
    both = jnp.broadcast_to(parts[:, None], (parts.shape[0], 2) + parts.shape[1:])
    return both.reshape((parts.shape[0] * 2,) + parts.shape[1:])


def on_device(queries, keys, values, attn_out, layer_in, out_grad, w_out, w_value):
    xl, z, y, xh, c = (lax.axis_index(a) for a in ("xl", "z", "y", "xh", "c"))
    place = jnp.stack([xl, c, y, z]).astype(jnp.int32)
    n_xl, n_z, n_y = SIZES["xl"], SIZES["z"], SIZES["y"]
    n_dp = n_xl * n_z * n_y
    q, k, v, ao, li, og = (a[0] for a in (queries, keys, values, attn_out, layer_in, out_grad))
    seq, width = q.shape
    rows, feats = og.shape
    quarter = feats // n_y
    cols = feats // n_dp

    shard = jnp.concatenate([w_out.T, w_value], axis=1)
    other = shift(shard, "xl", 1)
    plane = jnp.where(xl == 0, jnp.concatenate([shard, other]), jnp.concatenate([other, shard]))
    aos = [ao] + [shift(ao, "y", step) for step in range(1, n_y)]
    pieces = {0: plane}
    for step in range(1, n_z // 2):
        if step == 3:
            pieces[-2], pieces[2], *_ = lax.optimization_barrier((pieces[-2], pieces[2], *aos[1:]))
        pieces[-step] = shift(pieces[1 - step], "z", 1)
        pieces[step] = shift(pieces[step - 1], "z", -1)
    pieces[-n_z // 2] = shift(pieces[1 - n_z // 2], "z", 1)

    by_y = og.reshape(rows, n_xl, n_z, n_y, cols).transpose(3, 0, 2, 1, 4).reshape(n_y, rows, quarter)
    near = lax.all_to_all(after(for_each(by_y), plane), ("y", "xh"), 0, 0, tiled=True)
    near = after(near, pieces[-1], pieces[1])
    far = shift(near, "c", 1)

    li_near = lax.all_to_all(after(split(li, n_xl), near), ("xl", "xh"), 0, 0, tiled=True)
    li_near = after(li_near, pieces[-3], pieces[3])
    li_far = shift(li_near, "c", 1)

    own, *sends, wv = head_parts(place, after(near, li_far), far, pieces, seq, width)
    recv = [shift(send, "y", -step - 1) for step, send in enumerate(sends)]
    probs = probabilities(after(q, sends[0]), k)

    part = out_part(place, after(near, sends[0]), far, aos)
    part = lax.all_to_all(part.reshape(n_z, n_xl * cols, width), "z", 0, 0, tiled=True)
    part = jnp.sum(part.astype(F32), axis=0).astype(BF16)
    wv, probs, *recv = lax.optimization_barrier((wv, probs, *recv))
    wvs = [wv] + [shift(wv, "y", step) for step in range(1, n_y)]
    head_grad, value_grad = head_gradient(probs, own, recv)
    dvs = [value_grad, shift(value_grad, "xl", 1)]

    value_part = value_parts(place, li_near, li_far, dvs, n_y, cols)
    first_part = value_part[0]
    value_part = [value_part[0]] + [shift(value_part[step], "y", step) for step in range(1, n_y)]
    value_part = sum(piece.astype(F32) for piece in value_part).astype(BF16)

    keep, give = input_parts(place, value_grad.reshape(2, 2, rows, HEAD), wvs, n_xl, n_z, cols)
    give = shift(after(give, first_part), "c", 1)

    def sum_of(i):
        return lax.dynamic_index_in_dim(keep, i, 0, False) + lax.dynamic_index_in_dim(give, i, 0, False).astype(F32)

    last = shift(sum_of(1 - xh).astype(BF16), "xh", 1)
    value_part = lax.all_to_all(after(value_part, part), "z", 0, 0, tiled=True)

    part = part.reshape(n_xl, cols, width)
    mine = lax.dynamic_index_in_dim(part, xl, 0, False).astype(F32)
    other = shift(lax.dynamic_index_in_dim(part, 1 - xl, 0, False), "xl", 1)

    query_grad, key_grad = score_gradients(q, k, v, ao, after(head_grad, other))
    input_grad = (sum_of(xh) + after(last, key_grad).astype(F32)).astype(BF16)
    out_weight_grad = ((mine + other.astype(F32)) / n_dp).T
    value_weight_grad = jnp.sum(value_part.astype(F32), axis=0) / n_dp

    return (
        query_grad[None],
        key_grad[None],
        value_grad[None],
        input_grad[None],
        out_weight_grad,
        value_weight_grad,
    )


def solution(mesh):
    fine = Mesh(mesh.devices.reshape(tuple(SIZES.values())), tuple(SIZES))
    heads = P(DP, None, TENSOR)
    tokens = P(DP, TENSOR, None)
    return jax.shard_map(
        on_device,
        mesh=fine,
        in_specs=(heads, heads, heads, heads, tokens, tokens, P(TENSOR, DP), P(DP, TENSOR)),
        out_specs=(heads, heads, heads, tokens, P(TENSOR, DP), P(DP, TENSOR)),
        check_vma=False,
    )
```

```python
import functools

import jax
import jax.numpy as jnp
from jax import lax
from jax.experimental import pallas as pl
from jax.experimental.pallas import tpu as pltpu
from jax.sharding import Mesh
from jax.sharding import PartitionSpec as P

HEAD = 128
SIZES = {"xl": 2, "z": 8, "y": 4, "xh": 2, "c": 2}
DP = ("xl", "z", "y")
TENSOR = ("xh", "c")
F32 = jnp.float32
BF16 = jnp.bfloat16


def shift(array, axis, by):
    count = SIZES[axis]
    return lax.ppermute(array, axis, [(i, (i + by) % count) for i in range(count)])


LAST = (((1,), (1,)), ((), ()))
FIRST = (((0,), (0,)), ((), ()))


def after(array, *earlier):
    return lax.optimization_barrier((array,) + earlier)[0]


LIGHT = pl.CostEstimate(flops=1, bytes_accessed=1, transcendentals=0)
SHORT = pl.CostEstimate(flops=4 * 10**9, bytes_accessed=10**7, transcendentals=0)


def limits():
    return pltpu.CompilerParams(vmem_limit_bytes=16 * 1024 * 1024)


def whole(shape):
    return pl.BlockSpec(shape, lambda *_: (0,) * len(shape))


def probs_kernel(scale, heads, q_ref, k_ref, probs_ref):
    keys = k_ref[...]
    seq = keys.shape[0]
    rows = lax.broadcasted_iota(jnp.int32, (seq, seq), 0)
    cols = lax.broadcasted_iota(jnp.int32, (seq, seq), 1)
    for h in range(heads):
        q = q_ref[:, h * HEAD : (h + 1) * HEAD]
        scores = lax.dot_general(keys, q, LAST, preferred_element_type=F32) * scale
        scores = jnp.where(cols >= rows, scores, -jnp.inf)
        exponent = jnp.exp(scores - jnp.max(scores, axis=0, keepdims=True))
        probs_ref[h] = (exponent / jnp.sum(exponent, axis=0, keepdims=True)).astype(BF16)


def probabilities(q, k):
    seq, width = q.shape
    heads = 2
    count = width // HEAD
    return pl.pallas_call(
        functools.partial(probs_kernel, HEAD**-0.5, heads),
        grid=(count // heads,),
        in_specs=[pl.BlockSpec((seq, heads * HEAD), lambda i: (0, i)), whole((seq, HEAD))],
        out_specs=pl.BlockSpec((heads, seq, seq), lambda i: (i, 0, 0)),
        out_shape=jax.ShapeDtypeStruct((count, seq, seq), BF16),
        cost_estimate=LIGHT,
        compiler_params=limits(),
    )(q, k)


def gather_rows(position, c, near_ref, far_ref, rows_ref):
    count = near_ref.shape[0] // 2
    rows = near_ref.shape[1]
    for k in range(count):
        for xh in range(2):
            index = (position + count - k) % count * 2 + xh
            start = (k * 2 + xh) * 2 * rows
            rows_ref[pl.ds(pl.multiple_of(start + c * rows, rows), rows)] = near_ref[index]
            rows_ref[pl.ds(pl.multiple_of(start + (1 - c) * rows, rows), rows)] = far_ref[index]


def out_kernel(place, near_ref, far_ref, *refs):
    ao_refs, (part_ref, grads_ref) = refs[:-2], refs[-2:]
    step = pl.program_id(0)
    seq = ao_refs[0].shape[0]

    @pl.when(step == 0)
    def _():
        gather_rows(place[2], place[1], near_ref, far_ref, grads_ref)

    chunk = part_ref.shape[0]
    span = pl.ds(pl.multiple_of(step * chunk, chunk), chunk)
    total = jnp.zeros(part_ref.shape, F32)
    for k, ao_ref in enumerate(ao_refs):
        total += lax.dot_general(
            grads_ref[k * seq : (k + 1) * seq, span], ao_ref[...], FIRST, preferred_element_type=F32
        )
    part_ref[...] = total.astype(BF16)


def out_part(place, near, far, aos):
    seq, width = aos[0].shape
    feats = near.shape[2]
    chunk = feats // 5
    return pl.pallas_call(
        out_kernel,
        grid_spec=pltpu.PrefetchScalarGridSpec(
            num_scalar_prefetch=1,
            grid=(feats // chunk,),
            in_specs=[whole(near.shape), whole(far.shape)] + [whole(ao.shape) for ao in aos],
            out_specs=pl.BlockSpec((chunk, width), lambda i, place: (i, 0)),
            scratch_shapes=[pltpu.VMEM((len(aos) * seq, feats), BF16)],
        ),
        out_shape=jax.ShapeDtypeStruct((feats, width), BF16),
        cost_estimate=LIGHT,
        compiler_params=limits(),
    )(place, near, far, *aos)


def head_kernel(offsets, place, near_ref, far_ref, *refs):
    n_z = len(offsets)
    w_refs, wv_refs, refs = refs[:n_z], refs[n_z : 2 * n_z], refs[2 * n_z :]
    own_ref, send_refs, (wv_ref, grads_ref, w_all) = refs[0], refs[1:-3], refs[-3:]
    depth = w_refs[0].shape[0]

    def in_order(pieces, ref):
        for offset, piece in zip(offsets, pieces):
            start = (place[3] + offset + n_z) % n_z * depth
            ref[pl.ds(pl.multiple_of(start, depth), depth)] = piece[...]

    @pl.when(pl.program_id(0) == 0)
    def _():
        gather_rows(place[2], place[1], near_ref, far_ref, grads_ref)
        in_order(wv_refs, wv_ref)

    in_order(w_refs, w_all)
    seq = own_ref.shape[0]
    product = jnp.dot(grads_ref[...], w_all[...], preferred_element_type=F32)
    own_ref[...] = product[:seq]
    for k, ref in enumerate(send_refs):
        ref[...] = product[(k + 1) * seq : (k + 2) * seq].astype(BF16)


def head_parts(place, near, far, pieces, seq, width):
    feats = near.shape[2]
    count = near.shape[0] // 2
    block = 256
    depth = feats // len(pieces)
    wide = pl.BlockSpec((seq, block), lambda i, place: (0, i))
    return pl.pallas_call(
        functools.partial(head_kernel, tuple(pieces)),
        grid_spec=pltpu.PrefetchScalarGridSpec(
            num_scalar_prefetch=1,
            grid=(width // block,),
            in_specs=[whole(near.shape), whole(far.shape)]
            + [pl.BlockSpec((depth, block), lambda i, place: (0, i))] * len(pieces)
            + [pl.BlockSpec((depth, HEAD), lambda i, place: (0, width // HEAD))] * len(pieces),
            out_specs=[wide] * count + [whole((feats, HEAD))],
            scratch_shapes=[pltpu.VMEM((count * seq, feats), BF16), pltpu.VMEM((feats, block), BF16)],
        ),
        out_shape=[jax.ShapeDtypeStruct((seq, width), F32)]
        + [jax.ShapeDtypeStruct((seq, width), BF16)] * (count - 1)
        + [jax.ShapeDtypeStruct((feats, HEAD), BF16)],
        cost_estimate=LIGHT,
        compiler_params=limits(),
    )(place, near, far, *pieces.values(), *pieces.values())


def grad_kernel(heads, probs_ref, own_ref, *refs):
    recv_refs, (grad_ref, dv_ref) = refs[:-2], refs[-2:]
    total = jnp.zeros(dv_ref.shape, F32)
    for h in range(heads):
        span = slice(h * HEAD, (h + 1) * HEAD)
        grad = own_ref[:, span]
        for ref in recv_refs:
            grad += ref[:, span].astype(F32)
        grad = grad.astype(BF16)
        grad_ref[:, span] = grad
        total += jnp.dot(probs_ref[h], grad, preferred_element_type=F32)
    dv_ref[...] = total.astype(BF16)


def head_gradient(probs, own, recv):
    seq, width = own.shape
    return pl.pallas_call(
        functools.partial(grad_kernel, width // HEAD),
        out_shape=[jax.ShapeDtypeStruct((seq, width), BF16), jax.ShapeDtypeStruct((seq, HEAD), BF16)],
        cost_estimate=SHORT,
        compiler_params=limits(),
    )(probs, own, *recv)


def score_kernel(scale, heads, q_ref, k_ref, v_ref, ao_ref, grad_ref, dq_ref, dk_ref, dk_sum):
    step = pl.program_id(0)

    @pl.when(step == 0)
    def _():
        dk_sum[...] = jnp.zeros_like(dk_sum)

    keys = k_ref[...]
    vals = v_ref[...]
    seq = keys.shape[0]
    rows = lax.broadcasted_iota(jnp.int32, (seq, seq), 0)
    cols = lax.broadcasted_iota(jnp.int32, (seq, seq), 1)
    dk_here = jnp.zeros(dk_sum.shape, F32)
    for h in range(heads):
        span = slice(h * HEAD, (h + 1) * HEAD)
        q = q_ref[:, span]
        grad = grad_ref[:, span]
        scores = lax.dot_general(q, keys, LAST, preferred_element_type=F32) * scale
        scores = jnp.where(rows >= cols, scores, -jnp.inf)
        exponent = jnp.exp(scores - jnp.max(scores, axis=1, keepdims=True))
        probs = exponent / jnp.sum(exponent, axis=1, keepdims=True)
        prob_grad = lax.dot_general(grad, vals, LAST, preferred_element_type=F32)
        row_dot = jnp.sum(grad.astype(F32) * ao_ref[:, span].astype(F32), axis=1, keepdims=True)
        score_grad = (probs * (prob_grad - row_dot)).astype(BF16)
        dq_ref[:, span] = (jnp.dot(score_grad, keys, preferred_element_type=F32) * scale).astype(BF16)
        dk_here += lax.dot_general(score_grad, q, FIRST, preferred_element_type=F32)
    dk_sum[...] += dk_here

    @pl.when(step == pl.num_programs(0) - 1)
    def _():
        dk_ref[...] = (dk_sum[...] * scale).astype(BF16)


def score_gradients(q, k, v, ao, grad):
    seq, width = q.shape
    heads = 2
    count = width // HEAD
    wide = pl.BlockSpec((seq, heads * HEAD), lambda i: (0, i))
    narrow = whole((seq, HEAD))
    return pl.pallas_call(
        functools.partial(score_kernel, HEAD**-0.5, heads),
        grid=(count // heads,),
        in_specs=[wide, narrow, narrow, wide, wide],
        out_specs=[wide, narrow],
        out_shape=[jax.ShapeDtypeStruct((seq, width), BF16), jax.ShapeDtypeStruct((seq, HEAD), BF16)],
        scratch_shapes=[pltpu.VMEM((seq, HEAD), F32)],
        cost_estimate=LIGHT,
        compiler_params=limits(),
    )(q, k, v, ao, grad)


def input_kernel(n_xl, n_z, cols, place, dv_ref, *refs):
    wv_refs, (keep_ref, give_ref, wv_all) = refs[:-3], refs[-3:]
    c, y, n_y = place[1], place[2], len(wv_refs)
    for k, ref in enumerate(wv_refs):
        from_y = (y + n_y - k) % n_y
        for z in range(n_z):
            for xl in range(n_xl):
                start = (xl * n_z + z) * n_y + from_y
                block = ref[(z * n_xl + xl) * cols : (z * n_xl + xl + 1) * cols].astype(F32)
                wv_all[pl.ds(pl.multiple_of(start * cols, 8), cols)] = block
    wv = wv_all[...].astype(BF16)
    for xh in range(2):
        keep_ref[xh] = lax.dot_general(dv_ref[xh, c], wv, LAST, preferred_element_type=F32)
        give = lax.dot_general(dv_ref[xh, 1 - c], wv, LAST, preferred_element_type=F32)
        give_ref[xh] = give.astype(BF16)


def input_parts(place, dv, wvs, n_xl, n_z, cols):
    rows = dv.shape[2]
    feats = len(wvs) * wvs[0].shape[0]
    shape = (2, rows, feats)
    return pl.pallas_call(
        functools.partial(input_kernel, n_xl, n_z, cols),
        grid_spec=pltpu.PrefetchScalarGridSpec(
            num_scalar_prefetch=1,
            grid=(1,),
            in_specs=[whole(dv.shape)] + [whole(wv.shape) for wv in wvs],
            out_specs=[whole(shape), whole(shape)],
            scratch_shapes=[pltpu.VMEM((feats, HEAD), F32)],
        ),
        out_shape=[jax.ShapeDtypeStruct(shape, F32), jax.ShapeDtypeStruct(shape, BF16)],
        cost_estimate=SHORT,
        compiler_params=limits(),
    )(place, dv, *wvs)


def value_kernel(cols, scale, place, near_ref, far_ref, *refs):
    dv_refs, part_refs, rows_ref = refs[:2], refs[2:-1], refs[-1]
    y = place[2]
    gather_rows(place[0], place[1], near_ref, far_ref, rows_ref)
    seq = dv_refs[0].shape[0]
    total = jnp.zeros((rows_ref.shape[1], HEAD), F32)
    for k, ref in enumerate(dv_refs):
        total += lax.dot_general(rows_ref[k * seq : (k + 1) * seq], ref[...], FIRST, preferred_element_type=F32)
    n_y = len(part_refs)
    for to_y in range(n_y):
        for k, ref in enumerate(part_refs):

            @pl.when((y + k) % n_y == to_y)
            def _():
                for z in range(ref.shape[0]):
                    start = (z * n_y + to_y) * cols
                    ref[z] = (total[start : start + cols] * scale).astype(BF16)


def value_parts(place, near, far, dvs, n_y, cols, scale):
    half = near.shape[2]
    shape = (half // cols // n_y, cols, HEAD)
    return pl.pallas_call(
        functools.partial(value_kernel, cols, scale),
        grid_spec=pltpu.PrefetchScalarGridSpec(
            num_scalar_prefetch=1,
            grid=(1,),
            in_specs=[whole(array.shape) for array in [near, far] + dvs],
            out_specs=[whole(shape)] * n_y,
            scratch_shapes=[pltpu.VMEM((len(dvs) * dvs[0].shape[0], half), BF16)],
        ),
        out_shape=[jax.ShapeDtypeStruct(shape, BF16)] * n_y,
        cost_estimate=SHORT,
        compiler_params=limits(),
    )(place, near, far, *dvs)


def split_kernel(rows_ref, halves_ref):
    half = halves_ref.shape[2]
    for i in range(halves_ref.shape[0]):
        halves_ref[i] = rows_ref[:, i // 2 * half : (i // 2 + 1) * half]


def split(array, count):
    rows, feats = array.shape
    shape = (2 * count, rows, feats // count)
    return pl.pallas_call(
        split_kernel,
        in_specs=[whole(array.shape)],
        out_specs=whole(shape),
        out_shape=jax.ShapeDtypeStruct(shape, BF16),
        cost_estimate=LIGHT,
        compiler_params=limits(),
    )(array)


def for_each(parts):
    both = jnp.broadcast_to(parts[:, None], (parts.shape[0], 2) + parts.shape[1:])
    return both.reshape((parts.shape[0] * 2,) + parts.shape[1:])


def on_device(queries, keys, values, attn_out, layer_in, out_grad, w_out, w_value):
    xl, z, y, xh, c = (lax.axis_index(a) for a in ("xl", "z", "y", "xh", "c"))
    place = jnp.stack([xl, c, y, z]).astype(jnp.int32)
    n_xl, n_z, n_y = SIZES["xl"], SIZES["z"], SIZES["y"]
    n_dp = n_xl * n_z * n_y
    q, k, v, ao, li, og = (a[0] for a in (queries, keys, values, attn_out, layer_in, out_grad))
    seq, width = q.shape
    rows, feats = og.shape
    quarter = feats // n_y
    cols = feats // n_dp

    shard = jnp.concatenate([w_out.T, w_value], axis=1)
    other = shift(shard, "xl", 1)
    plane = jnp.where(xl == 0, jnp.concatenate([shard, other]), jnp.concatenate([other, shard]))
    aos = [ao] + [shift(ao, "y", step) for step in range(1, n_y)]
    pieces = {0: plane}
    for step in range(1, n_z // 2):
        if step == 3:
            pieces[-2], pieces[2], _, _ = lax.optimization_barrier((pieces[-2], pieces[2], aos[1], aos[3]))
        pieces[-step] = shift(pieces[1 - step], "z", 1)
        pieces[step] = shift(pieces[step - 1], "z", -1)
    pieces[-n_z // 2] = shift(after(pieces[1 - n_z // 2], aos[2]), "z", 1)

    by_y = og.reshape(rows, n_xl, n_z, n_y, cols).transpose(3, 0, 2, 1, 4).reshape(n_y, rows, quarter)
    near = lax.all_to_all(after(for_each(by_y), plane), ("y", "xh"), 0, 0, tiled=True)
    near = after(near, pieces[-1], pieces[1])
    far = shift(near, "c", 1)

    li_near = lax.all_to_all(after(split(li, n_xl), near), ("xl", "xh"), 0, 0, tiled=True)
    li_near = after(li_near, pieces[-3], pieces[3])
    li_far = shift(li_near, "c", 1)

    own, *sends, wv = head_parts(place, after(near, li_far), far, pieces, seq, width)
    recv = [shift(send, "y", -step - 1) for step, send in enumerate(sends)]
    probs = probabilities(after(q, sends[0]), k)

    part = out_part(place, after(near, sends[0]), far, aos)
    parts = lax.all_to_all(part.reshape(n_z, n_xl * cols, width), "z", 0, 0, tiled=True)
    part = jnp.sum(parts.astype(F32), axis=0).astype(BF16)
    wv, probs, *recv = lax.optimization_barrier((wv, probs, *recv))
    wvs = [wv] + [shift(wv, "y", step) for step in range(1, n_y)]
    head_grad, value_grad = head_gradient(probs, own, recv)
    dvs = [value_grad, shift(value_grad, "xl", 1)]

    value_part = value_parts(place, li_near, li_far, dvs, n_y, cols, 1 / n_dp)
    first_part = value_part[0]
    value_part = [value_part[0]] + [shift(value_part[step], "y", step) for step in range(1, n_y)]
    value_part = sum(piece.astype(F32) for piece in value_part).astype(BF16)

    keep, give = input_parts(place, value_grad.reshape(2, 2, rows, HEAD), wvs, n_xl, n_z, cols)
    give = shift(after(give, first_part), "c", 1)

    def sum_of(i):
        return lax.dynamic_index_in_dim(keep, i, 0, False) + lax.dynamic_index_in_dim(give, i, 0, False).astype(F32)

    last = shift(sum_of(1 - xh).astype(BF16), "xh", 1)
    value_part = lax.all_to_all(after(value_part, parts), "z", 0, 0, tiled=True)

    part = part.reshape(n_xl, cols, width)
    mine = lax.dynamic_index_in_dim(part, xl, 0, False).astype(F32)
    other = shift(lax.dynamic_index_in_dim(part, 1 - xl, 0, False), "xl", 1)

    query_grad, key_grad = score_gradients(q, k, v, ao, after(head_grad, other))
    input_grad = (sum_of(xh) + after(last, key_grad).astype(F32)).astype(BF16)
    out_weight_grad = ((mine + other.astype(F32)) / n_dp).T
    value_weight_grad = jnp.sum(value_part.astype(F32), axis=0)

    return (
        query_grad[None],
        key_grad[None],
        value_grad[None],
        input_grad[None],
        out_weight_grad,
        value_weight_grad,
    )


def solution(mesh):
    fine = Mesh(mesh.devices.reshape(tuple(SIZES.values())), tuple(SIZES))
    heads = P(DP, None, TENSOR)
    tokens = P(DP, TENSOR, None)
    return jax.shard_map(
        on_device,
        mesh=fine,
        in_specs=(heads, heads, heads, heads, tokens, tokens, P(TENSOR, DP), P(DP, TENSOR)),
        out_specs=(heads, heads, heads, tokens, P(TENSOR, DP), P(DP, TENSOR)),
        check_vma=False,
    )
```

```python
import functools

import jax
import jax.numpy as jnp
from jax import lax
from jax.experimental import pallas as pl
from jax.experimental.pallas import tpu as pltpu
from jax.sharding import Mesh
from jax.sharding import PartitionSpec as P

HEAD = 128
SIZES = {"xl": 2, "z": 8, "y": 4, "xh": 2, "c": 2}
DP = ("xl", "z", "y")
TENSOR = ("xh", "c")
F32 = jnp.float32
BF16 = jnp.bfloat16


def shift(array, axis, by):
    count = SIZES[axis]
    return lax.ppermute(array, axis, [(i, (i + by) % count) for i in range(count)])


LAST = (((1,), (1,)), ((), ()))
FIRST = (((0,), (0,)), ((), ()))


def after(array, *earlier):
    return lax.optimization_barrier((array,) + earlier)[0]


LIGHT = pl.CostEstimate(flops=1, bytes_accessed=1, transcendentals=0)
SHORT = pl.CostEstimate(flops=4 * 10**9, bytes_accessed=10**7, transcendentals=0)


def limits():
    return pltpu.CompilerParams(vmem_limit_bytes=16 * 1024 * 1024)


def whole(shape):
    return pl.BlockSpec(shape, lambda *_: (0,) * len(shape))


def probs_kernel(scale, heads, q_ref, k_ref, probs_ref):
    keys = k_ref[...]
    seq = keys.shape[0]
    rows = lax.broadcasted_iota(jnp.int32, (seq, seq), 0)
    cols = lax.broadcasted_iota(jnp.int32, (seq, seq), 1)
    for h in range(heads):
        q = q_ref[:, h * HEAD : (h + 1) * HEAD]
        scores = lax.dot_general(keys, q, LAST, preferred_element_type=F32) * scale
        scores = jnp.where(cols >= rows, scores, -jnp.inf)
        exponent = jnp.exp(scores - jnp.max(scores, axis=0, keepdims=True))
        probs_ref[h] = (exponent / jnp.sum(exponent, axis=0, keepdims=True)).astype(BF16)


def probabilities(q, k):
    seq, width = q.shape
    heads = 2
    count = width // HEAD
    return pl.pallas_call(
        functools.partial(probs_kernel, HEAD**-0.5, heads),
        grid=(count // heads,),
        in_specs=[pl.BlockSpec((seq, heads * HEAD), lambda i: (0, i)), whole((seq, HEAD))],
        out_specs=pl.BlockSpec((heads, seq, seq), lambda i: (i, 0, 0)),
        out_shape=jax.ShapeDtypeStruct((count, seq, seq), BF16),
        cost_estimate=LIGHT,
        compiler_params=limits(),
    )(q, k)


def gather_rows(position, c, near_ref, far_ref, rows_ref):
    count = near_ref.shape[0] // 2
    rows = near_ref.shape[1]
    for k in range(count):
        for xh in range(2):
            index = (position + count - k) % count * 2 + xh
            start = (k * 2 + xh) * 2 * rows
            rows_ref[pl.ds(pl.multiple_of(start + c * rows, rows), rows)] = near_ref[index]
            rows_ref[pl.ds(pl.multiple_of(start + (1 - c) * rows, rows), rows)] = far_ref[index]


def out_kernel(place, near_ref, far_ref, *refs):
    ao_refs, (part_ref, grads_ref) = refs[:-2], refs[-2:]
    step = pl.program_id(0)
    seq = ao_refs[0].shape[0]

    @pl.when(step == 0)
    def _():
        gather_rows(place[2], place[1], near_ref, far_ref, grads_ref)

    chunk = part_ref.shape[0]
    span = pl.ds(pl.multiple_of(step * chunk, chunk), chunk)
    total = jnp.zeros(part_ref.shape, F32)
    for k, ao_ref in enumerate(ao_refs):
        total += lax.dot_general(
            grads_ref[k * seq : (k + 1) * seq, span], ao_ref[...], FIRST, preferred_element_type=F32
        )
    part_ref[...] = total.astype(BF16)


def out_part(place, near, far, aos):
    seq, width = aos[0].shape
    feats = near.shape[2]
    chunk = feats // 5
    return pl.pallas_call(
        out_kernel,
        grid_spec=pltpu.PrefetchScalarGridSpec(
            num_scalar_prefetch=1,
            grid=(feats // chunk,),
            in_specs=[whole(near.shape), whole(far.shape)] + [whole(ao.shape) for ao in aos],
            out_specs=pl.BlockSpec((chunk, width), lambda i, place: (i, 0)),
            scratch_shapes=[pltpu.VMEM((len(aos) * seq, feats), BF16)],
        ),
        out_shape=jax.ShapeDtypeStruct((feats, width), BF16),
        cost_estimate=LIGHT,
        compiler_params=limits(),
    )(place, near, far, *aos)


def head_kernel(offsets, place, near_ref, far_ref, *refs):
    n_z = len(offsets)
    w_refs, wv_refs, refs = refs[:n_z], refs[n_z : 2 * n_z], refs[2 * n_z :]
    own_ref, send_refs, (wv_ref, grads_ref, w_all) = refs[0], refs[1:-3], refs[-3:]
    depth = w_refs[0].shape[0]

    def in_order(pieces, ref):
        for offset, piece in zip(offsets, pieces):
            start = (place[3] + offset + n_z) % n_z * depth
            ref[pl.ds(pl.multiple_of(start, depth), depth)] = piece[...]

    @pl.when(pl.program_id(0) == 0)
    def _():
        gather_rows(place[2], place[1], near_ref, far_ref, grads_ref)
        in_order(wv_refs, wv_ref)

    in_order(w_refs, w_all)
    seq = own_ref.shape[0]
    product = jnp.dot(grads_ref[...], w_all[...], preferred_element_type=F32)
    own_ref[...] = product[:seq]
    for k, ref in enumerate(send_refs):
        ref[...] = product[(k + 1) * seq : (k + 2) * seq].astype(BF16)


def head_parts(place, near, far, pieces, seq, width):
    feats = near.shape[2]
    count = near.shape[0] // 2
    block = 512
    depth = feats // len(pieces)
    wide = pl.BlockSpec((seq, block), lambda i, place: (0, i))
    return pl.pallas_call(
        functools.partial(head_kernel, tuple(pieces)),
        grid_spec=pltpu.PrefetchScalarGridSpec(
            num_scalar_prefetch=1,
            grid=(width // block,),
            in_specs=[whole(near.shape), whole(far.shape)]
            + [pl.BlockSpec((depth, block), lambda i, place: (0, i))] * len(pieces)
            + [pl.BlockSpec((depth, HEAD), lambda i, place: (0, width // HEAD))] * len(pieces),
            out_specs=[wide] * count + [whole((feats, HEAD))],
            scratch_shapes=[pltpu.VMEM((count * seq, feats), BF16), pltpu.VMEM((feats, block), BF16)],
        ),
        out_shape=[jax.ShapeDtypeStruct((seq, width), F32)]
        + [jax.ShapeDtypeStruct((seq, width), BF16)] * (count - 1)
        + [jax.ShapeDtypeStruct((feats, HEAD), BF16)],
        cost_estimate=LIGHT,
        compiler_params=limits(),
    )(place, near, far, *pieces.values(), *pieces.values())


def grad_kernel(heads, probs_ref, own_ref, *refs):
    recv_refs, (grad_ref, dv_ref) = refs[:-2], refs[-2:]
    total = jnp.zeros(dv_ref.shape, F32)
    for h in range(heads):
        span = slice(h * HEAD, (h + 1) * HEAD)
        grad = own_ref[:, span]
        for ref in recv_refs:
            grad += ref[:, span].astype(F32)
        grad = grad.astype(BF16)
        grad_ref[:, span] = grad
        total += jnp.dot(probs_ref[h], grad, preferred_element_type=F32)
    dv_ref[...] = total.astype(BF16)


def head_gradient(probs, own, recv):
    seq, width = own.shape
    return pl.pallas_call(
        functools.partial(grad_kernel, width // HEAD),
        out_shape=[jax.ShapeDtypeStruct((seq, width), BF16), jax.ShapeDtypeStruct((seq, HEAD), BF16)],
        cost_estimate=SHORT,
        compiler_params=limits(),
    )(probs, own, *recv)


def score_kernel(scale, heads, q_ref, k_ref, v_ref, ao_ref, grad_ref, dq_ref, dk_ref, dk_sum):
    step = pl.program_id(0)

    @pl.when(step == 0)
    def _():
        dk_sum[...] = jnp.zeros_like(dk_sum)

    keys = k_ref[...]
    vals = v_ref[...]
    seq = keys.shape[0]
    rows = lax.broadcasted_iota(jnp.int32, (seq, seq), 0)
    cols = lax.broadcasted_iota(jnp.int32, (seq, seq), 1)
    dk_here = jnp.zeros(dk_sum.shape, F32)
    for h in range(heads):
        span = slice(h * HEAD, (h + 1) * HEAD)
        q = q_ref[:, span]
        grad = grad_ref[:, span]
        scores = lax.dot_general(q, keys, LAST, preferred_element_type=F32) * scale
        scores = jnp.where(rows >= cols, scores, -jnp.inf)
        exponent = jnp.exp(scores - jnp.max(scores, axis=1, keepdims=True))
        probs = exponent / jnp.sum(exponent, axis=1, keepdims=True)
        prob_grad = lax.dot_general(grad, vals, LAST, preferred_element_type=F32)
        row_dot = jnp.sum(grad.astype(F32) * ao_ref[:, span].astype(F32), axis=1, keepdims=True)
        score_grad = (probs * (prob_grad - row_dot)).astype(BF16)
        dq_ref[:, span] = (jnp.dot(score_grad, keys, preferred_element_type=F32) * scale).astype(BF16)
        dk_here += lax.dot_general(score_grad, q, FIRST, preferred_element_type=F32)
    dk_sum[...] += dk_here

    @pl.when(step == pl.num_programs(0) - 1)
    def _():
        dk_ref[...] = (dk_sum[...] * scale).astype(BF16)


def score_gradients(q, k, v, ao, grad):
    seq, width = q.shape
    heads = 4
    count = width // HEAD
    wide = pl.BlockSpec((seq, heads * HEAD), lambda i: (0, i))
    narrow = whole((seq, HEAD))
    return pl.pallas_call(
        functools.partial(score_kernel, HEAD**-0.5, heads),
        grid=(count // heads,),
        in_specs=[wide, narrow, narrow, wide, wide],
        out_specs=[wide, narrow],
        out_shape=[jax.ShapeDtypeStruct((seq, width), BF16), jax.ShapeDtypeStruct((seq, HEAD), BF16)],
        scratch_shapes=[pltpu.VMEM((seq, HEAD), F32)],
        cost_estimate=LIGHT,
        compiler_params=limits(),
    )(q, k, v, ao, grad)


def input_kernel(n_xl, n_z, cols, place, dv_ref, *refs):
    wv_refs, (keep_ref, give_ref, wv_all) = refs[:-3], refs[-3:]
    c, y, n_y = place[1], place[2], len(wv_refs)
    for k, ref in enumerate(wv_refs):
        from_y = (y + n_y - k) % n_y
        for z in range(n_z):
            for xl in range(n_xl):
                start = (xl * n_z + z) * n_y + from_y
                block = ref[(z * n_xl + xl) * cols : (z * n_xl + xl + 1) * cols].astype(F32)
                wv_all[pl.ds(pl.multiple_of(start * cols, 8), cols)] = block
    wv = wv_all[...].astype(BF16)
    for xh in range(2):
        keep_ref[xh] = lax.dot_general(dv_ref[xh, c], wv, LAST, preferred_element_type=F32)
        give = lax.dot_general(dv_ref[xh, 1 - c], wv, LAST, preferred_element_type=F32)
        give_ref[xh] = give.astype(BF16)


def input_parts(place, dv, wvs, n_xl, n_z, cols):
    rows = dv.shape[2]
    feats = len(wvs) * wvs[0].shape[0]
    shape = (2, rows, feats)
    return pl.pallas_call(
        functools.partial(input_kernel, n_xl, n_z, cols),
        grid_spec=pltpu.PrefetchScalarGridSpec(
            num_scalar_prefetch=1,
            grid=(1,),
            in_specs=[whole(dv.shape)] + [whole(wv.shape) for wv in wvs],
            out_specs=[whole(shape), whole(shape)],
            scratch_shapes=[pltpu.VMEM((feats, HEAD), F32)],
        ),
        out_shape=[jax.ShapeDtypeStruct(shape, F32), jax.ShapeDtypeStruct(shape, BF16)],
        cost_estimate=SHORT,
        compiler_params=limits(),
    )(place, dv, *wvs)


def value_kernel(cols, scale, place, near_ref, far_ref, *refs):
    dv_refs, part_refs, rows_ref = refs[:2], refs[2:-1], refs[-1]
    y = place[2]
    gather_rows(place[0], place[1], near_ref, far_ref, rows_ref)
    seq = dv_refs[0].shape[0]
    total = jnp.zeros((rows_ref.shape[1], HEAD), F32)
    for k, ref in enumerate(dv_refs):
        total += lax.dot_general(rows_ref[k * seq : (k + 1) * seq], ref[...], FIRST, preferred_element_type=F32)
    n_y = len(part_refs)
    for to_y in range(n_y):
        for k, ref in enumerate(part_refs):

            @pl.when((y + k) % n_y == to_y)
            def _():
                for z in range(ref.shape[0]):
                    start = (z * n_y + to_y) * cols
                    ref[z] = (total[start : start + cols] * scale).astype(BF16)


def value_parts(place, near, far, dvs, n_y, cols, scale):
    half = near.shape[2]
    shape = (half // cols // n_y, cols, HEAD)
    return pl.pallas_call(
        functools.partial(value_kernel, cols, scale),
        grid_spec=pltpu.PrefetchScalarGridSpec(
            num_scalar_prefetch=1,
            grid=(1,),
            in_specs=[whole(array.shape) for array in [near, far] + dvs],
            out_specs=[whole(shape)] * n_y,
            scratch_shapes=[pltpu.VMEM((len(dvs) * dvs[0].shape[0], half), BF16)],
        ),
        out_shape=[jax.ShapeDtypeStruct(shape, BF16)] * n_y,
        cost_estimate=SHORT,
        compiler_params=limits(),
    )(place, near, far, *dvs)


def split_kernel(rows_ref, halves_ref):
    half = halves_ref.shape[2]
    for i in range(halves_ref.shape[0]):
        halves_ref[i] = rows_ref[:, i // 2 * half : (i // 2 + 1) * half]


def split(array, count):
    rows, feats = array.shape
    shape = (2 * count, rows, feats // count)
    return pl.pallas_call(
        split_kernel,
        in_specs=[whole(array.shape)],
        out_specs=whole(shape),
        out_shape=jax.ShapeDtypeStruct(shape, BF16),
        cost_estimate=LIGHT,
        compiler_params=limits(),
    )(array)


def for_each(parts):
    both = jnp.broadcast_to(parts[:, None], (parts.shape[0], 2) + parts.shape[1:])
    return both.reshape((parts.shape[0] * 2,) + parts.shape[1:])


def on_device(queries, keys, values, attn_out, layer_in, out_grad, w_out, w_value):
    xl, z, y, xh, c = (lax.axis_index(a) for a in ("xl", "z", "y", "xh", "c"))
    place = jnp.stack([xl, c, y, z]).astype(jnp.int32)
    n_xl, n_z, n_y = SIZES["xl"], SIZES["z"], SIZES["y"]
    n_dp = n_xl * n_z * n_y
    q, k, v, ao, li, og = (a[0] for a in (queries, keys, values, attn_out, layer_in, out_grad))
    seq, width = q.shape
    rows, feats = og.shape
    quarter = feats // n_y
    cols = feats // n_dp

    shard = jnp.concatenate([w_out.T, w_value], axis=1)
    other = shift(shard, "xl", 1)
    plane = jnp.where(xl == 0, jnp.concatenate([shard, other]), jnp.concatenate([other, shard]))
    aos = [ao] + [shift(ao, "y", step) for step in range(1, n_y)]
    pieces = {0: plane}
    for step in range(1, n_z // 2):
        if step == 3:
            pieces[-2], pieces[2], _, _ = lax.optimization_barrier((pieces[-2], pieces[2], aos[1], aos[3]))
        pieces[-step] = shift(pieces[1 - step], "z", 1)
        pieces[step] = shift(pieces[step - 1], "z", -1)
    pieces[-n_z // 2] = shift(after(pieces[1 - n_z // 2], aos[2]), "z", 1)

    by_y = og.reshape(rows, n_xl, n_z, n_y, cols).transpose(3, 0, 2, 1, 4).reshape(n_y, rows, quarter)
    near = lax.all_to_all(after(for_each(by_y), plane), ("y", "xh"), 0, 0, tiled=True)
    near = after(near, pieces[-1], pieces[1])
    far = shift(near, "c", 1)

    li_near = lax.all_to_all(after(split(li, n_xl), near), ("xl", "xh"), 0, 0, tiled=True)
    li_near = after(li_near, pieces[-3], pieces[3])
    li_far = shift(li_near, "c", 1)

    own, *sends, wv = head_parts(place, after(near, li_far), far, pieces, seq, width)
    recv = [shift(send, "y", -step - 1) for step, send in enumerate(sends)]
    probs = probabilities(after(q, sends[0]), k)

    part = out_part(place, after(near, sends[0]), far, aos)
    parts = lax.all_to_all(part.reshape(n_z, n_xl * cols, width), "z", 0, 0, tiled=True)
    part = jnp.sum(parts.astype(F32), axis=0).astype(BF16)
    wv, probs, *recv = lax.optimization_barrier((wv, probs, *recv))
    wvs = [wv] + [shift(wv, "y", step) for step in range(1, n_y)]
    head_grad, value_grad = head_gradient(probs, own, recv)
    dvs = [value_grad, shift(value_grad, "xl", 1)]

    value_part = value_parts(place, li_near, li_far, dvs, n_y, cols, 1 / n_dp)
    first_part = value_part[0]
    value_part = [value_part[0]] + [shift(value_part[step], "y", step) for step in range(1, n_y)]
    value_part = sum(piece.astype(F32) for piece in value_part).astype(BF16)

    keep, give = input_parts(place, value_grad.reshape(2, 2, rows, HEAD), wvs, n_xl, n_z, cols)
    give = shift(after(give, first_part), "c", 1)

    def sum_of(i):
        return lax.dynamic_index_in_dim(keep, i, 0, False) + lax.dynamic_index_in_dim(give, i, 0, False).astype(F32)

    last = shift(sum_of(1 - xh).astype(BF16), "xh", 1)
    value_part = lax.all_to_all(after(value_part, parts), "z", 0, 0, tiled=True)

    part = part.reshape(n_xl, cols, width)
    mine = lax.dynamic_index_in_dim(part, xl, 0, False).astype(F32)
    other = shift(lax.dynamic_index_in_dim(part, 1 - xl, 0, False), "xl", 1)

    query_grad, key_grad = score_gradients(q, k, v, ao, after(head_grad, other))
    input_grad = (sum_of(xh) + after(last, key_grad).astype(F32)).astype(BF16)
    out_weight_grad = ((mine + other.astype(F32)) / n_dp).T
    value_weight_grad = jnp.sum(value_part.astype(F32), axis=0)

    return (
        query_grad[None],
        key_grad[None],
        value_grad[None],
        input_grad[None],
        out_weight_grad,
        value_weight_grad,
    )


def solution(mesh):
    fine = Mesh(mesh.devices.reshape(tuple(SIZES.values())), tuple(SIZES))
    heads = P(DP, None, TENSOR)
    tokens = P(DP, TENSOR, None)
    return jax.shard_map(
        on_device,
        mesh=fine,
        in_specs=(heads, heads, heads, heads, tokens, tokens, P(TENSOR, DP), P(DP, TENSOR)),
        out_specs=(heads, heads, heads, tokens, P(TENSOR, DP), P(DP, TENSOR)),
        check_vma=False,
    )
```
